32 devices in a mesh: fsdp: 8 (over y, x, core), rep: 4 (over z).
Axes of the slice: x: 2, y: 2, z: 4, core: 2. Of those that a mesh axis runs over, the one named last changes fastest.
Arguments:
- history: bfloat16 [9, 4096, 2048], P(None, ('fsdp', 'rep')), may hold values from -6 to 6
- mix_in: float32 [4096, 36], P(('fsdp', 'rep')), may hold values from -3 to 3
- doc_ids: int32 [32, 128], P(('fsdp', 'rep')), may hold values from 0 to 3, never falling along the last dimension, each value on 1 to 64 neighbouring positions
- doc_group: int32 [32, 4], P(('fsdp', 'rep')), may hold values from 0 to 21
- group_weight: float32 [22], replicated, may hold values from 0.3 to 3
- norm_gain: float32 [3, 2048], P(None, ('fsdp', 'rep')), may hold values from 0.1 to 1.9
- norm_bias: float32 [2, 2048], P(None, ('fsdp', 'rep')), may hold values from -1.75 to 1.75
- w_qkv: float32 [2048, 6144], P(('fsdp', 'rep')), may hold values from -0.125 to 0.125
- b_qkv: float32 [6144], P(('fsdp', 'rep')), may hold values from -1.75 to 1.75
- w_out: float32 [2048, 2048], P(('fsdp', 'rep')), may hold values from -0.75 to 0.75
- b_out: float32 [2048], P(('fsdp', 'rep')), may hold values from -1.75 to 1.75
- w_fc1: float32 [2048, 8192], P(('fsdp', 'rep')), may hold values from -0.125 to 0.125
- b_fc1: float32 [8192], P(('fsdp', 'rep')), may hold values from -1.75 to 1.75
- w_fc2: float32 [2048, 8192], P(('fsdp', 'rep')), may hold values from -0.0625 to 0.0625
- b_fc2: float32 [2048], P(('fsdp', 'rep')), may hold values from -1.75 to 1.75
- w_mix1: float32 [2048, 100], P(('fsdp', 'rep')), may hold values from -0.125 to 0.125
- b_mix1: float32 [100], replicated, may hold values from -3 to 3
- w_mix2: float32 [100, 40], replicated, may hold values from -0.625 to 0.625
- b_mix2: float32 [40], replicated, may hold values from -3 to 3
- cotangent: bfloat16 [4, 4096, 2048], P(None, ('fsdp', 'rep')), may hold values from -6 to 6
Outputs:
- next_streams: bfloat16 [4, 4096, 2048], P(None, ('fsdp', 'rep'))
- grad_history: float32 [9, 4096, 2048], P(None, ('fsdp', 'rep'))
- grad_mix_in: float32 [4096, 36], P(('fsdp', 'rep'))
- grad_norm_gain: float32 [3, 2048], P(None, ('fsdp', 'rep'))
- grad_norm_bias: float32 [2, 2048], P(None, ('fsdp', 'rep'))
- grad_w_qkv: float32 [2048, 6144], P(('fsdp', 'rep'))
- grad_b_qkv: float32 [6144], P(('fsdp', 'rep'))
- grad_w_out: float32 [2048, 2048], P(('fsdp', 'rep'))
- grad_b_out: float32 [2048], P(('fsdp', 'rep'))
- grad_w_fc1: float32 [2048, 8192], P(('fsdp', 'rep'))
- grad_b_fc1: float32 [8192], P(('fsdp', 'rep'))
- grad_w_fc2: float32 [2048, 8192], P(('fsdp', 'rep'))
- grad_b_fc2: float32 [2048], P(('fsdp', 'rep'))
- grad_w_mix1: float32 [2048, 100], P(('fsdp', 'rep'))
- grad_b_mix1: float32 [100], replicated
- grad_w_mix2: float32 [100, 40], replicated
- grad_b_mix2: float32 [40], replicated
The draws below stay inside these ranges and needn't reach their ends.
Inputs may be any that keep to these rules, and one draw needn't show every extreme that they name: `doc_ids`: within a sequence document numbers never fall; each of the 4 documents has 1 to 64 tokens, and one has exactly that many.
All inputs are finite; a program needn't handle non-finite values.
Results may differ from the reference program's by a relative error of at most 0.015.
The reference program's roundings to bfloat16 on the way count: a program that leaves them out, or rounds other values in their place, can miss the bound.
Values may be sent and summed in bfloat16 or wider, within the bound.
No kernel may reach another device: no remote copies, remote signals or barrier semaphores. Data moves between devices by JAX's collectives and lax.ppermute only.
A program may use at most 384 MiB of HBM per device.

```python
import math
import jax
import jax.numpy as jnp
import numpy as np
from jax import lax

D = 2048
HEADS = 16
HEAD_DIM = 128
ROT = 32
FF = 8192
MIX_HID = 100
STREAMS = 4
HIST = 9
MIXES = 40
TOK_DEV = 128
SEQS = 32
TOKENS = 4096
DOCS = 4
GROUPS = 22


def touch_ends(values, stream_key, low, largest):
    spot = [jax.random.randint(jax.random.fold_in(stream_key, axis), (), 0, length) for axis, length in enumerate(values.shape)]
    main_axis = values.shape.index(max(values.shape))
    neighbour = spot[:main_axis] + [(spot[main_axis] + 1) % values.shape[main_axis]] + spot[main_axis + 1:]
    return values.at[tuple(spot)].set(low).at[tuple(neighbour)].set(largest)


def steps_of(rng, shape, split, least, high):
    loudness = 1.0
    for axis_at, shards_of in split:
        heights = jax.random.uniform(jax.random.fold_in(jax.random.fold_in(rng, 6), axis_at), (shards_of,), jnp.float32, least / len(split), high / len(split))
        loudness = loudness * jnp.repeat(jnp.exp(heights), shape[axis_at] // shards_of).reshape((-1,) + (1,) * (len(shape) - 1 - axis_at))
    return loudness


def split_up(number_of, total, reach, skew):
    loads = [(1 << 20) // math.isqrt(rank ** skew) + 1 for rank in range(2, number_of + 1)]
    rest, counts = total - reach - (number_of - 1), [1] * (number_of - 1)
    while rest > 0:
        free = [i for i in range(number_of - 1) if counts[i] < reach]
        whole, remaining = sum([loads[i] for i in free]), rest
        for i in free:
            addition = min(reach - counts[i], max(1, remaining * loads[i] // whole), rest)
            counts[i] = counts[i] + addition
            rest = rest - addition
    return np.array([reach] + counts)


def ragged_sizes(stream_key, number_of, total, limit, skew):
    if number_of == 2:
        one = jax.random.randint(stream_key, (), max(1, total - limit), min(limit, total - 1) + 1)
        return jnp.stack([one, total - one])
    tallies = jnp.asarray(split_up(number_of, total, limit, skew), jnp.int32)
    pairs = (number_of - 1) // 2
    donor, receiver = tallies[1:1 + 2 * pairs:2], tallies[2:2 + 2 * pairs:2]
    margin = jnp.minimum(donor - 1, limit - receiver)
    shifted = jax.random.randint(jax.random.fold_in(stream_key, 1), (pairs,), 0, 1 << 20) % (margin + 1)
    tallies = tallies.at[1:1 + 2 * pairs:2].set(donor - shifted).at[2:2 + 2 * pairs:2].set(receiver + shifted)
    return tallies[jax.random.permutation(jax.random.fold_in(stream_key, 2), number_of)]


def noise(own_key, extent, width, reach, pieces=(), dtype=jnp.bfloat16):
    gain = steps_of(own_key, extent, pieces, -0.22, 0.18) if pieces else 1.0
    drawn = jax.random.normal(own_key, extent, jnp.float32) * width * gain
    return jnp.minimum(jnp.maximum(drawn, -reach), reach).astype(dtype)


def setup_inputs(seed: int = 0) -> dict:
    arg_keys = jax.random.split(jax.random.key(seed), 21)
    history = noise(arg_keys[0], (HIST, TOKENS, D), 1.0, 6.0, ((1, 32),))
    mix_in = noise(arg_keys[1], (TOKENS, STREAMS * HIST), 0.5, 3.0, ((0, 32),), jnp.float32)
    doc_ids = jax.vmap(lambda own: jnp.searchsorted(jnp.cumsum(ragged_sizes(own, DOCS, TOK_DEV, TOK_DEV // 2, 2)), jnp.arange(TOK_DEV), side="right"))(jax.random.split(arg_keys[2], SEQS)).reshape((SEQS, TOK_DEV)).astype(jnp.int32)
    doc_group = touch_ends(jax.random.randint(arg_keys[3], (SEQS, DOCS), 0, GROUPS), jax.random.fold_in(arg_keys[3], 1), 0, GROUPS - 1).astype(jnp.int32)
    group_weight = jnp.clip(jnp.exp(jax.random.uniform(arg_keys[4], (GROUPS,), jnp.float32, math.log(0.3), math.log(3.0))), 0.3, 3.0)
    norm_gain = jnp.clip(1.0 + 0.18 * jax.random.normal(arg_keys[5], (3, D), jnp.float32), 0.1, 1.9)
    norm_bias = noise(arg_keys[6], (2, D), 0.3, 1.75, ((1, 32),), jnp.float32)
    w_qkv = noise(arg_keys[7], (D, 3 * D), D ** -0.5, 0.125, ((0, 32),), jnp.float32)
    b_qkv = noise(arg_keys[8], (3 * D,), 0.3, 1.75, ((0, 32),), jnp.float32)
    w_out = noise(arg_keys[9], (D, D), (D // 32) ** -0.5, 0.75, ((0, 32),), jnp.float32)
    b_out = noise(arg_keys[10], (D,), 0.3, 1.75, ((0, 32),), jnp.float32)
    w_fc1 = noise(arg_keys[11], (D, FF), D ** -0.5, 0.125, ((0, 32),), jnp.float32)
    b_fc1 = noise(arg_keys[12], (FF,), 0.3, 1.75, ((0, 32),), jnp.float32)
    w_fc2 = noise(arg_keys[13], (D, FF), FF ** -0.5, 0.0625, ((0, 32),), jnp.float32)
    b_fc2 = noise(arg_keys[14], (D,), 0.3, 1.75, ((0, 32),), jnp.float32)
    w_mix1 = noise(arg_keys[15], (D, MIX_HID), D ** -0.5, 0.125, ((0, 32),), jnp.float32)
    b_mix1 = noise(arg_keys[16], (MIX_HID,), 0.5, 3.0, (), jnp.float32)
    w_mix2 = noise(arg_keys[17], (MIX_HID, MIXES), MIX_HID ** -0.5, 0.625, (), jnp.float32)
    b_mix2 = noise(arg_keys[18], (MIXES,), 0.5, 3.0, (), jnp.float32)
    cotangent = noise(arg_keys[19], (STREAMS, TOKENS, D), 1.0, 6.0, ((1, 32),))
    return dict(history=history, mix_in=mix_in, doc_ids=doc_ids, doc_group=doc_group, group_weight=group_weight, norm_gain=norm_gain, norm_bias=norm_bias, w_qkv=w_qkv, b_qkv=b_qkv, w_out=w_out, b_out=b_out, w_fc1=w_fc1, b_fc1=b_fc1, w_fc2=w_fc2, b_fc2=b_fc2, w_mix1=w_mix1, b_mix1=b_mix1, w_mix2=w_mix2, b_mix2=b_mix2, cotangent=cotangent)


@jax.custom_vjp
def low(v):
    return lax.optimization_barrier(v.astype(jnp.bfloat16)).astype(jnp.float32)

@jax.custom_vjp
def low_back(v):
    return v

def low_keep(v):
    return (low(v), None)

def low_pass(kept, grad):
    return (grad,)

def back_keep(v):
    return (v, None)

def back_low(kept, grad):
    return (low(grad),)
low.defvjp(low_keep, low_pass)
low_back.defvjp(back_keep, back_low)

def matmul(left, right):
    return jnp.dot(left, right, precision=lax.Precision.HIGHEST, preferred_element_type=jnp.float32)

def layer_norm(values, gain_row, shift_row):
    center = values - lax.optimization_barrier(jnp.mean(values, -1, keepdims=True))
    spread = lax.optimization_barrier(jnp.mean(center * center, -1, keepdims=True))
    return center * lax.rsqrt(spread + 1e-05) * gain_row + shift_row

def rotate(values, cosine, sine):
    halfway = ROT // 2
    former = values[..., :halfway]
    latter = values[..., halfway:ROT]
    return jnp.concatenate([former * cosine - latter * sine, latter * cosine + former * sine, values[..., ROT:]], -1)

def layer_block(params, hist, mixing, docs):
    norm_gain, norm_bias, w_qkv, b_qkv, w_out, b_out, w_fc1, b_fc1, w_fc2, b_fc2, w_mix1, b_mix1, w_mix2, b_mix2 = params
    seq_count = docs.shape[0]
    length = docs.shape[1]
    count_rows = seq_count * length
    gains = low(norm_gain)
    shifts = low(norm_bias)
    alpha = mixing.reshape(count_rows, STREAMS, HIST)
    streams = jnp.einsum('rsj,jrd->srd', alpha, hist, precision=lax.Precision.HIGHEST)
    query_norm = low(layer_norm(streams[0], gains[0], shifts[0]))
    key_norm = low(layer_norm(streams[1], gains[0], shifts[0]))
    value_norm = low(layer_norm(streams[2], gains[0], shifts[0]))
    resid_norm = low(layer_norm(streams[3], gains[1], shifts[1]))
    qkv_weight = low(w_qkv)
    qkv_bias = low(b_qkv)
    query = low_back(matmul(query_norm, qkv_weight[:, :D])) + qkv_bias[:D]
    key = low_back(matmul(key_norm, qkv_weight[:, D:2 * D])) + qkv_bias[D:2 * D]
    value = low_back(matmul(value_norm, qkv_weight[:, 2 * D:])) + qkv_bias[2 * D:]
    position = jnp.arange(length).astype(jnp.float32)
    frequency = 10000.0 ** (-jnp.arange(0, ROT, 2).astype(jnp.float32) / ROT)
    angle = position[:, None] * frequency[None, :]
    cosine = jnp.cos(angle)[:, None, :]
    sine = jnp.sin(angle)[:, None, :]
    query = low(rotate(query.reshape(seq_count, length, HEADS, HEAD_DIM), cosine, sine))
    key = low(rotate(key.reshape(seq_count, length, HEADS, HEAD_DIM), cosine, sine))
    value = low(value).reshape(seq_count, length, HEADS, HEAD_DIM)
    scores = low_back(jnp.einsum('bqhd,bkhd->bhqk', query, key, precision=lax.Precision.HIGHEST) * HEAD_DIM ** (-0.5))
    causal = jnp.arange(length)[None, :] <= jnp.arange(length)[:, None]
    allowed = causal[None] & (docs[:, None, :] == docs[:, :, None])
    probs = jax.nn.softmax(jnp.where(allowed[:, None], scores, -1e+30), axis=-1)
    mixed = jnp.einsum('bhqk,bkhd->bqhd', low(probs), value, precision=lax.Precision.HIGHEST).reshape(count_rows, D)
    mixed = low(low_back(mixed))
    attn = low_back(matmul(mixed, low(w_out).T)) + low(b_out)
    hidden = low(jax.nn.gelu(low_back(matmul(resid_norm, low(w_fc1))) + low(b_fc1), approximate=False))
    mlp = low_back(matmul(hidden, low(w_fc2).T)) + low(b_fc2)
    entry = streams[3] + attn + mlp
    scaled = low(entry * lax.rsqrt(lax.optimization_barrier(jnp.mean(entry * entry, -1, keepdims=True)) + 1e-06) * gains[2])
    mix_hidden = jax.nn.gelu(low_back(matmul(scaled, low(w_mix1))) + b_mix1, approximate=False)
    weights = matmul(mix_hidden, w_mix2) + b_mix2
    sources = jnp.concatenate([hist, entry[None]], 0)
    return jnp.einsum('rsj,jrd->srd', weights.reshape(count_rows, STREAMS, HIST + 1), sources, precision=lax.Precision.HIGHEST)

def reference(history, mix_in, doc_ids, doc_group, group_weight, norm_gain, norm_bias, w_qkv, b_qkv, w_out, b_out, w_fc1, b_fc1, w_fc2, b_fc2, w_mix1, b_mix1, w_mix2, b_mix2, cotangent):
    seq_block = math.gcd(SEQS, max(1, 4096 // TOK_DEV))
    blocks = SEQS // seq_block
    block_rows = seq_block * TOK_DEV
    params = (norm_gain, norm_bias, w_qkv, b_qkv, w_out, b_out, w_fc1, b_fc1, w_fc2, b_fc2, w_mix1, b_mix1, w_mix2, b_mix2)
    hist_all = history.astype(jnp.float32)
    doc_blocks = doc_ids.reshape(blocks, seq_block, TOK_DEV)

    def whole(params, hist_all, mixing):
        hist_blocks = hist_all.reshape(HIST, blocks, block_rows, D).transpose(1, 0, 2, 3)
        mix_blocks = mixing.reshape(blocks, block_rows, STREAMS * HIST)

        def advance(carry, inputs):
            return (carry, layer_block(params, inputs[0], inputs[1], inputs[2]))
        carry, stacked = lax.scan(jax.checkpoint(advance), jnp.zeros((), jnp.float32), (hist_blocks, mix_blocks, doc_blocks))
        return stacked.transpose(1, 0, 2, 3).reshape(STREAMS, TOKENS, D)
    outputs, backward = jax.vjp(whole, params, hist_all, mix_in)
    token_group = jnp.take_along_axis(doc_group, doc_ids, axis=1).reshape(TOKENS)
    token_weight = group_weight[token_group]
    grads = backward(cotangent.astype(jnp.float32) * token_weight[None, :, None])
    pgrad = grads[0]
    return (outputs.astype(jnp.bfloat16), grads[1], grads[2], pgrad[0], pgrad[1], pgrad[2], pgrad[3], pgrad[4], pgrad[5], pgrad[6], pgrad[7], pgrad[8], pgrad[9], pgrad[10], pgrad[11], pgrad[12], pgrad[13])
```

```python
import jax
import jax.numpy as jnp
from jax import lax
from jax.sharding import PartitionSpec as P

HEAD_DIM = 128
ROT = 32
NARROW = jnp.bfloat16
SINGLE = jnp.float32
NORM_EPSILON = 1e-05
RMS_EPSILON = 1e-06
AXES = ("fsdp", "rep")


def layer_norm(values, gain_row, shift_row):
    center = values - jnp.mean(values, -1, keepdims=True)
    spread = jnp.mean(center * center, -1, keepdims=True)
    return center * lax.rsqrt(spread + NORM_EPSILON) * gain_row + shift_row


def norm_streams(query_in, key_in, value_in, resid_in, gains, shifts):
    return (
        layer_norm(query_in, gains[0], shifts[0]),
        layer_norm(key_in, gains[0], shifts[0]),
        layer_norm(value_in, gains[0], shifts[0]),
        layer_norm(resid_in, gains[1], shifts[1]),
    )


def rms_norm(entry, gain_row):
    return entry * lax.rsqrt(jnp.mean(entry * entry, -1, keepdims=True) + RMS_EPSILON) * gain_row


def gelu_exact(values):
    return jax.nn.gelu(values, approximate=False)


def rotate(values, cosine, sine):
    halfway = ROT // 2
    former = values[..., :halfway]
    latter = values[..., halfway:ROT]
    return jnp.concatenate(
        [former * cosine - latter * sine, latter * cosine + former * sine, values[..., ROT:]], -1
    )


def times(left, right):
    return jnp.dot(left, right, preferred_element_type=SINGLE)


def times_transposed(left, right):
    return lax.dot_general(left, right, (((1,), (1,)), ((), ())), preferred_element_type=SINGLE)


def transposed_times(left, right):
    return lax.dot_general(left, right, (((0,), (0,)), ((), ())), preferred_element_type=SINGLE)


def blend(weights, sources):
    result = weights[:, 0:1] * sources[0]
    for index in range(1, len(sources)):
        result = result + weights[:, index : index + 1] * sources[index]
    return result


def pick(values, index, axis=0):
    return lax.dynamic_index_in_dim(values, index, axis, keepdims=False)


def ordered(parts, own, axis=0):
    shape = parts[0].shape[:axis] + (len(parts),) + parts[0].shape[axis:]
    result = jnp.zeros(shape, parts[0].dtype)
    for k, part in enumerate(parts):
        result = lax.dynamic_update_index_in_dim(result, part, own ^ k, axis)
    return result


def on_device(
    fsdp,
    rep,
    history,
    mix_in,
    doc_ids,
    doc_group,
    group_weight,
    norm_gain,
    norm_bias,
    w_qkv,
    b_qkv,
    w_out,
    b_out,
    w_fc1,
    b_fc1,
    w_fc2,
    b_fc2,
    w_mix1,
    b_mix1,
    w_mix2,
    b_mix2,
    cotangent,
):
    entries, length, width = history.shape
    stream_count = cotangent.shape[0]
    rows = w_qkv.shape[0]
    hidden = w_fc1.shape[1]
    chips = fsdp // 2
    devices = fsdp * rep
    head_cols = width // fsdp
    heads = head_cols // HEAD_DIM
    hid_cols = hidden // (2 * rep)
    place = lax.axis_index("fsdp")
    line = lax.axis_index("rep")
    core = place & 1
    chip = place >> 1

    def swap_core(values):
        return lax.ppermute(values, "fsdp", [(i, i ^ 1) for i in range(fsdp)])

    def hop_chip(values, m):
        return lax.ppermute(values, "fsdp", [(i, i ^ (2 * m)) for i in range(fsdp)])

    def hop_rep(values, k):
        return lax.ppermute(values, "rep", [(i, i ^ k) for i in range(rep)])

    def both_cores(mine, theirs):
        other = swap_core(theirs)
        return jnp.stack([jnp.where(core == 0, mine, other), jnp.where(core == 0, other, mine)])

    small = [
        norm_gain.reshape(-1),
        norm_bias.reshape(-1),
        b_qkv,
        b_out,
        b_fc1,
        b_fc2,
        doc_ids.reshape(-1),
        w_mix1.reshape(-1),
    ]
    sizes = [part.shape[0] for part in small]
    packed = jnp.concatenate([part.astype(NARROW) for part in small])
    gathered = lax.all_to_all(
        jnp.broadcast_to(packed[None], (devices, packed.shape[0])), AXES, 0, 0, tiled=True
    )
    fields, start = [], 0
    for size in sizes:
        fields.append(gathered[:, start : start + size])
        start += size
    gains = fields[0].reshape(devices, 3, rows).transpose(1, 0, 2).reshape(3, width).astype(SINGLE)
    shifts = fields[1].reshape(devices, 2, rows).transpose(1, 0, 2).reshape(2, width).astype(SINGLE)
    qkv_bias = fields[2].reshape(3, fsdp, head_cols).astype(SINGLE)
    out_bias = fields[3].reshape(width).astype(SINGLE)
    first_bias = fields[4].reshape(2 * rep, hid_cols).astype(SINGLE)
    second_bias = fields[5].reshape(width).astype(SINGLE)
    docs_all = fields[6].reshape(fsdp, rep, length)
    mix_first = fields[7].reshape(width, -1)
    my_qkv_bias = pick(qkv_bias, place, 1).reshape(3 * head_cols)
    my_first_bias = pick(first_bias, core * rep + line)

    def spread_hidden(weight):
        split = weight.astype(NARROW).reshape(rows, 2, rep, hid_cols)
        pair = both_cores(pick(split, core, 1), pick(split, 1 - core, 1))
        parts = [pick(pair, line, 2)]
        for k in range(1, rep):
            parts.append(hop_rep(pick(pair, line ^ k, 2), k))
        block = ordered(parts, line, 1).reshape(2 * rep * rows, hid_cols)
        blocks = [block] + [hop_chip(block, m) for m in range(1, chips)]
        return ordered(blocks, chip, 0).reshape(width, hid_cols)

    def spread_heads():
        split = jnp.concatenate(
            [
                w_qkv.astype(NARROW).reshape(rows, 3, fsdp, head_cols),
                w_out.astype(NARROW).reshape(rows, 1, fsdp, head_cols),
            ],
            1,
        )
        split = split.transpose(2, 0, 1, 3).reshape(chips, 2, rows, 4 * head_cols)
        pair = both_cores(pick(split, core, 1), pick(split, 1 - core, 1))
        parts = [pick(pair, chip, 1)]
        for m in range(1, chips):
            parts.append(hop_chip(pick(pair, chip ^ m, 1), m))
        block = ordered(parts, chip, 0)
        blocks = [block] + [hop_rep(block, k) for k in range(1, rep)]
        return ordered(blocks, line, 2).reshape(width, 4 * head_cols)

    first_full = spread_hidden(w_fc1)
    second_full = spread_hidden(w_fc2)
    heads_full = spread_heads()
    qkv_full = heads_full[:, : 3 * head_cols]
    out_full = heads_full[:, 3 * head_cols :]

    def gather_rep(values):
        parts = [values] + [hop_rep(values, k) for k in range(1, rep)]
        mine = jnp.stack(parts)
        return jnp.stack([mine, swap_core(mine)])

    def scatter_rep(values):
        mine = values[0] + swap_core(values[1].astype(NARROW)).astype(SINGLE)
        total = mine[0]
        for k in range(1, rep):
            total = total + hop_rep(mine[k].astype(NARROW), k).astype(SINGLE)
        return total

    def gather_fsdp(values):
        parts = [values] + [hop_chip(values, m) for m in range(1, chips)]
        mine = jnp.stack(parts)
        return jnp.stack([mine, swap_core(mine)])

    def scatter_fsdp(values):
        mine = values[0] + swap_core(values[1].astype(NARROW)).astype(SINGLE)
        total = mine[0]
        for m in range(1, chips):
            total = total + hop_chip(mine[m].astype(NARROW), m).astype(SINGLE)
        return total

    sources = [history[index].astype(SINGLE) for index in range(entries)]
    alpha = mix_in.reshape(length, stream_count, entries)
    stream_in = [blend(alpha[:, stream], sources) for stream in range(stream_count)]
    normed, norm_back = jax.vjp(
        norm_streams,
        stream_in[0],
        stream_in[1],
        stream_in[2],
        stream_in[3],
        gains[:2],
        shifts,
    )
    resid_norm = gather_rep(normed[3].astype(NARROW)).reshape(2 * rep * length, width)
    qkv_norm = gather_fsdp(jnp.stack(normed[:3]).astype(NARROW))
    qkv_norm = qkv_norm.transpose(2, 0, 1, 3, 4).reshape(3, fsdp * length, width)

    seqs = fsdp
    position = jnp.arange(length).astype(SINGLE)
    frequency = 10000.0 ** (-jnp.arange(0, ROT, 2).astype(SINGLE) / ROT)
    angle = position[:, None] * frequency[None, :]
    cosine = jnp.cos(angle)[None, :, None, :]
    sine = jnp.sin(angle)[None, :, None, :]
    linear = [
        times(qkv_norm[i], qkv_full[:, i * head_cols : (i + 1) * head_cols])
        + my_qkv_bias[i * head_cols : (i + 1) * head_cols]
        for i in range(3)
    ]
    linear = [values.reshape(seqs, length, heads, HEAD_DIM) for values in linear]
    query_rot = rotate(linear[0], cosine, sine).astype(NARROW)
    key_rot = rotate(linear[1], cosine, sine).astype(NARROW)
    value_low = linear[2].astype(NARROW)
    scale = HEAD_DIM ** (-0.5)
    docs_line = pick(docs_all, line, 1)
    docs = jnp.stack(
        [pick(docs_line, place ^ (2 * m + other)) for other in range(2) for m in range(chips)]
    )
    spot = jnp.arange(length)
    allowed = (spot[None, None, :] <= spot[None, :, None]) & (docs[:, None, :] == docs[:, :, None])

    def attention_scores():
        raw = jnp.einsum("bqhd,bkhd->bhqk", query_rot, key_rot, preferred_element_type=SINGLE)
        return jnp.where(allowed[:, None], raw * scale, -1e30)

    scores = attention_scores()
    largest = jnp.max(scores, -1, keepdims=True)
    summed = jnp.sum(jnp.exp(scores - largest), -1, keepdims=True)
    log_total = largest + jnp.log(summed)
    probs = jnp.exp(scores - log_total)
    mixed = jnp.einsum(
        "bhqk,bkhd->bqhd", probs.astype(NARROW), value_low, preferred_element_type=SINGLE
    )
    mixed_low = mixed.reshape(seqs * length, head_cols).astype(NARROW)
    attn_branch = scatter_fsdp(
        times_transposed(mixed_low, out_full).reshape(2, chips, length, width)
    )

    hidden_pre = times(resid_norm, first_full) + my_first_bias
    hidden_act, gelu_back = jax.vjp(gelu_exact, hidden_pre)
    hidden_low = hidden_act.astype(NARROW)
    mlp_branch = scatter_rep(
        times_transposed(hidden_low, second_full).reshape(2, rep, length, width)
    )

    new_entry = stream_in[3] + attn_branch + mlp_branch + (out_bias + second_bias)
    scaled, rms_back = jax.vjp(rms_norm, new_entry, gains[2])
    scaled_low = scaled.astype(NARROW)
    mix_pre = times(scaled_low, mix_first) + b_mix1
    mix_hidden, mix_back = jax.vjp(gelu_exact, mix_pre)
    mix_weights = (
        jnp.dot(mix_hidden, w_mix2, precision=lax.Precision.HIGHEST, preferred_element_type=SINGLE)
        + b_mix2
    )
    all_sources = sources + [new_entry]
    coef = mix_weights.reshape(length, stream_count, entries + 1)
    next_streams = jnp.stack(
        [blend(coef[:, stream], all_sources) for stream in range(stream_count)]
    ).astype(NARROW)

    documents = doc_ids[0]
    doc_match = documents[:, None] == jnp.arange(doc_group.shape[1], dtype=jnp.int32)[None, :]
    token_group = jnp.sum(jnp.where(doc_match, doc_group[0][None, :], 0), axis=1)
    group_match = (
        token_group[:, None] == jnp.arange(group_weight.shape[0], dtype=jnp.int32)[None, :]
    )
    token_weight = jnp.sum(jnp.where(group_match, group_weight[None, :], 0.0), axis=1)
    grad_out = cotangent.astype(SINGLE) * token_weight[None, :, None]
    grad_list = [grad_out[stream] for stream in range(stream_count)]
    grad_sources = [blend(coef[:, :, index], grad_list) for index in range(entries + 1)]
    grad_coef = jnp.stack(
        [
            jnp.stack(
                [
                    jnp.sum(grad_list[stream] * all_sources[index], -1)
                    for index in range(entries + 1)
                ],
                -1,
            )
            for stream in range(stream_count)
        ],
        1,
    )
    grad_mix_weights = grad_coef.reshape(length, stream_count * (entries + 1))
    grad_w_mix2 = jnp.dot(
        mix_hidden.T,
        grad_mix_weights,
        precision=lax.Precision.HIGHEST,
        preferred_element_type=SINGLE,
    )
    grad_b_mix2 = jnp.sum(grad_mix_weights, 0)
    grad_mix_hidden = jnp.dot(
        grad_mix_weights, w_mix2.T, precision=lax.Precision.HIGHEST, preferred_element_type=SINGLE
    )
    (grad_mix_pre,) = mix_back(grad_mix_hidden)
    grad_b_mix1 = jnp.sum(grad_mix_pre, 0)
    grad_mix_low = grad_mix_pre.astype(NARROW)
    grad_w_mix1 = transposed_times(scaled_low, grad_mix_low)
    grad_scaled = times_transposed(grad_mix_low, mix_first)
    grad_entry_rms, grad_rms_gain = rms_back(grad_scaled)
    grad_entry = grad_sources[entries] + grad_entry_rms
    grad_branch_bias = jnp.sum(grad_entry, 0)
    grad_branch = grad_entry.astype(NARROW)
    grad_rep = gather_rep(grad_branch).reshape(2 * rep * length, width)
    grad_fsdp = gather_fsdp(grad_branch).reshape(fsdp * length, width)

    grad_hidden = times(grad_rep, second_full)
    (grad_hidden_pre,) = gelu_back(grad_hidden)
    grad_first_bias = jnp.sum(grad_hidden_pre, 0)
    grad_hidden_low = grad_hidden_pre.astype(NARROW)
    grad_resid_norm = scatter_rep(
        times_transposed(grad_hidden_low, first_full).reshape(2, rep, length, width)
    )

    def collect_hidden(grad):
        blocks = grad.reshape(chips, 2 * rep * rows, hid_cols)
        total = pick(blocks, chip)
        for m in range(1, chips):
            total = total + hop_chip(pick(blocks, chip ^ m).astype(NARROW), m).astype(SINGLE)
        split = total.astype(NARROW).reshape(2, rep, rows, hid_cols)
        parts = [pick(split, line, 1)]
        for k in range(1, rep):
            parts.append(hop_rep(pick(split, line ^ k, 1), k))
        across = ordered(parts, line, 1)
        pair = both_cores(pick(across, core), pick(across, 1 - core))
        return pair.transpose(2, 0, 1, 3).reshape(rows, hidden).astype(SINGLE)

    grad_w_fc2 = collect_hidden(transposed_times(grad_rep, hidden_low))
    grad_w_fc1 = collect_hidden(transposed_times(resid_norm, grad_hidden_low))

    grad_mixed_low = (
        times(grad_fsdp, out_full).astype(NARROW).reshape(seqs, length, heads, HEAD_DIM)
    )
    again_probs = probs
    grad_value = jnp.einsum(
        "bhqk,bqhd->bkhd", again_probs.astype(NARROW), grad_mixed_low, preferred_element_type=SINGLE
    )
    grad_probs = jnp.einsum(
        "bqhd,bkhd->bhqk", grad_mixed_low, value_low, preferred_element_type=SINGLE
    )
    inner = jnp.sum(again_probs * grad_probs, -1, keepdims=True)
    grad_scores = (again_probs * (grad_probs - inner)).astype(NARROW)
    grad_query_rot = (
        jnp.einsum("bhqk,bkhd->bqhd", grad_scores, key_rot, preferred_element_type=SINGLE) * scale
    )
    grad_key_rot = (
        jnp.einsum("bhqk,bqhd->bkhd", grad_scores, query_rot, preferred_element_type=SINGLE) * scale
    )
    grad_linear = [
        values.reshape(seqs * length, head_cols)
        for values in (
            rotate(grad_query_rot, cosine, -sine),
            rotate(grad_key_rot, cosine, -sine),
            grad_value,
        )
    ]
    grad_qkv_bias = jnp.stack([jnp.sum(values, 0) for values in grad_linear])
    grad_linear_low = [values.astype(NARROW) for values in grad_linear]
    grad_qkv_norm = jnp.stack(
        [
            times_transposed(grad_linear_low[i], qkv_full[:, i * head_cols : (i + 1) * head_cols])
            for i in range(3)
        ]
    )
    grad_qkv_norm = scatter_fsdp(
        grad_qkv_norm.reshape(3, 2, chips, length, width).transpose(1, 2, 0, 3, 4)
    )
    grad_heads = jnp.concatenate(
        [transposed_times(qkv_norm[i], grad_linear_low[i]) for i in range(3)]
        + [transposed_times(grad_fsdp, mixed_low)],
        1,
    )

    def collect_heads(grad):
        blocks = grad.reshape(chips, 2, rep, rows, 4 * head_cols)
        total = pick(blocks, line, 2)
        for k in range(1, rep):
            total = total + hop_rep(pick(blocks, line ^ k, 2).astype(NARROW), k).astype(SINGLE)
        split = total.astype(NARROW)
        parts = [pick(split, chip)]
        for m in range(1, chips):
            parts.append(hop_chip(pick(split, chip ^ m), m))
        across = ordered(parts, chip, 1)
        pair = both_cores(pick(across, core), pick(across, 1 - core))
        return pair.transpose(2, 1, 0, 3).reshape(rows, fsdp, 4, head_cols).transpose(0, 2, 1, 3)

    grad_heads = collect_heads(grad_heads)
    grad_w_qkv = grad_heads[:, :3].reshape(rows, 3 * width).astype(SINGLE)
    grad_w_out = grad_heads[:, 3].reshape(rows, width).astype(SINGLE)

    grad_normed = norm_back(
        (grad_qkv_norm[0], grad_qkv_norm[1], grad_qkv_norm[2], grad_resid_norm)
    )
    stream_grads = [grad_normed[0], grad_normed[1], grad_normed[2], grad_normed[3] + grad_entry]
    grad_history = jnp.stack(
        [grad_sources[index] + blend(alpha[:, :, index], stream_grads) for index in range(entries)]
    )
    grad_mix_in = jnp.stack(
        [
            jnp.stack(
                [jnp.sum(stream_grads[stream] * sources[index], -1) for index in range(entries)], -1
            )
            for stream in range(stream_count)
        ],
        1,
    ).reshape(length, stream_count * entries)

    grad_gain_all = jnp.concatenate([grad_normed[4], grad_rms_gain[None]], 0)
    qkv_bias_all = lax.dynamic_update_index_in_dim(
        jnp.zeros((3, fsdp, head_cols), SINGLE), grad_qkv_bias, place, 1
    )
    first_bias_all = lax.dynamic_update_index_in_dim(
        jnp.zeros((2 * rep, hid_cols), SINGLE), grad_first_bias, core * rep + line, 0
    )
    tail = jnp.concatenate([grad_b_mix1, grad_w_mix2.reshape(-1), grad_b_mix2])
    sums = [
        grad_gain_all.reshape(3, devices, rows).transpose(1, 0, 2).reshape(devices, -1),
        grad_normed[5].reshape(2, devices, rows).transpose(1, 0, 2).reshape(devices, -1),
        qkv_bias_all.reshape(devices, -1),
        grad_branch_bias.reshape(devices, -1),
        first_bias_all.reshape(devices, -1),
        grad_w_mix1.reshape(devices, -1),
        jnp.broadcast_to(tail[None], (devices, tail.shape[0])),
    ]
    widths = [part.shape[1] for part in sums]
    total = jnp.sum(lax.all_to_all(jnp.concatenate(sums, 1), AXES, 0, 0, tiled=True), 0)
    outs, start = [], 0
    for size in widths:
        outs.append(total[start : start + size])
        start += size
    hid = b_mix1.shape[0]
    mixes = b_mix2.shape[0]
    return (
        next_streams,
        grad_history,
        grad_mix_in,
        outs[0].reshape(3, rows),
        outs[1].reshape(2, rows),
        grad_w_qkv,
        outs[2],
        grad_w_out,
        outs[3],
        grad_w_fc1,
        outs[4],
        grad_w_fc2,
        outs[3],
        outs[5].reshape(rows, hid),
        outs[6][:hid],
        outs[6][hid : hid + hid * mixes].reshape(hid, mixes),
        outs[6][hid + hid * mixes :],
    )


def solution(mesh):
    fsdp, rep = mesh.shape["fsdp"], mesh.shape["rep"]
    rows = P(AXES, None)
    line = P(AXES)
    streams = P(None, AXES, None)
    columns = P(None, AXES)
    in_specs = (
        streams,
        rows,
        rows,
        rows,
        P(),
        columns,
        columns,
        rows,
        line,
        rows,
        line,
        rows,
        line,
        rows,
        line,
        rows,
        P(),
        P(),
        P(),
        streams,
    )
    out_specs = (
        streams,
        streams,
        rows,
        columns,
        columns,
        rows,
        line,
        rows,
        line,
        rows,
        line,
        rows,
        line,
        rows,
        P(),
        P(),
        P(),
    )

    def local(*args):
        return on_device(fsdp, rep, *args)

    return jax.shard_map(
        local, mesh=mesh, in_specs=in_specs, out_specs=out_specs, check_vma=False
    )
```

```python
import functools
import math

import jax
import jax.numpy as jnp
from jax import lax
from jax.experimental import pallas as pl
from jax.experimental.pallas import tpu as pltpu
from jax.sharding import Mesh
from jax.sharding import PartitionSpec as P

HEAD_DIM = 128
ROT = 32
LANES = 128
NARROW = jnp.bfloat16
SINGLE = jnp.float32
NORM_EPSILON = 1e-05
RMS_EPSILON = 1e-06
AXES = ("chip", "core", "rep")
GROUP = ("core", "rep")
RING = ("chip", "core")
ROWS = 16
MIX_ROWS = 32
CHUNK = 512
VMEM_BYTES = 56 * 1024 * 1024
EXACT = lax.Precision.HIGHEST


def times(left, right, precision=None):
    return lax.dot_general(
        left, right, (((1,), (0,)), ((), ())), precision=precision, preferred_element_type=SINGLE
    )


def times_transposed(left, right, precision=None):
    return lax.dot_general(
        left, right, (((1,), (1,)), ((), ())), precision=precision, preferred_element_type=SINGLE
    )


def transposed_times(left, right, precision=None):
    return lax.dot_general(
        left, right, (((0,), (0,)), ((), ())), precision=precision, preferred_element_type=SINGLE
    )


def gelu_parts(values):
    cumulative = 0.5 * (1.0 + lax.erf(values * math.sqrt(0.5)))
    density = jnp.exp(-0.5 * values * values) * (1.0 / math.sqrt(2.0 * math.pi))
    return values * cumulative, cumulative + values * density


def params(*semantics):
    return pltpu.CompilerParams(vmem_limit_bytes=VMEM_BYTES)


def spec(shape, index=None):
    if index is None:
        index = lambda *i: (0,) * len(shape)
    return pl.BlockSpec(shape, index)


def scalar_spec():
    return pl.BlockSpec(memory_space=pltpu.SMEM)


def cost(flops, moved):
    return pl.CostEstimate(flops=flops // 1000, bytes_accessed=moved // 1000, transcendentals=0)


def mean(values):
    return jnp.mean(values, -1, keepdims=True)


def same_token(shape):
    row = lax.broadcasted_iota(jnp.int32, shape, 0)
    col = lax.broadcasted_iota(jnp.int32, shape, 1)
    return row == col % ROWS


def places(first, count):
    row = lax.broadcasted_iota(jnp.int32, (LANES, count * ROWS), 0)
    col = lax.broadcasted_iota(jnp.int32, (LANES, count * ROWS), 1)
    return (row == first + col // ROWS).astype(SINGLE)


def spread_out(coef, count, entries, stride):
    mask = same_token((ROWS, entries * ROWS))
    highs, lows = [], []
    for s in range(count):
        full = jnp.where(mask, times(coef, places(s * stride, entries), EXACT), 0.0)
        high = full.astype(NARROW)
        highs.append(high)
        lows.append((full - high.astype(SINGLE)).astype(NARROW))
    return jnp.concatenate(highs, 0), jnp.concatenate(lows, 0)


def draw_in(products, count, entries, stride):
    mask = same_token((ROWS, entries * ROWS))
    total = None
    for s in range(count):
        own = jnp.where(mask, products[s * ROWS : (s + 1) * ROWS], 0.0)
        term = times_transposed(own, places(s * stride, entries), EXACT)
        total = term if s == 0 else total + term
    return total


def blend_streams(hist, mix, streams):
    entries, _, width = hist.shape
    count = streams.shape[0]
    both = jnp.concatenate(spread_out(mix[...], count, entries, entries), 0)
    for start in range(0, width, CHUNK):
        sources = hist[:, :, start : start + CHUNK].reshape(entries * ROWS, CHUNK)
        total = times(both, sources)
        total = total[: count * ROWS] + total[count * ROWS :]
        streams[:, :, start : start + CHUNK] = total.reshape(count, ROWS, CHUNK)


def streams_kernel(chips, chip, hist, mix, affine, qkv, resid, last, streams):
    width = hist.shape[2]
    blend_streams(hist, mix, streams)
    for s in range(4):
        values = streams[s]
        center = values - mean(values)
        row = 0 if s < 3 else 2
        normed = (
            center * lax.rsqrt(mean(center * center) + NORM_EPSILON) * affine[row : row + 1]
            + affine[row + 1 : row + 2]
        )
        if s < 3:
            qkv[s] = normed.astype(NARROW)
        else:
            last[...] = values
            streams[0] = normed
    part = width // chips
    for m in range(chips):
        start = pl.multiple_of((chip[0] ^ m) * part, part)
        resid[:, m * part : (m + 1) * part] = streams[0, :, pl.ds(start, part)].astype(NARROW)


def history_dots_kernel(hist, cot, weight, out):
    entries, rows, width = hist.shape
    count = cot.shape[0]
    products = times_transposed(
        cot[...].reshape(count * rows, width), hist[...].reshape(entries * rows, width)
    )
    out[...] = draw_in(products, count, entries, entries + 1) * weight[...]


def mix_kernel(
    chips,
    near,
    rep,
    entries,
    chip,
    last,
    attn_own,
    *refs,
):
    attn_rest, mlp_parts, refs = refs[:near], refs[near : near + rep], refs[near + rep :]
    mix_body(chips, entries, chip, last, attn_own, attn_rest, mlp_parts, *refs)


def mix_body(
    chips,
    entries,
    chip,
    last,
    attn_own,
    attn_rest,
    mlp_parts,
    branch_bias,
    gain,
    first,
    first_bias,
    second,
    second_bias,
    cot,
    weight,
    dots,
    entry_out,
    grad_out,
    grad_low,
    grad_turned,
    scaled_out,
    grad_pre_low,
    act_out,
    grad_coef_out,
    coef_out,
    grad_gain,
    grad_bias,
    grad_pre_sum,
    grad_coef_sum,
    turned,
):
    rows, width = last.shape
    count = cot.shape[0]
    entry = last[...] + attn_own[...] + branch_bias[...]
    for part in attn_rest:
        entry = entry + part[...].astype(SINGLE)
    total = mlp_parts[0][...].astype(SINGLE)
    for values in mlp_parts[1:]:
        total = total + values[...].astype(SINGLE)
    part = width // chips
    for m in range(chips):
        start = pl.multiple_of((chip[0] ^ m) * part, part)
        turned[:, pl.ds(start, part)] = total[:, m * part : (m + 1) * part]
    entry = entry + turned[...]
    entry_out[...] = entry
    scale = lax.rsqrt(mean(entry * entry) + RMS_EPSILON)
    scaled = (entry * scale * gain[...]).astype(NARROW)
    scaled_out[...] = scaled
    pre = times(scaled, first[...]) + first_bias[...]
    act, slope = gelu_parts(pre)
    act_out[...] = act
    coef = times(act, second[...], EXACT) + second_bias[...]
    coef_out[...] = coef
    lane = lax.broadcasted_iota(jnp.int32, (rows, LANES), 1)
    grad_coef = dots[...]
    grad = jnp.zeros((rows, width), SINGLE)
    for s in range(count):
        arriving = cot[s].astype(SINGLE)
        place = s * (entries + 1) + entries
        total = jnp.sum(arriving * entry, -1, keepdims=True) * weight[...]
        grad_coef = jnp.where(lane == place, total, grad_coef)
        grad = grad + (coef[:, place : place + 1] * weight[...]) * arriving
    grad_coef_out[...] = grad_coef
    grad_pre = slope * times_transposed(grad_coef, second[...], EXACT)
    grad_pre_narrow = grad_pre.astype(NARROW)
    grad_pre_low[...] = grad_pre_narrow
    grad_scaled = times_transposed(grad_pre_narrow, first[...])
    gained = grad_scaled * gain[...]
    grad = grad + scale * gained - entry * (scale * scale * scale * mean(gained * entry))
    grad_out[...] = grad
    grad_low[...] = grad.astype(NARROW)
    for m in range(chips):
        start = pl.multiple_of((chip[0] ^ m) * part, part)
        grad_turned[:, m * part : (m + 1) * part] = grad_out[:, pl.ds(start, part)].astype(NARROW)

    @pl.when(pl.program_id(0) == 0)
    def _():
        grad_gain[...] = jnp.zeros_like(grad_gain)
        grad_bias[...] = jnp.zeros_like(grad_bias)
        grad_pre_sum[...] = jnp.zeros_like(grad_pre_sum)
        grad_coef_sum[...] = jnp.zeros_like(grad_coef_sum)

    grad_gain[...] += jnp.sum(grad_scaled * entry * scale, 0, keepdims=True)
    grad_bias[...] += jnp.sum(grad, 0, keepdims=True)
    grad_pre_sum[...] += jnp.sum(grad_pre, 0, keepdims=True)
    grad_coef_sum[...] += jnp.sum(grad_coef, 0, keepdims=True)


def next_kernel(hist, entry, coef, out):
    entries, _, width = hist.shape
    count = out.shape[0]
    both = jnp.concatenate(spread_out(coef[...], count, entries, entries + 1), 0)
    for start in range(0, width, CHUNK):
        cols = slice(start, start + CHUNK)
        sources = hist[:, :, cols].reshape(entries * ROWS, CHUNK)
        total = times(both, sources)
        total = total[: count * ROWS] + total[count * ROWS :]
        for s in range(count):
            place = s * (entries + 1) + entries
            out[s, :, cols] = (
                total[s * ROWS : (s + 1) * ROWS] + coef[:, place : place + 1] * entry[:, cols]
            ).astype(NARROW)


def close_kernel(
    chips,
    near,
    rep,
    chip,
    hist,
    cot,
    coef,
    weight,
    mix,
    affine,
    grad_entry,
    qkv_own,
    *refs,
):
    qkv_rest, resid, refs = refs[:near], refs[near : near + rep], refs[near + rep :]
    close_body(
        chips, chip, hist, cot, coef, weight, mix, affine, grad_entry, resid, qkv_own, qkv_rest, *refs
    )


def close_body(
    chips,
    chip,
    hist,
    cot,
    coef,
    weight,
    mix,
    affine,
    grad_entry,
    resid,
    qkv_own,
    qkv_rest,
    grad_hist,
    grad_mix,
    grad_affine,
    streams,
    turned,
    stacked,
):
    entries, rows, width = hist.shape
    count = cot.shape[0]
    part = width // chips

    @pl.when(pl.program_id(0) == 0)
    def _():
        grad_affine[...] = jnp.zeros_like(grad_affine)

    blend_streams(hist, mix, streams)
    for s in range(count):
        values = streams[s]
        center = values - mean(values)
        scale = lax.rsqrt(mean(center * center) + NORM_EPSILON)
        unit = center * scale
        if s < 3:
            arriving = qkv_own[s]
            for rest in qkv_rest:
                arriving = arriving + rest[s].astype(SINGLE)
        else:
            total = resid[0][...].astype(SINGLE)
            for rest in resid[1:]:
                total = total + rest[...].astype(SINGLE)
            for m in range(chips):
                start = pl.multiple_of((chip[0] ^ m) * part, part)
                turned[:, pl.ds(start, part)] = total[:, m * part : (m + 1) * part]
            arriving = turned[...]
        row = 0 if s < 3 else 2
        grad_affine[row : row + 1] += jnp.sum(arriving * unit, 0, keepdims=True)
        grad_affine[row + 1 : row + 2] += jnp.sum(arriving, 0, keepdims=True)
        gained = arriving * affine[row : row + 1]
        grad = scale * (gained - mean(gained) - unit * mean(gained * unit))
        streams[s] = grad if s < 3 else grad + grad_entry[...]
    size = count * rows
    grads = streams[...].reshape(size, width)
    high = grads.astype(NARROW)
    stacked[0:size] = high
    stacked[size : 2 * size] = (grads - high.astype(SINGLE)).astype(NARROW)
    stacked[2 * size : 3 * size] = high
    arriving = cot[...].reshape(size, width)
    stacked[3 * size : 4 * size] = arriving
    stacked[4 * size : 5 * size] = arriving
    mix_high, mix_low = spread_out(mix[...], count, entries, entries)
    out_high, out_low = spread_out(coef[...] * weight[...], count, entries, entries + 1)
    spread = jnp.concatenate([mix_high, mix_high, mix_low, out_high, out_low], 0)
    products = jnp.zeros((2 * size, entries * rows), SINGLE)
    for start in range(0, width, CHUNK):
        cols = slice(start, start + CHUNK)
        grad_hist[:, :, cols] = transposed_times(spread, stacked[:, cols]).reshape(
            entries, rows, CHUNK
        )
        sources = hist[:, :, cols].reshape(entries * rows, CHUNK)
        products = products + times_transposed(stacked[0 : 2 * size, cols], sources)
    products = products[:size] + products[size:]
    grad_mix[...] = draw_in(products, count, entries, entries)[:, : grad_mix.shape[1]]


def turn(values, rope, sign):
    forward = pltpu.roll(values, HEAD_DIM - ROT // 2, 1)
    backward = pltpu.roll(values, ROT // 2, 1)
    return values * rope[0] + sign * (forward * rope[1] + backward * rope[2])


def allowed_pairs(row, column, length):
    query = lax.broadcasted_iota(jnp.int32, (length, length), 0)
    key = lax.broadcasted_iota(jnp.int32, (length, length), 1)
    return (key <= query) & (row == column)


def probabilities(query, key, allowed):
    scores = jnp.where(allowed, times_transposed(query, key) * HEAD_DIM ** (-0.5), -1e30)
    raised = jnp.exp(scores - jnp.max(scores, -1, keepdims=True))
    return raised / jnp.sum(raised, -1, keepdims=True)


def attend_kernel(own, other, weight, bias, rope, doc_row, doc_column, qkv, mixed, out_own, out_other):
    _, length, _ = own.shape
    cols = bias.shape[1] // 3
    for i in range(3):
        tokens = jnp.concatenate([own[i], other[i]], 0)
        linear = times(tokens, weight[:, i * cols : (i + 1) * cols]) + bias[:, i * cols : (i + 1) * cols]
        if i == 2:
            qkv[i] = linear.astype(NARROW)
            continue
        for s in range(2):
            for start in range(0, cols, HEAD_DIM):
                piece = linear[s * length : (s + 1) * length, start : start + HEAD_DIM]
                qkv[i, s * length : (s + 1) * length, start : start + HEAD_DIM] = turn(
                    piece, rope, 1.0
                ).astype(NARROW)
    for s in range(2):
        allowed = allowed_pairs(doc_row[s], doc_column[s], length)
        rows = slice(s * length, (s + 1) * length)
        for start in range(0, cols, HEAD_DIM):
            head = slice(start, start + HEAD_DIM)
            probs = probabilities(qkv[0, rows, head], qkv[1, rows, head], allowed)
            mixed[rows, head] = times(probs.astype(NARROW), qkv[2, rows, head]).astype(NARROW)
    result = times_transposed(mixed[...], weight[:, 3 * cols :])
    out_own[...] = result[:length]
    out_other[...] = result[length:].astype(NARROW)


def attend_back_kernel(
    own, other, weight, qkv, rope, doc_row, doc_column, grad_linear, grad_bias, out_own, out_other
):
    length = own.shape[0]
    cols = qkv.shape[2]
    scale = HEAD_DIM ** (-0.5)
    arriving = jnp.concatenate([own[...], other[...]], 0)
    grad_mixed = times(arriving, weight[:, 3 * cols :]).astype(NARROW)
    for start in range(0, cols, HEAD_DIM):
        head = slice(start, start + HEAD_DIM)
        sums = [jnp.zeros((1, HEAD_DIM), SINGLE) for _ in range(3)]
        for s in range(2):
            allowed = allowed_pairs(doc_row[s], doc_column[s], length)
            rows = slice(s * length, (s + 1) * length)
            query, key, value = (qkv[i, rows, head] for i in range(3))
            grad = grad_mixed[rows, head]
            probs = probabilities(query, key, allowed)
            grad_value = transposed_times(probs.astype(NARROW), grad)
            grad_probs = times_transposed(grad, value)
            inner = jnp.sum(probs * grad_probs, -1, keepdims=True)
            grad_scores = (probs * (grad_probs - inner)).astype(NARROW)
            grad_query = turn(times(grad_scores, key) * scale, rope, -1.0)
            grad_key = turn(transposed_times(grad_scores, query) * scale, rope, -1.0)
            for i, values in enumerate((grad_query, grad_key, grad_value)):
                sums[i] = sums[i] + jnp.sum(values, 0, keepdims=True)
                grad_linear[i, rows, head] = values.astype(NARROW)
        for i in range(3):
            grad_bias[:, i * cols + start : i * cols + start + HEAD_DIM] = sums[i]
    for i in range(3):
        result = times_transposed(grad_linear[i], weight[:, i * cols : (i + 1) * cols])
        out_own[i] = result[:length]
        out_other[i] = result[length:].astype(NARROW)


def heads_grad_kernel(chips, *refs):
    norms, branches = refs[: 2 * chips], refs[2 * chips : 4 * chips]
    linears, mixeds, out = refs[4 * chips : 5 * chips], refs[5 * chips : 6 * chips], refs[6 * chips]
    cols = mixeds[0].shape[1]
    rep, _, rows, _ = out.shape
    for i in range(4):
        total = None
        for m in range(chips):
            sides = norms[2 * m : 2 * m + 2] if i < 3 else branches[2 * m : 2 * m + 2]
            left = jnp.concatenate([values[i] if i < 3 else values[...] for values in sides], 0)
            right = linears[m][i] if i < 3 else mixeds[m][...]
            term = transposed_times(left, right)
            total = term if total is None else total + term
        total = total.astype(NARROW)
        for k in range(rep):
            out[k, 0, :, i * cols : (i + 1) * cols] = total[k * rows : (k + 1) * rows]


def hidden_kernel(chips, tokens, *refs):
    weights, (bias, act_out, slope_out) = refs[:chips], refs[chips:]
    part = weights[0].shape[1]
    total = bias[...]
    for m in range(chips):
        total = total + times(tokens[:, m * part : (m + 1) * part], weights[m][0])
    act, slope = gelu_parts(total)
    act_out[...] = act.astype(NARROW)
    slope_out[...] = slope


def put_places(outs, length, cols, result):
    many = result.shape[0] // length
    for k, out in enumerate(outs):

        @pl.when(pl.program_id(0) == k // many)
        def _():
            out[:, cols] = result[(k % many) * length : (k % many + 1) * length].astype(NARROW)


def branch_kernel(chips, merged, act, *refs):
    weights, refs = refs[:chips], refs[chips:]
    part = weights[0].shape[1]
    for m in range(chips):
        cols = slice(m * part, (m + 1) * part)
        result = times_transposed(act[...], weights[m][0])
        if merged:
            put_places(refs[1:], refs[1].shape[0], cols, result + refs[0][:, cols].astype(SINGLE))
        else:
            refs[0][:, cols] = result.astype(NARROW)


def hidden_back_kernel(chips, merged, grad, slope, *refs):
    firsts, seconds, refs = refs[:chips], refs[chips : 2 * chips], refs[2 * chips :]
    came, refs = (refs[0], refs[1:]) if merged else (None, refs)
    grad_low, grad_sum, *outs = refs
    part = firsts[0].shape[1]
    total = None
    for m in range(chips):
        term = times(grad[:, m * part : (m + 1) * part], seconds[m][0])
        total = term if m == 0 else total + term
    total = total * slope[...]

    @pl.when(pl.program_id(0) == 0)
    def _():
        grad_sum[...] = jnp.zeros_like(grad_sum)

    grad_sum[...] += jnp.sum(total, 0, keepdims=True)
    low = total.astype(NARROW)
    grad_low[...] = low
    for m in range(chips):
        cols = slice(m * part, (m + 1) * part)
        result = times_transposed(low, firsts[m][0])
        if merged:
            put_places(outs, outs[0].shape[0], cols, result + came[:, cols].astype(SINGLE))
        else:
            outs[0][:, cols] = result.astype(NARROW)


def outer_kernel(left_own, left_other, right_own, right_other, *outs):
    result = (
        transposed_times(left_own[...], right_own[...])
        + transposed_times(left_other[...], right_other[...])
    ).astype(NARROW)
    for m, out in enumerate(outs):

        @pl.when(pl.program_id(0) == m)
        def _():
            out[...] = result


def merge_kernel(first, count, own, came, *refs):
    total = own[...] + came[...].astype(SINGLE)
    refs[-1][...] = total.astype(NARROW)
    if len(refs) > 1:

        @pl.when((pl.program_id(0) >= first) & (pl.program_id(0) < first + count))
        def _():
            refs[-1][...] = (total + refs[0][...].astype(SINGLE)).astype(NARROW)


def pack_hidden_kernel(rep, line, first, second, *outs):
    cols = outs[0].shape[3]
    for k in range(rep):
        for c in range(2):
            start = pl.multiple_of((c * rep + (line[0] ^ k)) * cols, cols)
            outs[k][c, 0] = first[:, pl.ds(start, cols)].astype(NARROW)
            outs[k][c, 1] = second[:, pl.ds(start, cols)].astype(NARROW)


def join_hidden_kernel(rep, core, line, swapped, *refs):
    owns, out = refs[:rep], refs[rep]
    for k in range(rep):
        for i in range(2):
            out[i, core[0], line[0] ^ k] = owns[k][core[0], i]
            out[i, 1 - core[0], line[0] ^ k] = swapped[k, i]


def pack_heads_kernel(query, key, value, out_weight, out):
    cols = query.shape[1]
    for i, weight in enumerate((query, key, value, out_weight)):
        out[0, :, i * cols : (i + 1) * cols] = weight[...].astype(NARROW)


class Order:
    def __init__(self, legal):
        self.legal = legal
        self.last = ()

    def hold(self, *values):
        tied = lax.optimization_barrier(tuple(values) + self.last)[: len(values)]
        return tied[0] if len(values) == 1 else tied

    def wait(self, *values):
        tied = lax.optimization_barrier(tuple(values) + self.last)[: len(values)]
        self.last = (tied[0],)
        return tied[0] if len(values) == 1 else list(tied)

    def scope(self, steps):
        inside = lambda: steps(Order(self.legal))
        shapes = jax.eval_shape(inside)
        never = lambda: jax.tree.map(lambda leaf: jnp.zeros(leaf.shape, leaf.dtype), shapes)
        results = lax.cond(self.hold(self.legal), inside, never)
        smallest = min(jax.tree.leaves(results), key=lambda leaf: leaf.size)
        self.last = (smallest,)
        return results


def on_device(
    chips,
    rep,
    history,
    mix_in,
    doc_ids,
    doc_group,
    group_weight,
    norm_gain,
    norm_bias,
    w_qkv,
    b_qkv,
    w_out,
    b_out,
    w_fc1,
    b_fc1,
    w_fc2,
    b_fc2,
    w_mix1,
    b_mix1,
    w_mix2,
    b_mix2,
    cotangent,
):
    entries, length, width = history.shape
    count = cotangent.shape[0]
    rows = w_qkv.shape[0]
    hidden = w_fc1.shape[1]
    hid = b_mix1.shape[0]
    mixes = b_mix2.shape[0]
    fsdp = 2 * chips
    group = 2 * rep
    devices = fsdp * rep
    cols = width // fsdp
    hid_cols = hidden // group
    part = width // chips
    chip = lax.axis_index("chip")
    core = lax.axis_index("core")
    line = lax.axis_index("rep")
    chip_at = chip.astype(jnp.int32).reshape(1)
    core_at = core.astype(jnp.int32).reshape(1)
    line_at = line.astype(jnp.int32).reshape(1)
    shape = jax.ShapeDtypeStruct

    def swap_core(values):
        return lax.ppermute(values, "core", [(0, 1), (1, 0)])

    def hop_chip(values, m):
        return lax.ppermute(values, "chip", [(i, i ^ m) for i in range(chips)])

    def hop_rep(values, k):
        return lax.ppermute(values, "rep", [(i, i ^ k) for i in range(rep)])

    def merge(own, came):
        return (own.astype(SINGLE) + came.astype(SINGLE)).astype(NARROW)

    def pieces(values, axis):
        size = values.shape[axis] // 2
        return (
            lax.slice_in_dim(values, 0, size, axis=axis),
            lax.slice_in_dim(values, size, 2 * size, axis=axis),
        )

    square = chips == 4
    around = range(1, 3 if square else chips)
    far = chips - 1

    def pass_on(first, axis):
        if not square:
            return ()
        return hop_chip(pieces(first[0], axis)[0], 2), hop_chip(pieces(first[1], axis)[1], 1)

    def joined_halves(halves, axis):
        return [jnp.concatenate(halves, axis)] if square else []

    def send_far(far, axis):
        if not square:
            return ()
        upper, lower = pieces(far, axis)
        return hop_chip(upper, 1), hop_chip(lower, 2)

    def take_along(terms, halves, axis):
        if not square:
            return terms
        upper, lower = halves
        near = pieces(terms[0], axis)
        far = pieces(terms[1], axis)
        return [
            jnp.concatenate([near[0], merge(near[1], lower)], axis),
            jnp.concatenate([merge(far[0], upper), far[1]], axis),
        ]

    order = Order(doc_ids[0, 0] >= 0)
    steps = length // ROWS
    block = 256
    blocks = rep * length // block
    tall = lambda n: spec((n, ROWS, width), lambda i: (0, i, 0))
    flat = lambda n: spec((ROWS, n), lambda i: (i, 0))
    tall2 = lambda n: spec((n, MIX_ROWS, width), lambda i: (0, i, 0))
    flat2 = lambda n: spec((MIX_ROWS, n), lambda i: (i, 0))
    token_block = lambda n: spec((block, n), lambda i: (i, 0))
    weight_specs = lambda which: [spec((1, part, hid_cols), lambda *_: (which, 0, 0))] * (
        3 if square else chips
    ) + [spec((1, part, hid_cols))] * square
    in_vmem = pl.BlockSpec(memory_space=pltpu.VMEM)

    small = (norm_gain, norm_bias, b_qkv, b_out, b_fc1, b_fc2, doc_ids)
    packed = jnp.concatenate([values.reshape(-1).astype(NARROW) for values in small])
    packed = order.wait(jnp.broadcast_to(packed[None], (devices, packed.shape[0])))
    gathered = lax.all_to_all(packed, AXES, 0, 0, tiled=True)
    hidden_sends = pl.pallas_call(
        functools.partial(pack_hidden_kernel, rep),
        in_specs=[scalar_spec()] + [in_vmem] * 2,
        out_shape=[shape((2, 2, rows, hid_cols), NARROW)] * rep,
        compiler_params=params(),
        cost_estimate=cost(10**6, 6 * 10**6),
        name="pack_hidden",
    )(line_at, *order.hold(w_fc1, w_fc2))
    hidden_sends = order.wait(*hidden_sends)
    head_block = lambda i: spec((rows, cols), lambda j: (0, i * fsdp + j))
    from_qkv, from_out = order.hold(w_qkv, w_out)
    heads_sends = pl.pallas_call(
        pack_heads_kernel,
        grid=(fsdp,),
        in_specs=[head_block(0), head_block(1), head_block(2), head_block(0)],
        out_specs=spec((1, rows, 4 * cols), lambda j: (j, 0, 0)),
        out_shape=shape((fsdp, rows, 4 * cols), NARROW),
        compiler_params=params(),
        cost_estimate=cost(10**6, 3 * 10**6),
        name="pack_heads",
    )(from_qkv, from_qkv, from_qkv, from_out)
    heads_sends = order.wait(heads_sends)
    mix_padded = order.wait(jnp.pad(mix_in, ((0, 0), (0, LANES - count * entries))))
    gathered = order.wait(gathered)
    heads_came = lax.all_to_all(order.hold(heads_sends), RING, 0, 0, tiled=True)
    hidden_going = order.hold(*hidden_sends)
    hidden_hops = [hop_rep(hidden_going[k], k) for k in range(1, rep)]

    def fields_of(gathered):
        fields, start = [], 0
        for values in small:
            fields.append(gathered[:, start : start + values.size])
            start += values.size
        return fields

    def open_layer(inner):
        fields = fields_of(gathered)
        gains = fields[0].reshape(devices, 3, rows).transpose(1, 0, 2).reshape(3, width)
        shifts = fields[1].reshape(devices, 2, rows).transpose(1, 0, 2).reshape(2, width)
        affine = jnp.stack([gains[0], shifts[0], gains[1], shifts[1]]).astype(SINGLE)
        normed = pl.pallas_call(
            functools.partial(streams_kernel, chips),
            grid=(steps,),
            in_specs=[scalar_spec(), tall(entries), flat(LANES), spec((4, width))],
            out_specs=[tall(3), flat(width), flat(width)],
            out_shape=[
                shape((3, length, width), NARROW),
                shape((length, width), NARROW),
                shape((length, width), SINGLE),
            ],
            scratch_shapes=[pltpu.VMEM((count, ROWS, width), SINGLE)],
            compiler_params=params(),
            cost_estimate=cost(10**8, 10**7),
            name="streams",
        )(chip_at, history, mix_padded, affine)
        normed = inner.wait(*normed)
        qkv_near = [hop_chip(normed[0], m) for m in around]
        documents, group_of, weight_of = inner.hold(doc_ids[0], doc_group[0], group_weight)
        doc_match = documents[:, None] == jnp.arange(doc_group.shape[1], dtype=jnp.int32)[None, :]
        token_group = jnp.sum(jnp.where(doc_match, group_of[None, :], 0), axis=1)
        group_match = (
            token_group[:, None] == jnp.arange(group_weight.shape[0], dtype=jnp.int32)[None, :]
        )
        token_weight = jnp.sum(jnp.where(group_match, weight_of[None, :], 0.0), 1, keepdims=True)
        dots = pl.pallas_call(
            history_dots_kernel,
            grid=(steps,),
            in_specs=[tall(entries), tall(count), flat(1)],
            out_specs=flat(LANES),
            out_shape=shape((length, LANES), SINGLE),
            compiler_params=params(),
            cost_estimate=cost(10**8, 10**7),
            name="history_dots",
        )(history, cotangent, token_weight)
        dots = inner.wait(dots)
        return normed, affine, dots, token_weight, inner.wait(*qkv_near)

    normed, affine, dots, token_weight, qkv_near = order.scope(open_layer)
    qkv_norm, resid_norm, last = normed
    heads_came = order.wait(heads_came)
    hidden_came = [hidden_sends[0], *order.wait(*hidden_hops)]

    first_mix = order.hold(w_mix1).astype(NARROW).reshape(1, -1)
    first_mix = order.wait(jnp.broadcast_to(first_mix, (devices, rows * hid)))
    first_mix = lax.all_to_all(first_mix, AXES, 0, 0, tiled=True)
    resid_norm = order.hold(resid_norm)
    resid_hops = [hop_rep(resid_norm, k) for k in range(1, rep)]

    def join_hidden(inner):
        for_other = jnp.stack(
            [lax.dynamic_index_in_dim(values, 1 - core, 0, False) for values in hidden_came]
        )
        joined = pl.pallas_call(
            functools.partial(join_hidden_kernel, rep),
            in_specs=[scalar_spec()] * 2 + [in_vmem] * (rep + 1),
            out_shape=shape((2, 2, rep, rows, hid_cols), NARROW),
            compiler_params=params(),
            cost_estimate=cost(10**6, 5 * 10**6),
            name="join_hidden",
        )(core_at, line_at, swap_core(for_other), *hidden_came)
        return joined.reshape(2, part, hid_cols)

    def prepare(inner):
        fields = fields_of(inner.hold(gathered))
        gain = fields[0].reshape(devices, 3, rows)[:, 2].reshape(1, width).astype(SINGLE)
        qkv_bias = fields[2].reshape(3, fsdp, cols).astype(SINGLE)
        branch_bias = fields[3].reshape(1, width).astype(SINGLE)
        branch_bias = branch_bias + fields[5].reshape(1, width).astype(SINGLE)
        first_bias = fields[4].reshape(group, hid_cols).astype(SINGLE)
        docs_all = fields[6].reshape(chips, 2, rep, length)
        my_qkv_bias = lax.dynamic_index_in_dim(qkv_bias, chip * 2 + core, 1, False)
        my_first_bias = lax.dynamic_index_in_dim(first_bias, core * rep + line, 0, True)
        docs_line = lax.dynamic_index_in_dim(docs_all, line, 2, False).astype(SINGLE)
        doc_rows = []
        for m in range(chips):
            pair = lax.dynamic_index_in_dim(docs_line, chip ^ m, 0, False)
            doc_rows.append(jnp.where(core == 0, pair, pair[::-1]))
        position = jnp.arange(length).astype(SINGLE)
        frequency = 10000.0 ** (-jnp.arange(0, ROT, 2).astype(SINGLE) / ROT)
        angle = position[:, None] * frequency[None, :]
        cosine, sine = jnp.cos(angle), jnp.sin(angle)
        nothing = jnp.zeros_like(sine)
        rest = HEAD_DIM - ROT
        rope = jnp.stack(
            [
                jnp.concatenate([cosine, cosine, jnp.ones((length, rest), SINGLE)], 1),
                jnp.concatenate([-sine, nothing, jnp.zeros((length, rest), SINGLE)], 1),
                jnp.concatenate([nothing, sine, jnp.zeros((length, rest), SINGLE)], 1),
            ]
        )
        pairs = [(pair[:, None, :], pair[:, :, None]) for pair in doc_rows]
        ready = (gain, my_qkv_bias.reshape(1, 3 * cols), my_first_bias, branch_bias, rope, pairs)
        leaves, tree = jax.tree.flatten(ready)
        return jax.tree.unflatten(tree, inner.wait(*leaves))

    def spread_weights(inner):
        joined = inner.scope(join_hidden)
        near = [hop_chip(joined, m) for m in around]
        prepared = inner.scope(prepare)
        near = inner.wait(*near)
        return joined, near, prepared

    hidden_own, hidden_near, prepared = order.scope(spread_weights)
    gain, my_qkv_bias, my_first_bias, branch_bias, rope, doc_pairs = prepared
    resid_hops = order.wait(*resid_hops)
    first_mix = order.wait(first_mix)

    heads_all = lax.all_gather(order.hold(heads_came), "rep", axis=0)

    def hidden_side(firsts, tokens):
        return pl.pallas_call(
            functools.partial(hidden_kernel, chips),
            grid=(blocks,),
            in_specs=[token_block(width)] + weight_specs(0) + [spec((1, hid_cols))],
            out_specs=[token_block(hid_cols)] * 2,
            out_shape=[
                shape((rep * length, hid_cols), NARROW),
                shape((rep * length, hid_cols), SINGLE),
            ],
            compiler_params=params(),
            cost_estimate=cost(2 * rep * length * width * hid_cols, 10**7),
            name="hidden",
        )(tokens, *firsts, my_first_bias)

    side = shape((rep * length, width), NARROW)
    places = [shape((length, width), NARROW)] * rep
    place_specs = [spec((length, width))] * rep

    def branch_side(seconds, act, *came):
        return pl.pallas_call(
            functools.partial(branch_kernel, chips, bool(came)),
            grid=(blocks,),
            in_specs=[token_block(hid_cols)] + weight_specs(1) + [token_block(width)] * len(came),
            out_specs=place_specs if came else token_block(width),
            out_shape=places if came else side,
            compiler_params=params(),
            cost_estimate=cost(2 * rep * length * width * hid_cols, 10**7),
            name="branch",
        )(act, *seconds, *came)


    qkv_first = [qkv_norm, *qkv_near]

    def feed_forward(inner):
        ends = []
        mix_first = jnp.pad(inner.hold(first_mix).reshape(width, hid), ((0, 0), (0, LANES - hid)))
        if square:
            upper = hop_chip(inner.hold(hidden_near[0])[0:1], 2)
            lower = hop_chip(inner.hold(hidden_near[1])[1:2], 1)
        whole = inner.wait(jnp.stack([resid_norm, *resid_hops]))
        other = inner.wait(swap_core(whole))
        qkv_other = inner.scope(lambda _: [swap_core(values) for values in qkv_first])
        mix_first = inner.wait(mix_first)
        if square:
            ends = inner.wait(upper, lower)
            halves = pass_on(inner.hold(*qkv_near), 1)
        firsts = [hidden_own, *hidden_near, *ends[:1]]
        seconds = [hidden_own, *hidden_near, *ends[1:]]
        sides = [values.reshape(rep * length, width) for values in (whole, other)]
        act_other, slope_other = inner.wait(*hidden_side(firsts, inner.hold(sides[1])))

        def branch_both(inner):
            back = inner.wait(branch_side(seconds, act_other))
            came = swap_core(back)
            act_own, slope_own = inner.wait(*hidden_side(firsts, inner.hold(sides[0])))
            return act_own, slope_own, branch_side(seconds, act_own, inner.wait(came))

        act_own, slope_own, branch_places = inner.scope(branch_both)
        qkv_last = []
        if square:
            qkv_last.append(inner.wait(jnp.concatenate(inner.wait(*halves), 1)))
            qkv_other.append(inner.wait(swap_core(qkv_last[0])))
        acts, slopes = (act_own, act_other), (slope_own, slope_other)
        return ends, sides, acts, slopes, branch_places, qkv_last, qkv_other, mix_first

    ends, resid_sides, acts, slopes, branch_places, qkv_last, qkv_other, mix_first = order.scope(
        feed_forward
    )
    first_parts = [hidden_own, *hidden_near, *ends[:1]]
    second_parts = [hidden_own, *hidden_near, *ends[1:]]
    qkv_own = [*qkv_first, *qkv_last]
    heads_all = order.wait(heads_all)

    branch_places = order.hold(*branch_places)
    mlp_hops = [hop_rep(branch_places[k], k) for k in range(1, rep)]

    def attend(heads, own, other, m):
        return pl.pallas_call(
            attend_kernel,
            out_shape=[
                shape((3, 2 * length, cols), NARROW),
                shape((2 * length, cols), NARROW),
                shape((length, width), SINGLE),
                shape((length, width), NARROW),
            ],
            compiler_params=params(),
            cost_estimate=cost(4 * 2 * 2 * length * width * cols, 8 * 10**6),
            name="attend",
        )(own, other, heads, my_qkv_bias, rope, *doc_pairs[m])


    def add_up(own, came, first=0, *along):
        rows_of = 32
        half = length // 2 // rows_of
        block_of = lambda index: spec((3, rows_of, width), index)
        return pl.pallas_call(
            functools.partial(merge_kernel, first, half),
            grid=(2 * half,),
            in_specs=[block_of(lambda i: (0, i, 0))] * 2
            + [block_of(lambda i: (0, jnp.clip(i - first, 0, half - 1), 0))] * len(along),
            out_specs=block_of(lambda i: (0, i, 0)),
            out_shape=shape(own.shape, NARROW),
            compiler_params=params(),
            cost_estimate=cost(10**6, 10**7),
            name="merge",
        )(own, came, *along)

    def near_sums(inner, results, came, halves):
        terms = []
        for m in around:
            along = ()
            if square:
                along = (length // 2 // 32, halves[1]) if m == 1 else (0, halves[0])
            terms.append(inner.wait(add_up(results[m], came[m], *along)))
        return terms

    def attention(inner):
        heads = inner.wait(heads_all.transpose(1, 0, 2, 3).reshape(width, 4 * cols))
        results, came = [None] * chips, [None] * chips

        def step(m):
            own, other = inner.hold(qkv_own[m], qkv_other[m])
            results[m] = inner.wait(*attend(heads, own, other, m))

        step(far)
        came[far] = swap_core(inner.hold(results[far][3]))
        step(1)
        came[far] = inner.wait(came[far])
        halves = None
        if square:
            halves = send_far(inner.wait(merge(results[far][2], came[far])), 0)
        for m in range(2, far):
            step(m)
        if square:
            halves = inner.wait(*halves)
        middle = range(1, far)
        swapped = inner.wait(swap_core(inner.wait(jnp.stack([results[m][3] for m in middle]))))
        for m in middle:
            came[m] = swapped[m - 1]
        terms = [merge(results[m][2], came[m]) for m in around]
        terms = inner.wait(*take_along(terms, halves, 0))
        hops = [hop_chip(terms[m - 1], m) for m in around]
        step(0)
        hops = inner.wait(*hops)
        came[0] = inner.wait(swap_core(inner.hold(results[0][3])))
        lows = [values[0] for values in results]
        return heads, lows, [values[1] for values in results], results[0][2], [came[0], *hops]

    heads, qkv_low, mixed_low, attn_own, attn_rest = order.scope(attention)
    mlp_parts = [branch_places[0], *order.wait(*mlp_hops)]

    mix_second = jnp.pad(w_mix2, ((0, LANES - hid), (0, LANES - mixes)))
    mixed_results = pl.pallas_call(
        functools.partial(mix_kernel, chips, len(attn_rest), rep, entries),
        grid=(length // MIX_ROWS,),
        in_specs=[
            scalar_spec(),
            flat2(width),
            flat2(width),
            *[flat2(width)] * (len(attn_rest) + rep),
            spec((1, width)),
            spec((1, width)),
            spec((width, LANES)),
            spec((1, LANES)),
            spec((LANES, LANES)),
            spec((1, LANES)),
            tall2(count),
            flat2(1),
            flat2(LANES),
        ],
        out_specs=[flat2(width)] * 5
        + [flat2(LANES)] * 4
        + [spec((1, width))] * 2
        + [spec((1, LANES))] * 2,
        out_shape=[
            shape((length, width), SINGLE),
            shape((length, width), SINGLE),
            shape((length, width), NARROW),
            shape((length, width), NARROW),
            shape((length, width), NARROW),
            shape((length, LANES), NARROW),
            shape((length, LANES), SINGLE),
            shape((length, LANES), SINGLE),
            shape((length, LANES), SINGLE),
            shape((1, width), SINGLE),
            shape((1, width), SINGLE),
            shape((1, LANES), SINGLE),
            shape((1, LANES), SINGLE),
        ],
        scratch_shapes=[pltpu.VMEM((MIX_ROWS, width), SINGLE)],
        compiler_params=params(),
        cost_estimate=cost(2 * 10**8, 10**7),
        name="mixing",
    )(
        chip_at,
        last,
        attn_own,
        *attn_rest,
        *mlp_parts,
        branch_bias,
        gain,
        mix_first,
        jnp.pad(b_mix1, (0, LANES - hid))[None],
        mix_second,
        jnp.pad(b_mix2, (0, LANES - mixes))[None],
        cotangent,
        token_weight,
        dots,
    )
    (
        entry,
        grad_entry,
        grad_low,
        grad_turned,
        scaled_low,
        grad_pre_low,
        mix_act,
        grad_coef,
        coef,
        grad_rms_gain,
        grad_branch_bias,
        grad_pre_sum,
        grad_coef_sum,
    ) = order.wait(*mixed_results)

    grad_hops = [hop_rep(grad_turned, k) for k in range(1, rep)]

    def attend_back(own, other, heads, qkv, rope, pair):
        return pl.pallas_call(
            attend_back_kernel,
            out_shape=[
                shape((3, 2 * length, cols), NARROW),
                shape((1, 3 * cols), SINGLE),
                shape((3, length, width), SINGLE),
                shape((3, length, width), NARROW),
            ],
            compiler_params=params(),
            cost_estimate=cost(4 * 2 * 2 * length * width * cols, 8 * 10**6),
            name="attend_back",
        )(own, other, heads, qkv, rope, *pair)


    def back(inner, m, own, other):
        own, other = inner.hold(own, other)
        return inner.wait(*attend_back(own, other, heads, qkv_low[m], rope, doc_pairs[m]))

    def spread_branch(inner):
        swapped = inner.wait(swap_core(grad_low))
        near = [hop_chip(inner.hold(grad_low), m) for m in around]
        result = back(inner, 0, grad_low, swapped)
        near = inner.wait(*near)
        halves = pass_on(near, 0)
        next_streams = pl.pallas_call(
            next_kernel,
            grid=(steps,),
            in_specs=[tall(entries), flat(width), flat(LANES)],
            out_specs=tall(count),
            out_shape=shape((count, length, width), NARROW),
            compiler_params=params(),
            cost_estimate=cost(10**8, 10**7),
            name="next_streams",
        )(inner.hold(history), entry, coef)
        next_streams = inner.wait(next_streams)
        if square:
            near.append(inner.wait(jnp.concatenate(inner.wait(*halves), 0)))
        others = list(swap_core(jnp.stack(near)))
        others = inner.wait(*others)
        last = back(inner, far, near[far - 1], others[far - 1])
        grad_w_mix2 = transposed_times(mix_act, grad_coef, EXACT)[:hid, :mixes]
        grad_w_mix1 = transposed_times(scaled_low, grad_pre_low)[:, :hid]
        grad_w_mix1, grad_w_mix2 = inner.wait(grad_w_mix1, grad_w_mix2)
        return result, last, near, [swapped, *others], next_streams, grad_w_mix1, grad_w_mix2

    returned, terms = [None] * chips, [None] * chips
    returned[0], returned[far], branch_near, branch_other, *rest = order.scope(spread_branch)
    next_streams, grad_w_mix1, grad_w_mix2 = rest
    branch_own = [grad_low, *branch_near]
    grad_hops = order.wait(*grad_hops)

    interleave = lambda a, b: [values for pair in zip(a, b) for values in pair]
    row_block = width // fsdp

    def hidden_back_side(firsts, seconds, grad, slope, *came):
        return pl.pallas_call(
            functools.partial(hidden_back_kernel, chips, bool(came)),
            grid=(blocks,),
            in_specs=[token_block(width), token_block(hid_cols)]
            + weight_specs(0)
            + weight_specs(1)
            + [token_block(width)] * len(came),
            out_specs=[token_block(hid_cols), spec((1, hid_cols))]
            + (place_specs if came else [token_block(width)]),
            out_shape=[shape((rep * length, hid_cols), NARROW), shape((1, hid_cols), SINGLE)]
            + (places if came else [side]),
            compiler_params=params(),
            cost_estimate=cost(4 * rep * length * width * hid_cols, 2 * 10**7),
            name="hidden_back",
        )(grad, slope, *firsts, *seconds, *came)

    def outer(inner, lefts, rights):
        whole = lambda n: spec((rep * length, n))
        return inner.wait(
            *pl.pallas_call(
                outer_kernel,
                grid=(chips,),
                in_specs=[spec((rep * length, part), lambda i: (0, i))] * 2 + [whole(hid_cols)] * 2,
                out_specs=[spec((part, hid_cols))] * chips,
                out_shape=[shape((part, hid_cols), NARROW)] * chips,
                compiler_params=params(),
                cost_estimate=cost(4 * rep * length * width * hid_cols, 2 * 10**7),
                name="outer",
            )(*lefts, *rights)
        )

    def feed_forward_back(inner):
        whole = inner.wait(jnp.stack([grad_turned, *grad_hops]))
        came = [swap_core(returned[far][3]), swap_core(whole), swap_core(returned[0][3])]
        grad_own = whole.reshape(rep * length, width)
        low_own, sum_own, back_own = inner.wait(
            *hidden_back_side(first_parts, second_parts, inner.hold(grad_own), slopes[0])
        )
        came = inner.wait(*came)
        far_term = inner.wait(add_up(returned[far][2], came[0]))
        halves = send_far(far_term, 1) if square else ()

        def other_side(inner):
            grad_sides = (grad_own, came[1].reshape(rep * length, width))
            low_other, sum_other, back = inner.wait(
                *hidden_back_side(first_parts, second_parts, grad_sides[1], slopes[1])
            )
            back = swap_core(back)
            grads = outer(inner, (inner.hold(grad_sides[0]), grad_sides[1]), acts)
            back = inner.wait(back)
            merged = [
                merge(back_own[k * length : (k + 1) * length], back[k * length : (k + 1) * length])
                for k in range(rep)
            ]
            return grads, low_other, sum_own + sum_other, merged

        grads, low_other, first_bias, merged = inner.scope(other_side)
        halves = inner.wait(*halves) if square else [far_term]
        return grads, low_own, low_other, first_bias, merged, halves, came[0], came[2]

    second_grads, low_own, low_other, grad_first_bias, grad_resid, halves, far_came, own_came = (
        order.scope(feed_forward_back)
    )

    def attention_back(inner):
        results = {0: returned[0], far: returned[far]}
        middle = range(1, far)
        swaps = []
        for m in middle:
            results[m] = back(inner, m, branch_own[m], branch_other[m])
            swaps.append(swap_core(results[m][3]))
        linears = inner.hold(*[results[m][0] for m in range(chips)])
        grad_heads = pl.pallas_call(
            functools.partial(heads_grad_kernel, chips),
            grid=(fsdp,),
            in_specs=[spec((3, length, row_block), lambda i: (0, 0, i))] * fsdp
            + [spec((length, row_block), lambda i: (0, i))] * fsdp
            + [spec((3, 2 * length, cols))] * chips
            + [spec((2 * length, cols))] * chips,
            out_specs=spec((rep, 1, rows, 4 * cols), lambda i: (0, i, 0, 0)),
            out_shape=shape((rep, fsdp, rows, 4 * cols), NARROW),
            compiler_params=params(),
            cost_estimate=cost(8 * fsdp * length * width * cols, 3 * 10**7),
            name="heads_grad",
        )(
            *interleave(qkv_own, qkv_other),
            *interleave(branch_own, branch_other),
            *linears,
            *mixed_low,
        )
        grad_heads = inner.wait(grad_heads)
        swaps = inner.wait(*swaps)
        owns = [results[m][2] for m in range(chips)]
        near_terms = near_sums(inner, owns, [None, *swaps, far_came], halves)
        return grad_heads, near_terms, [results[m][1] for m in range(chips)]

    def residual_back(inner):
        hops = inner.hold(*grad_resid)
        hops = [hop_rep(hops[k], k) for k in range(1, rep)]
        results = inner.scope(attention_back)
        return inner.wait(*hops), *results

    resid_hops, grad_heads, near_terms, qkv_biases = order.scope(residual_back)
    grad_resid = [grad_resid[0], *resid_hops]

    def by_owner(vector):
        return vector.reshape(-1, devices, rows).transpose(1, 0, 2).reshape(devices, -1)

    grad_heads = lax.psum_scatter(grad_heads, "rep", scatter_dimension=0, tiled=False)
    widths = [rows, 3 * cols * fsdp // devices, rows, rows * hid]
    held_bias = order.hold(grad_branch_bias)
    qkv_bias_all = lax.dynamic_update_index_in_dim(
        jnp.zeros((3, fsdp, cols), SINGLE), sum(qkv_biases).reshape(3, cols), chip * 2 + core, 1
    )
    tail = jnp.concatenate(
        [grad_pre_sum[0, :hid], grad_w_mix2.reshape(-1), grad_coef_sum[0, :mixes]]
    )
    sums = [
        by_owner(grad_rms_gain[0]),
        qkv_bias_all.reshape(devices, -1),
        held_bias.reshape(devices, -1),
        grad_w_mix1.reshape(devices, -1),
        jnp.broadcast_to(tail[None], (devices, tail.shape[0])),
    ]
    sums = order.wait(jnp.concatenate(sums, 1))
    sums = lax.all_to_all(sums, AXES, 0, 0, tiled=True)

    def total_hidden(inner, own, hops):
        total = own.astype(SINGLE)
        for values in inner.wait(*hops):
            total = total + values.astype(SINGLE)
        return inner.wait(total.astype(NARROW).reshape(group, rows, hid_cols))

    def whole_rows(came):
        return came.transpose(1, 0, 2).reshape(rows, hidden).astype(SINGLE)

    def exchange(sums):
        widths = [values.shape[1] for values in sums]
        return widths, lax.all_to_all(jnp.concatenate(sums, 1), AXES, 0, 0, tiled=True)

    def send_terms(inner):
        held = inner.hold(*near_terms)
        qkv_back = [hop_chip(held[m - 1], m) for m in around]
        first_grads = outer(inner, (inner.hold(resid_sides[0]), resid_sides[1]), (low_own, low_other))
        return first_grads, inner.wait(*qkv_back)

    first_grads, qkv_back = order.scope(send_terms)

    def near_of(inner, grads):
        halves = send_far(inner.hold(grads[far]), 0)
        if not square:
            return inner.wait(*grads[1:])
        halves = inner.wait(*halves)
        return inner.wait(*take_along(grads[1:far], halves, 0))

    qkv_rest = [own_came, *qkv_back]

    def close_layer(inner):
        held = near_of(inner, second_grads)
        second_hops = [hop_chip(held[m - 1], m) for m in around]
        close_from = inner.hold(history, cotangent)
        grad_history, grad_mix_in, grad_affine = pl.pallas_call(
            functools.partial(close_kernel, chips, len(qkv_rest), rep),
            grid=(steps,),
            in_specs=[
                scalar_spec(),
                tall(entries),
                tall(count),
                flat(LANES),
                flat(1),
                flat(LANES),
                spec((4, width)),
                flat(width),
                *[tall(3)] * (1 + len(qkv_rest)),
                *[flat(width)] * rep,
            ],
            out_specs=[tall(entries), flat(count * entries), spec((4, width))],
            out_shape=[
                shape((entries, length, width), SINGLE),
                shape((length, count * entries), SINGLE),
                shape((4, width), SINGLE),
            ],
            scratch_shapes=[
                pltpu.VMEM((count, ROWS, width), SINGLE),
                pltpu.VMEM((ROWS, width), SINGLE),
                pltpu.VMEM((5 * count * ROWS, width), NARROW),
            ],
            compiler_params=params(),
            cost_estimate=cost(2 * 10**8, 2 * 10**7),
            name="close",
        )(
            chip_at,
            *close_from,
            coef,
            token_weight,
            mix_padded,
            affine,
            grad_entry,
            returned[0][2],
            *qkv_rest,
            *grad_resid,
        )
        grad_history, grad_mix_in, grad_affine = inner.wait(grad_history, grad_mix_in, grad_affine)

        return grad_history, grad_mix_in, grad_affine, total_hidden(inner, second_grads[0], second_hops)

    grad_history, grad_mix_in, grad_affine, second_total = order.scope(close_layer)
    sums = order.wait(sums)
    second_came = lax.all_to_all(order.hold(second_total), GROUP, 0, 0, tiled=True)

    def collect_first(inner):
        held = near_of(inner, first_grads)
        first_hops = [hop_chip(held[m - 1], m) for m in around]
        total = inner.wait(jnp.sum(inner.hold(sums), 0))
        return total, total_hidden(inner, first_grads[0], first_hops)

    total, first_total = order.scope(collect_first)
    second_came = order.wait(second_came)
    first_bias_all = lax.dynamic_update_index_in_dim(
        jnp.zeros((group, hid_cols), SINGLE), grad_first_bias[0], core * rep + line, 0
    )
    every = order.wait(
        jnp.concatenate([by_owner(grad_affine), first_bias_all.reshape(devices, -1)], 1)
    )
    every = order.wait(lax.all_to_all(every, AXES, 0, 0, tiled=True))
    first_came = lax.all_to_all(order.hold(first_total), GROUP, 0, 0, tiled=True)
    grad_w_fc2 = order.wait(whole_rows(second_came))
    every = order.wait(jnp.sum(every, 0))
    grad_heads = order.wait(grad_heads)

    def around_ring(inner):
        split = inner.hold(grad_heads).reshape(chips, 2, rows, 4 * cols)
        parts = [lax.dynamic_index_in_dim(split, chip ^ m, 0, False) for m in range(chips)]
        parts = [parts[0]] + [hop_chip(parts[m], m) for m in range(1, chips)]
        parts = jnp.stack(inner.wait(*parts))
        mine = lax.dynamic_index_in_dim(parts, core, 1, False)
        came = swap_core(lax.dynamic_index_in_dim(parts, 1 - core, 1, False))
        result = jnp.zeros((chips, 2, rows, 4 * cols), NARROW)
        for m in range(chips):
            pair = jnp.where(core == 0, jnp.stack([mine[m], came[m]]), jnp.stack([came[m], mine[m]]))
            result = lax.dynamic_update_index_in_dim(result, pair, chip ^ m, 0)
        result = result.reshape(fsdp, rows, 4, cols).transpose(1, 2, 0, 3).astype(SINGLE)
        return result[:, :3].reshape(rows, 3 * width), result[:, 3].reshape(rows, width)

    grad_w_qkv, grad_w_out = order.scope(around_ring)
    first_came = order.wait(first_came)
    grad_w_fc1 = whole_rows(first_came)
    outs, start = [], 0
    for size in widths:
        outs.append(total[start : start + size])
        start += size
    outs.append(total[start:])
    affine_sums = every[: 4 * rows].reshape(4, rows)
    gain_grads = jnp.stack([affine_sums[0], affine_sums[2], outs[0]])
    bias_grads = jnp.stack([affine_sums[1], affine_sums[3]])
    return (
        next_streams,
        grad_history,
        grad_mix_in,
        gain_grads,
        bias_grads,
        grad_w_qkv,
        outs[1],
        grad_w_out,
        outs[2],
        grad_w_fc1,
        every[4 * rows :],
        grad_w_fc2,
        outs[2],
        outs[3].reshape(rows, hid),
        outs[4][:hid],
        outs[4][hid : hid + hid * mixes].reshape(hid, mixes),
        outs[4][hid + hid * mixes :],
    )


def solution(mesh):
    fsdp, rep = mesh.shape["fsdp"], mesh.shape["rep"]
    chips = fsdp // 2
    finer = Mesh(mesh.devices.reshape(chips, 2, rep), AXES)
    rows = P(AXES, None)
    line = P(AXES)
    streams = P(None, AXES, None)
    columns = P(None, AXES)
    in_specs = (
        streams,
        rows,
        rows,
        rows,
        P(),
        columns,
        columns,
        rows,
        line,
        rows,
        line,
        rows,
        line,
        rows,
        line,
        rows,
        P(),
        P(),
        P(),
        streams,
    )
    out_specs = (
        streams,
        streams,
        rows,
        columns,
        columns,
        rows,
        line,
        rows,
        line,
        rows,
        line,
        rows,
        line,
        rows,
        P(),
        P(),
        P(),
    )
    return jax.shard_map(
        functools.partial(on_device, chips, rep),
        mesh=finer,
        in_specs=in_specs,
        out_specs=out_specs,
        check_vma=False,
    )
```

```python
import functools
import math

import jax
import jax.numpy as jnp
from jax import lax
from jax.experimental import pallas as pl
from jax.experimental.pallas import tpu as pltpu
from jax.sharding import Mesh
from jax.sharding import PartitionSpec as P

HEAD_DIM = 128
ROT = 32
LANES = 128
NARROW = jnp.bfloat16
SINGLE = jnp.float32
NORM_EPSILON = 1e-05
RMS_EPSILON = 1e-06
AXES = ("chip", "core", "rep")
GROUP = ("core", "rep")
RING = ("chip", "core")
ROWS = 16
MIX_ROWS = 32
CHUNK = 512
VMEM_BYTES = 56 * 1024 * 1024
EXACT = lax.Precision.HIGHEST


def times(left, right, precision=None):
    return lax.dot_general(
        left, right, (((1,), (0,)), ((), ())), precision=precision, preferred_element_type=SINGLE
    )


def times_transposed(left, right, precision=None):
    return lax.dot_general(
        left, right, (((1,), (1,)), ((), ())), precision=precision, preferred_element_type=SINGLE
    )


def transposed_times(left, right, precision=None):
    return lax.dot_general(
        left, right, (((0,), (0,)), ((), ())), precision=precision, preferred_element_type=SINGLE
    )


def gelu_parts(values):
    cumulative = 0.5 * (1.0 + lax.erf(values * math.sqrt(0.5)))
    density = jnp.exp(-0.5 * values * values) * (1.0 / math.sqrt(2.0 * math.pi))
    return values * cumulative, cumulative + values * density


def params(*semantics):
    return pltpu.CompilerParams(vmem_limit_bytes=VMEM_BYTES)


def spec(shape, index=None):
    if index is None:
        index = lambda *i: (0,) * len(shape)
    return pl.BlockSpec(shape, index)


def scalar_spec():
    return pl.BlockSpec(memory_space=pltpu.SMEM)


def cost(flops, moved):
    return pl.CostEstimate(flops=flops // 1000, bytes_accessed=moved // 1000, transcendentals=0)


def mean(values):
    return jnp.mean(values, -1, keepdims=True)


def same_token(shape):
    row = lax.broadcasted_iota(jnp.int32, shape, 0)
    col = lax.broadcasted_iota(jnp.int32, shape, 1)
    return row == col % ROWS


def places(first, count):
    row = lax.broadcasted_iota(jnp.int32, (LANES, count * ROWS), 0)
    col = lax.broadcasted_iota(jnp.int32, (LANES, count * ROWS), 1)
    return (row == first + col // ROWS).astype(NARROW)


def two_parts(values):
    high = values.astype(NARROW)
    return jnp.concatenate([high, (values - high.astype(SINGLE)).astype(NARROW)], 0)


def spread_out(coef, count, entries, stride):
    mask = same_token((ROWS, entries * ROWS))
    parts = two_parts(coef)
    highs, lows = [], []
    for s in range(count):
        full = times(parts, places(s * stride, entries))
        highs.append(jnp.where(mask, full[:ROWS], 0.0).astype(NARROW))
        lows.append(jnp.where(mask, full[ROWS:], 0.0).astype(NARROW))
    return jnp.concatenate(highs, 0), jnp.concatenate(lows, 0)


def draw_in(products, count, entries, stride):
    mask = same_token((ROWS, entries * ROWS))
    total = None
    for s in range(count):
        own = jnp.where(mask, products[s * ROWS : (s + 1) * ROWS], 0.0)
        term = times_transposed(two_parts(own), places(s * stride, entries))
        total = term if s == 0 else total + term
    return total[:ROWS] + total[ROWS:]


def blend_streams(hist, mix, streams):
    entries, _, width = hist.shape
    count = streams.shape[0]
    both = jnp.concatenate(spread_out(mix[...], count, entries, entries), 0)
    for start in range(0, width, CHUNK):
        sources = hist[:, :, start : start + CHUNK].reshape(entries * ROWS, CHUNK)
        total = times(both, sources)
        total = total[: count * ROWS] + total[count * ROWS :]
        streams[:, :, start : start + CHUNK] = total.reshape(count, ROWS, CHUNK)


def streams_kernel(chips, chip, hist, mix, affine, qkv, resid, last, streams):
    width = hist.shape[2]
    blend_streams(hist, mix, streams)
    for s in range(4):
        values = streams[s]
        center = values - mean(values)
        row = 0 if s < 3 else 2
        normed = (
            center * lax.rsqrt(mean(center * center) + NORM_EPSILON) * affine[row : row + 1]
            + affine[row + 1 : row + 2]
        )
        if s < 3:
            qkv[s] = normed.astype(NARROW)
        else:
            last[...] = values
            streams[0] = normed
    part = width // chips
    for m in range(chips):
        start = pl.multiple_of((chip[0] ^ m) * part, part)
        resid[:, m * part : (m + 1) * part] = streams[0, :, pl.ds(start, part)].astype(NARROW)


def history_dots_kernel(hist, cot, weight, out):
    entries, rows, width = hist.shape
    count = cot.shape[0]
    products = times_transposed(
        cot[...].reshape(count * rows, width), hist[...].reshape(entries * rows, width)
    )
    out[...] = draw_in(products, count, entries, entries + 1) * weight[...]


def mix_kernel(
    chips,
    near,
    rep,
    entries,
    chip,
    last,
    attn_own,
    *refs,
):
    attn_rest, mlp_parts, refs = refs[:near], refs[near : near + rep], refs[near + rep :]
    mix_body(chips, entries, chip, last, attn_own, attn_rest, mlp_parts, *refs)


def mix_body(
    chips,
    entries,
    chip,
    last,
    attn_own,
    attn_rest,
    mlp_parts,
    branch_bias,
    gain,
    first,
    first_bias,
    second,
    second_bias,
    cot,
    weight,
    dots,
    entry_out,
    grad_out,
    grad_low,
    grad_turned,
    scaled_out,
    grad_pre_low,
    act_out,
    grad_coef_out,
    coef_out,
    grad_gain,
    grad_bias,
    grad_pre_sum,
    grad_coef_sum,
    turned,
):
    rows, width = last.shape
    count = cot.shape[0]
    entry = last[...] + attn_own[...] + branch_bias[...]
    for part in attn_rest:
        entry = entry + part[...].astype(SINGLE)
    total = mlp_parts[0][...].astype(SINGLE)
    for values in mlp_parts[1:]:
        total = total + values[...].astype(SINGLE)
    part = width // chips
    for m in range(chips):
        start = pl.multiple_of((chip[0] ^ m) * part, part)
        turned[:, pl.ds(start, part)] = total[:, m * part : (m + 1) * part]
    entry = entry + turned[...]
    entry_out[...] = entry
    scale = lax.rsqrt(mean(entry * entry) + RMS_EPSILON)
    scaled = (entry * scale * gain[...]).astype(NARROW)
    scaled_out[...] = scaled
    pre = times(scaled, first[...]) + first_bias[...]
    act, slope = gelu_parts(pre)
    act_out[...] = act
    coef = times(act, second[...], EXACT) + second_bias[...]
    coef_out[...] = coef
    lane = lax.broadcasted_iota(jnp.int32, (rows, LANES), 1)
    grad_coef = dots[...]
    grad = jnp.zeros((rows, width), SINGLE)
    for s in range(count):
        arriving = cot[s].astype(SINGLE)
        place = s * (entries + 1) + entries
        total = jnp.sum(arriving * entry, -1, keepdims=True) * weight[...]
        grad_coef = jnp.where(lane == place, total, grad_coef)
        grad = grad + (coef[:, place : place + 1] * weight[...]) * arriving
    grad_coef_out[...] = grad_coef
    grad_pre = slope * times_transposed(grad_coef, second[...], EXACT)
    grad_pre_narrow = grad_pre.astype(NARROW)
    grad_pre_low[...] = grad_pre_narrow
    grad_scaled = times_transposed(grad_pre_narrow, first[...])
    gained = grad_scaled * gain[...]
    grad = grad + scale * gained - entry * (scale * scale * scale * mean(gained * entry))
    grad_out[...] = grad
    grad_low[...] = grad.astype(NARROW)
    for m in range(chips):
        start = pl.multiple_of((chip[0] ^ m) * part, part)
        grad_turned[:, m * part : (m + 1) * part] = grad_out[:, pl.ds(start, part)].astype(NARROW)

    @pl.when(pl.program_id(0) == 0)
    def _():
        grad_gain[...] = jnp.zeros_like(grad_gain)
        grad_bias[...] = jnp.zeros_like(grad_bias)
        grad_pre_sum[...] = jnp.zeros_like(grad_pre_sum)
        grad_coef_sum[...] = jnp.zeros_like(grad_coef_sum)

    grad_gain[...] += jnp.sum(grad_scaled * entry * scale, 0, keepdims=True)
    grad_bias[...] += jnp.sum(grad, 0, keepdims=True)
    grad_pre_sum[...] += jnp.sum(grad_pre, 0, keepdims=True)
    grad_coef_sum[...] += jnp.sum(grad_coef, 0, keepdims=True)


def next_kernel(hist, entry, coef, out):
    entries, _, width = hist.shape
    count = out.shape[0]
    both = jnp.concatenate(spread_out(coef[...], count, entries, entries + 1), 0)
    for start in range(0, width, CHUNK):
        cols = slice(start, start + CHUNK)
        sources = hist[:, :, cols].reshape(entries * ROWS, CHUNK)
        total = times(both, sources)
        total = total[: count * ROWS] + total[count * ROWS :]
        for s in range(count):
            place = s * (entries + 1) + entries
            out[s, :, cols] = (
                total[s * ROWS : (s + 1) * ROWS] + coef[:, place : place + 1] * entry[:, cols]
            ).astype(NARROW)


def close_kernel(
    chips,
    near,
    rep,
    chip,
    hist,
    cot,
    coef,
    weight,
    mix,
    affine,
    grad_entry,
    qkv_own,
    *refs,
):
    qkv_rest, resid, refs = refs[:near], refs[near : near + rep], refs[near + rep :]
    close_body(
        chips, chip, hist, cot, coef, weight, mix, affine, grad_entry, resid, qkv_own, qkv_rest, *refs
    )


def close_body(
    chips,
    chip,
    hist,
    cot,
    coef,
    weight,
    mix,
    affine,
    grad_entry,
    resid,
    qkv_own,
    qkv_rest,
    grad_hist,
    grad_mix,
    grad_affine,
    streams,
    turned,
    stacked,
):
    entries, rows, width = hist.shape
    count = cot.shape[0]
    part = width // chips

    @pl.when(pl.program_id(0) == 0)
    def _():
        grad_affine[...] = jnp.zeros_like(grad_affine)

    blend_streams(hist, mix, streams)
    for s in range(count):
        values = streams[s]
        center = values - mean(values)
        scale = lax.rsqrt(mean(center * center) + NORM_EPSILON)
        unit = center * scale
        if s < 3:
            arriving = qkv_own[s]
            for rest in qkv_rest:
                arriving = arriving + rest[s].astype(SINGLE)
        else:
            total = resid[0][...].astype(SINGLE)
            for rest in resid[1:]:
                total = total + rest[...].astype(SINGLE)
            for m in range(chips):
                start = pl.multiple_of((chip[0] ^ m) * part, part)
                turned[:, pl.ds(start, part)] = total[:, m * part : (m + 1) * part]
            arriving = turned[...]
        row = 0 if s < 3 else 2
        grad_affine[row : row + 1] += jnp.sum(arriving * unit, 0, keepdims=True)
        grad_affine[row + 1 : row + 2] += jnp.sum(arriving, 0, keepdims=True)
        gained = arriving * affine[row : row + 1]
        grad = scale * (gained - mean(gained) - unit * mean(gained * unit))
        streams[s] = grad if s < 3 else grad + grad_entry[...]
    size = count * rows
    grads = streams[...].reshape(size, width)
    high = grads.astype(NARROW)
    stacked[0:size] = high
    stacked[size : 2 * size] = (grads - high.astype(SINGLE)).astype(NARROW)
    stacked[2 * size : 3 * size] = high
    arriving = cot[...].reshape(size, width)
    stacked[3 * size : 4 * size] = arriving
    stacked[4 * size : 5 * size] = arriving
    mix_high, mix_low = spread_out(mix[...], count, entries, entries)
    out_high, out_low = spread_out(coef[...] * weight[...], count, entries, entries + 1)
    spread = jnp.concatenate([mix_high, mix_high, mix_low, out_high, out_low], 0)
    products = jnp.zeros((2 * size, entries * rows), SINGLE)
    for start in range(0, width, CHUNK):
        cols = slice(start, start + CHUNK)
        grad_hist[:, :, cols] = transposed_times(spread, stacked[:, cols]).reshape(
            entries, rows, CHUNK
        )
        sources = hist[:, :, cols].reshape(entries * rows, CHUNK)
        products = products + times_transposed(stacked[0 : 2 * size, cols], sources)
    products = products[:size] + products[size:]
    grad_mix[...] = draw_in(products, count, entries, entries)[:, : grad_mix.shape[1]]


def turn(values, rope, sign):
    forward = pltpu.roll(values, HEAD_DIM - ROT // 2, 1)
    backward = pltpu.roll(values, ROT // 2, 1)
    return values * rope[0] + sign * (forward * rope[1] + backward * rope[2])


def allowed_pairs(row, column):
    size = row.shape[1]
    query = lax.broadcasted_iota(jnp.int32, (size, size), 0)
    key = lax.broadcasted_iota(jnp.int32, (size, size), 1)
    return (key <= query) & (row == column)


def probabilities(query, key, allowed):
    scores = jnp.where(allowed, times_transposed(query, key) * HEAD_DIM ** (-0.5), -1e30)
    raised = jnp.exp(scores - jnp.max(scores, -1, keepdims=True))
    return raised / jnp.sum(raised, -1, keepdims=True)


def attend_kernel(own, other, weight, bias, rope, doc_row, doc_column, qkv, mixed, out_own, out_other):
    _, length, _ = own.shape
    cols = bias.shape[1] // 3
    for i in range(3):
        tokens = jnp.concatenate([own[i], other[i]], 0)
        linear = times(tokens, weight[:, i * cols : (i + 1) * cols]) + bias[:, i * cols : (i + 1) * cols]
        for start in range(0, cols, HEAD_DIM):
            head = slice(start, start + HEAD_DIM)
            piece = linear[:, head]
            qkv[i, :, head] = (turn(piece, rope, 1.0) if i < 2 else piece).astype(NARROW)
    allowed = allowed_pairs(doc_row[...], doc_column[...])
    for start in range(0, cols, HEAD_DIM):
        head = slice(start, start + HEAD_DIM)
        probs = probabilities(qkv[0, :, head], qkv[1, :, head], allowed)
        mixed[:, head] = times(probs.astype(NARROW), qkv[2, :, head]).astype(NARROW)
    result = times_transposed(mixed[...], weight[:, 3 * cols :])
    out_own[...] = result[:length]
    out_other[...] = result[length:].astype(NARROW)


def attend_back_kernel(
    own, other, weight, qkv, rope, doc_row, doc_column, grad_linear, grad_bias, out_own, out_other
):
    length = own.shape[0]
    cols = qkv.shape[2]
    scale = HEAD_DIM ** (-0.5)
    arriving = jnp.concatenate([own[...], other[...]], 0)
    grad_mixed = times(arriving, weight[:, 3 * cols :]).astype(NARROW)
    allowed = allowed_pairs(doc_row[...], doc_column[...])
    for start in range(0, cols, HEAD_DIM):
        head = slice(start, start + HEAD_DIM)
        query, key, value = (qkv[i, :, head] for i in range(3))
        grad = grad_mixed[:, head]
        probs = probabilities(query, key, allowed)
        grad_value = transposed_times(probs.astype(NARROW), grad)
        grad_probs = times_transposed(grad, value)
        inner = jnp.sum(probs * grad_probs, -1, keepdims=True)
        grad_scores = (probs * (grad_probs - inner)).astype(NARROW)
        grad_query = turn(times(grad_scores, key) * scale, rope, -1.0)
        grad_key = turn(transposed_times(grad_scores, query) * scale, rope, -1.0)
        for i, values in enumerate((grad_query, grad_key, grad_value)):
            grad_bias[:, i * cols + start : i * cols + start + HEAD_DIM] = jnp.sum(
                values, 0, keepdims=True
            )
            grad_linear[i, :, head] = values.astype(NARROW)
    for i in range(3):
        result = times_transposed(grad_linear[i], weight[:, i * cols : (i + 1) * cols])
        out_own[i] = result[:length]
        out_other[i] = result[length:].astype(NARROW)


def heads_grad_kernel(chips, *refs):
    norms, branches = refs[: 2 * chips], refs[2 * chips : 4 * chips]
    linears, mixeds, out = refs[4 * chips : 5 * chips], refs[5 * chips : 6 * chips], refs[6 * chips]
    cols = mixeds[0].shape[1]
    rep, _, rows, _ = out.shape
    for i in range(4):
        total = None
        for m in range(chips):
            sides = norms[2 * m : 2 * m + 2] if i < 3 else branches[2 * m : 2 * m + 2]
            left = jnp.concatenate([values[i] if i < 3 else values[...] for values in sides], 0)
            right = linears[m][i] if i < 3 else mixeds[m][...]
            term = transposed_times(left, right)
            total = term if total is None else total + term
        total = total.astype(NARROW)
        for k in range(rep):
            out[k, 0, :, i * cols : (i + 1) * cols] = total[k * rows : (k + 1) * rows]


def hidden_kernel(chips, tokens, *refs):
    weights, (bias, act_out, slope_out) = refs[:chips], refs[chips:]
    part = weights[0].shape[1]
    total = bias[...]
    for m in range(chips):
        total = total + times(tokens[:, m * part : (m + 1) * part], weights[m][0])
    act, slope = gelu_parts(total)
    act_out[...] = act.astype(NARROW)
    slope_out[...] = slope


def put_places(outs, length, cols, result):
    many = result.shape[0] // length
    for k, out in enumerate(outs):

        @pl.when(pl.program_id(0) == k // many)
        def _():
            out[:, cols] = result[(k % many) * length : (k % many + 1) * length].astype(NARROW)


def branch_kernel(chips, merged, act, *refs):
    weights, refs = refs[:chips], refs[chips:]
    part = weights[0].shape[1]
    for m in range(chips):
        cols = slice(m * part, (m + 1) * part)
        result = times_transposed(act[...], weights[m][0])
        if merged:
            put_places(refs[1:], refs[1].shape[0], cols, result + refs[0][:, cols].astype(SINGLE))
        else:
            refs[0][:, cols] = result.astype(NARROW)


def hidden_back_kernel(chips, merged, grad, slope, *refs):
    firsts, seconds, refs = refs[:chips], refs[chips : 2 * chips], refs[2 * chips :]
    came, refs = (refs[0], refs[1:]) if merged else (None, refs)
    grad_low, grad_sum, *outs = refs
    part = firsts[0].shape[1]
    total = None
    for m in range(chips):
        term = times(grad[:, m * part : (m + 1) * part], seconds[m][0])
        total = term if m == 0 else total + term
    total = total * slope[...]

    @pl.when(pl.program_id(0) == 0)
    def _():
        grad_sum[...] = jnp.zeros_like(grad_sum)

    grad_sum[...] += jnp.sum(total, 0, keepdims=True)
    low = total.astype(NARROW)
    grad_low[...] = low
    for m in range(chips):
        cols = slice(m * part, (m + 1) * part)
        result = times_transposed(low, firsts[m][0])
        if merged:
            put_places(outs, outs[0].shape[0], cols, result + came[:, cols].astype(SINGLE))
        else:
            outs[0][:, cols] = result.astype(NARROW)


def outer_kernel(left_own, left_other, right_own, right_other, *outs):
    result = (
        transposed_times(left_own[...], right_own[...])
        + transposed_times(left_other[...], right_other[...])
    ).astype(NARROW)
    for m, out in enumerate(outs):

        @pl.when(pl.program_id(0) == m)
        def _():
            out[...] = result


def merge_kernel(first, count, own, came, *refs):
    total = own[...] + came[...].astype(SINGLE)
    refs[-1][...] = total.astype(NARROW)
    if len(refs) > 1:

        @pl.when((pl.program_id(0) >= first) & (pl.program_id(0) < first + count))
        def _():
            refs[-1][...] = (total + refs[0][...].astype(SINGLE)).astype(NARROW)


def pack_hidden_kernel(rep, line, first, second, *outs):
    cols = outs[0].shape[3]
    for k in range(rep):
        for c in range(2):
            start = pl.multiple_of((c * rep + (line[0] ^ k)) * cols, cols)
            outs[k][c, 0] = first[:, pl.ds(start, cols)].astype(NARROW)
            outs[k][c, 1] = second[:, pl.ds(start, cols)].astype(NARROW)


def join_hidden_kernel(rep, core, line, swapped, *refs):
    owns, out = refs[:rep], refs[rep]
    for k in range(rep):
        for i in range(2):
            out[i, core[0], line[0] ^ k] = owns[k][core[0], i]
            out[i, 1 - core[0], line[0] ^ k] = swapped[k, i]


def pack_heads_kernel(query, key, value, out_weight, out):
    cols = query.shape[1]
    for i, weight in enumerate((query, key, value, out_weight)):
        out[0, :, i * cols : (i + 1) * cols] = weight[...].astype(NARROW)


class Order:
    def __init__(self, legal):
        self.legal = legal
        self.last = ()

    def hold(self, *values):
        tied = lax.optimization_barrier(tuple(values) + self.last)[: len(values)]
        return tied[0] if len(values) == 1 else tied

    def wait(self, *values):
        tied = lax.optimization_barrier(tuple(values) + self.last)[: len(values)]
        self.last = (tied[0],)
        return tied[0] if len(values) == 1 else list(tied)

    def scope(self, steps):
        inside = lambda: steps(Order(self.legal))
        shapes = jax.eval_shape(inside)
        never = lambda: jax.tree.map(lambda leaf: jnp.zeros(leaf.shape, leaf.dtype), shapes)
        results = lax.cond(self.hold(self.legal), inside, never)
        smallest = min(jax.tree.leaves(results), key=lambda leaf: leaf.size)
        self.last = (smallest,)
        return results


def on_device(
    chips,
    rep,
    history,
    mix_in,
    doc_ids,
    doc_group,
    group_weight,
    norm_gain,
    norm_bias,
    w_qkv,
    b_qkv,
    w_out,
    b_out,
    w_fc1,
    b_fc1,
    w_fc2,
    b_fc2,
    w_mix1,
    b_mix1,
    w_mix2,
    b_mix2,
    cotangent,
):
    entries, length, width = history.shape
    count = cotangent.shape[0]
    rows = w_qkv.shape[0]
    hidden = w_fc1.shape[1]
    hid = b_mix1.shape[0]
    mixes = b_mix2.shape[0]
    fsdp = 2 * chips
    group = 2 * rep
    devices = fsdp * rep
    cols = width // fsdp
    hid_cols = hidden // group
    part = width // chips
    chip = lax.axis_index("chip")
    core = lax.axis_index("core")
    line = lax.axis_index("rep")
    chip_at = chip.astype(jnp.int32).reshape(1)
    core_at = core.astype(jnp.int32).reshape(1)
    line_at = line.astype(jnp.int32).reshape(1)
    shape = jax.ShapeDtypeStruct

    def swap_core(values):
        return lax.ppermute(values, "core", [(0, 1), (1, 0)])

    def hop_chip(values, m):
        return lax.ppermute(values, "chip", [(i, i ^ m) for i in range(chips)])

    def hop_rep(values, k):
        return lax.ppermute(values, "rep", [(i, i ^ k) for i in range(rep)])

    def merge(own, came):
        return (own.astype(SINGLE) + came.astype(SINGLE)).astype(NARROW)

    def pieces(values, axis):
        size = values.shape[axis] // 2
        return (
            lax.slice_in_dim(values, 0, size, axis=axis),
            lax.slice_in_dim(values, size, 2 * size, axis=axis),
        )

    square = chips == 4
    around = range(1, 3 if square else chips)
    far = chips - 1

    def pass_on(first, axis):
        if not square:
            return ()
        return hop_chip(pieces(first[0], axis)[0], 2), hop_chip(pieces(first[1], axis)[1], 1)

    def joined_halves(halves, axis):
        return [jnp.concatenate(halves, axis)] if square else []

    def send_far(far, axis):
        if not square:
            return ()
        upper, lower = pieces(far, axis)
        return hop_chip(upper, 1), hop_chip(lower, 2)

    def take_along(terms, halves, axis):
        if not square:
            return terms
        upper, lower = halves
        near = pieces(terms[0], axis)
        far = pieces(terms[1], axis)
        return [
            jnp.concatenate([near[0], merge(near[1], lower)], axis),
            jnp.concatenate([merge(far[0], upper), far[1]], axis),
        ]

    order = Order(doc_ids[0, 0] >= 0)
    steps = length // ROWS
    block = 256
    blocks = rep * length // block
    tall = lambda n: spec((n, ROWS, width), lambda i: (0, i, 0))
    flat = lambda n: spec((ROWS, n), lambda i: (i, 0))
    tall2 = lambda n: spec((n, MIX_ROWS, width), lambda i: (0, i, 0))
    flat2 = lambda n: spec((MIX_ROWS, n), lambda i: (i, 0))
    token_block = lambda n: spec((block, n), lambda i: (i, 0))
    weight_specs = lambda which: [spec((1, part, hid_cols), lambda *_: (which, 0, 0))] * (
        3 if square else chips
    ) + [spec((1, part, hid_cols))] * square
    in_vmem = pl.BlockSpec(memory_space=pltpu.VMEM)

    small = (norm_gain, norm_bias, b_qkv, b_out, b_fc1, b_fc2, doc_ids)
    packed = jnp.concatenate([values.reshape(-1).astype(NARROW) for values in small])
    packed = order.wait(jnp.broadcast_to(packed[None], (devices, packed.shape[0])))
    gathered = lax.all_to_all(packed, AXES, 0, 0, tiled=True)
    hidden_sends = pl.pallas_call(
        functools.partial(pack_hidden_kernel, rep),
        in_specs=[scalar_spec()] + [in_vmem] * 2,
        out_shape=[shape((2, 2, rows, hid_cols), NARROW)] * rep,
        compiler_params=params(),
        cost_estimate=cost(10**6, 6 * 10**6),
        name="pack_hidden",
    )(line_at, *order.hold(w_fc1, w_fc2))
    hidden_sends = order.wait(*hidden_sends)
    head_block = lambda i: spec((rows, cols), lambda j: (0, i * fsdp + j))
    from_qkv, from_out = order.hold(w_qkv, w_out)
    heads = pl.pallas_call(
        pack_heads_kernel,
        grid=(fsdp,),
        in_specs=[head_block(0), head_block(1), head_block(2), head_block(0)],
        out_specs=spec((1, rows, 4 * cols), lambda j: (j, 0, 0)),
        out_shape=shape((fsdp, rows, 4 * cols), NARROW),
        compiler_params=params(),
        cost_estimate=cost(10**6, 3 * 10**6),
        name="pack_heads",
    )(from_qkv, from_qkv, from_qkv, from_out)
    heads = order.wait(heads)
    gathered = order.wait(gathered)
    hidden_going = order.hold(*hidden_sends)
    hidden_hops = [hop_rep(hidden_going[k], k) for k in range(1, rep)]
    heads_came = lax.all_to_all(order.hold(heads), RING, 0, 0, tiled=True)

    def fields_of(gathered):
        fields, start = [], 0
        for values in small:
            fields.append(gathered[:, start : start + values.size])
            start += values.size
        return fields

    def open_layer(inner):
        mix_padded = jnp.pad(mix_in, ((0, 0), (0, LANES - count * entries)))
        fields = fields_of(gathered)
        gains = fields[0].reshape(devices, 3, rows).transpose(1, 0, 2).reshape(3, width)
        shifts = fields[1].reshape(devices, 2, rows).transpose(1, 0, 2).reshape(2, width)
        affine = jnp.stack([gains[0], shifts[0], gains[1], shifts[1]]).astype(SINGLE)
        normed = pl.pallas_call(
            functools.partial(streams_kernel, chips),
            grid=(steps,),
            in_specs=[scalar_spec(), tall(entries), flat(LANES), spec((4, width))],
            out_specs=[tall(3), flat(width), flat(width)],
            out_shape=[
                shape((3, length, width), NARROW),
                shape((length, width), NARROW),
                shape((length, width), SINGLE),
            ],
            scratch_shapes=[pltpu.VMEM((count, ROWS, width), SINGLE)],
            compiler_params=params(),
            cost_estimate=cost(10**8, 10**7),
            name="streams",
        )(chip_at, history, mix_padded, affine)
        normed = inner.wait(*normed)
        qkv_near = [hop_chip(normed[0], m) for m in around]
        documents, group_of, weight_of = inner.hold(doc_ids[0], doc_group[0], group_weight)
        doc_match = documents[:, None] == jnp.arange(doc_group.shape[1], dtype=jnp.int32)[None, :]
        token_group = jnp.sum(jnp.where(doc_match, group_of[None, :], 0), axis=1)
        group_match = (
            token_group[:, None] == jnp.arange(group_weight.shape[0], dtype=jnp.int32)[None, :]
        )
        token_weight = jnp.sum(jnp.where(group_match, weight_of[None, :], 0.0), 1, keepdims=True)
        dots = pl.pallas_call(
            history_dots_kernel,
            grid=(steps,),
            in_specs=[tall(entries), tall(count), flat(1)],
            out_specs=flat(LANES),
            out_shape=shape((length, LANES), SINGLE),
            compiler_params=params(),
            cost_estimate=cost(10**8, 10**7),
            name="history_dots",
        )(history, cotangent, token_weight)
        dots = inner.wait(dots)
        return normed, affine, dots, token_weight, inner.wait(*qkv_near), mix_padded

    normed, affine, dots, token_weight, qkv_near, mix_padded = order.scope(open_layer)
    heads_came = order.wait(heads_came)
    qkv_norm, resid_norm, last = normed
    hidden_came = [hidden_sends[0], *order.wait(*hidden_hops)]

    resid_norm = order.hold(resid_norm)
    resid_hops = [hop_rep(resid_norm, k) for k in range(1, rep)]

    def join_hidden(inner):
        for_other = jnp.stack(
            [lax.dynamic_index_in_dim(values, 1 - core, 0, False) for values in hidden_came]
        )
        joined = pl.pallas_call(
            functools.partial(join_hidden_kernel, rep),
            in_specs=[scalar_spec()] * 2 + [in_vmem] * (rep + 1),
            out_shape=shape((2, 2, rep, rows, hid_cols), NARROW),
            compiler_params=params(),
            cost_estimate=cost(10**6, 5 * 10**6),
            name="join_hidden",
        )(core_at, line_at, swap_core(for_other), *hidden_came)
        return joined.reshape(2, part, hid_cols)

    def prepare(inner):
        mix_copies = jnp.pad(w_mix1.astype(NARROW), ((0, 0), (0, LANES - hid)))
        mix_copies = inner.wait(jnp.broadcast_to(mix_copies[None], (devices, rows, LANES)))
        fields = fields_of(inner.hold(gathered))
        gain = fields[0].reshape(devices, 3, rows)[:, 2].reshape(1, width).astype(SINGLE)
        qkv_bias = fields[2].reshape(3, fsdp, cols).astype(SINGLE)
        branch_bias = fields[3].reshape(1, width).astype(SINGLE)
        branch_bias = branch_bias + fields[5].reshape(1, width).astype(SINGLE)
        first_bias = fields[4].reshape(group, hid_cols).astype(SINGLE)
        docs_all = fields[6].reshape(chips, 2, rep, length)
        my_qkv_bias = lax.dynamic_index_in_dim(qkv_bias, chip * 2 + core, 1, False)
        my_first_bias = lax.dynamic_index_in_dim(first_bias, core * rep + line, 0, True)
        docs_line = lax.dynamic_index_in_dim(docs_all, line, 2, False).astype(SINGLE)
        doc_rows = []
        for m in range(chips):
            pair = lax.dynamic_index_in_dim(docs_line, chip ^ m, 0, False)
            pair = pair + doc_group.shape[1] * jnp.arange(2, dtype=SINGLE)[:, None]
            doc_rows.append(jnp.where(core == 0, pair, pair[::-1]).reshape(1, 2 * length))
        position = jnp.arange(length).astype(SINGLE)
        frequency = 10000.0 ** (-jnp.arange(0, ROT, 2).astype(SINGLE) / ROT)
        angle = position[:, None] * frequency[None, :]
        cosine, sine = jnp.cos(angle), jnp.sin(angle)
        nothing = jnp.zeros_like(sine)
        rest = HEAD_DIM - ROT
        rope = jnp.stack(
            [
                jnp.concatenate([cosine, cosine, jnp.ones((length, rest), SINGLE)], 1),
                jnp.concatenate([-sine, nothing, jnp.zeros((length, rest), SINGLE)], 1),
                jnp.concatenate([nothing, sine, jnp.zeros((length, rest), SINGLE)], 1),
            ]
        )
        rope = jnp.concatenate([rope, rope], 1)
        pairs = [(pair, pair.reshape(2 * length, 1)) for pair in doc_rows]
        ready = (gain, my_qkv_bias.reshape(1, 3 * cols), my_first_bias, branch_bias, rope, pairs)
        leaves, tree = jax.tree.flatten(ready)
        return mix_copies, jax.tree.unflatten(tree, inner.wait(*leaves))

    def spread_weights(inner):
        joined = inner.scope(join_hidden)
        near = [hop_chip(joined, m) for m in around]
        mix_copies, prepared = inner.scope(prepare)
        first_mix = lax.all_to_all(inner.hold(mix_copies), AXES, 0, 0, tiled=True)
        near = inner.wait(*near)
        return joined, near, inner.wait(first_mix).reshape(width, LANES), prepared

    hidden_own, hidden_near, mix_first, prepared = order.scope(spread_weights)
    gain, my_qkv_bias, my_first_bias, branch_bias, rope, doc_pairs = prepared
    resid_hops = order.wait(*resid_hops)

    heads_all = lax.all_gather(order.hold(heads_came), "rep", axis=0)

    def hidden_side(firsts, tokens):
        return pl.pallas_call(
            functools.partial(hidden_kernel, chips),
            grid=(blocks,),
            in_specs=[token_block(width)] + weight_specs(0) + [spec((1, hid_cols))],
            out_specs=[token_block(hid_cols)] * 2,
            out_shape=[
                shape((rep * length, hid_cols), NARROW),
                shape((rep * length, hid_cols), SINGLE),
            ],
            compiler_params=params(),
            cost_estimate=cost(2 * rep * length * width * hid_cols, 10**7),
            name="hidden",
        )(tokens, *firsts, my_first_bias)

    side = shape((rep * length, width), NARROW)
    places = [shape((length, width), NARROW)] * rep
    place_specs = [spec((length, width))] * rep

    def branch_side(seconds, act, *came):
        return pl.pallas_call(
            functools.partial(branch_kernel, chips, bool(came)),
            grid=(blocks,),
            in_specs=[token_block(hid_cols)] + weight_specs(1) + [token_block(width)] * len(came),
            out_specs=place_specs if came else token_block(width),
            out_shape=places if came else side,
            compiler_params=params(),
            cost_estimate=cost(2 * rep * length * width * hid_cols, 10**7),
            name="branch",
        )(act, *seconds, *came)


    qkv_first = [qkv_norm, *qkv_near]

    def feed_forward(inner):
        ends = []
        if square:
            upper = hop_chip(inner.hold(hidden_near[0])[0:1], 2)
            lower = hop_chip(inner.hold(hidden_near[1])[1:2], 1)
        whole = inner.wait(jnp.stack([resid_norm, *resid_hops]))
        other = inner.wait(swap_core(whole))
        qkv_other = inner.scope(lambda _: [swap_core(values) for values in qkv_first])
        if square:
            ends = inner.wait(upper, lower)
            halves = pass_on(inner.hold(*qkv_near), 1)
        firsts = [hidden_own, *hidden_near, *ends[:1]]
        seconds = [hidden_own, *hidden_near, *ends[1:]]
        sides = [values.reshape(rep * length, width) for values in (whole, other)]
        act_other, slope_other = inner.wait(*hidden_side(firsts, inner.hold(sides[1])))

        def branch_both(inner):
            back = inner.wait(branch_side(seconds, act_other))
            came = swap_core(back)
            act_own, slope_own = inner.wait(*hidden_side(firsts, inner.hold(sides[0])))
            return act_own, slope_own, branch_side(seconds, act_own, inner.wait(came))

        act_own, slope_own, branch_places = inner.scope(branch_both)
        qkv_last = []
        if square:
            qkv_last.append(inner.wait(jnp.concatenate(inner.wait(*halves), 1)))
            qkv_other.append(inner.wait(swap_core(qkv_last[0])))
        acts, slopes = (act_own, act_other), (slope_own, slope_other)
        return ends, sides, acts, slopes, branch_places, qkv_last, qkv_other

    ends, resid_sides, acts, slopes, branch_places, qkv_last, qkv_other = order.scope(
        feed_forward
    )
    first_parts = [hidden_own, *hidden_near, *ends[:1]]
    second_parts = [hidden_own, *hidden_near, *ends[1:]]
    qkv_own = [*qkv_first, *qkv_last]
    heads_all = order.wait(heads_all)

    branch_places = order.hold(*branch_places)
    mlp_hops = [hop_rep(branch_places[k], k) for k in range(1, rep)]

    def attend(heads, own, other, m):
        return pl.pallas_call(
            attend_kernel,
            out_shape=[
                shape((3, 2 * length, cols), NARROW),
                shape((2 * length, cols), NARROW),
                shape((length, width), SINGLE),
                shape((length, width), NARROW),
            ],
            compiler_params=params(),
            cost_estimate=cost(4 * 2 * 2 * length * width * cols, 8 * 10**6),
            name="attend",
        )(own, other, heads, my_qkv_bias, rope, *doc_pairs[m])


    def add_up(own, came, first=0, *along):
        rows_of = 32
        half = length // 2 // rows_of
        block_of = lambda index: spec((3, rows_of, width), index)
        return pl.pallas_call(
            functools.partial(merge_kernel, first, half),
            grid=(2 * half,),
            in_specs=[block_of(lambda i: (0, i, 0))] * 2
            + [block_of(lambda i: (0, jnp.clip(i - first, 0, half - 1), 0))] * len(along),
            out_specs=block_of(lambda i: (0, i, 0)),
            out_shape=shape(own.shape, NARROW),
            compiler_params=params(),
            cost_estimate=cost(10**6, 10**7),
            name="merge",
        )(own, came, *along)

    def near_sums(inner, results, came, halves):
        terms = []
        for m in around:
            along = ()
            if square:
                along = (length // 2 // 32, halves[1]) if m == 1 else (0, halves[0])
            terms.append(inner.wait(add_up(results[m], came[m], *along)))
        return terms

    def attention(inner):
        heads = inner.wait(heads_all.transpose(1, 0, 2, 3).reshape(width, 4 * cols))
        results, came = [None] * chips, [None] * chips

        def step(m):
            own, other = inner.hold(qkv_own[m], qkv_other[m])
            results[m] = inner.wait(*attend(heads, own, other, m))

        step(far)
        came[far] = swap_core(inner.hold(results[far][3]))
        step(1)
        came[far] = inner.wait(came[far])
        halves = None
        if square:
            halves = send_far(inner.wait(merge(results[far][2], came[far])), 0)
        for m in range(2, far):
            step(m)
        if square:
            halves = inner.wait(*halves)
        middle = range(1, far)
        swapped = inner.wait(swap_core(inner.wait(jnp.stack([results[m][3] for m in middle]))))
        for m in middle:
            came[m] = swapped[m - 1]
        terms = [merge(results[m][2], came[m]) for m in around]
        terms = inner.wait(*take_along(terms, halves, 0))
        hops = [hop_chip(terms[m - 1], m) for m in around]
        step(0)
        hops = inner.wait(*hops)
        came[0] = inner.wait(swap_core(inner.hold(results[0][3])))
        lows = [values[0] for values in results]
        return heads, lows, [values[1] for values in results], results[0][2], [came[0], *hops]

    heads, qkv_low, mixed_low, attn_own, attn_rest = order.scope(attention)
    mlp_parts = [branch_places[0], *order.wait(*mlp_hops)]

    mix_second = jnp.pad(w_mix2, ((0, LANES - hid), (0, LANES - mixes)))
    mixed_results = pl.pallas_call(
        functools.partial(mix_kernel, chips, len(attn_rest), rep, entries),
        grid=(length // MIX_ROWS,),
        in_specs=[
            scalar_spec(),
            flat2(width),
            flat2(width),
            *[flat2(width)] * (len(attn_rest) + rep),
            spec((1, width)),
            spec((1, width)),
            spec((width, LANES)),
            spec((1, LANES)),
            spec((LANES, LANES)),
            spec((1, LANES)),
            tall2(count),
            flat2(1),
            flat2(LANES),
        ],
        out_specs=[flat2(width)] * 5
        + [flat2(LANES)] * 4
        + [spec((1, width))] * 2
        + [spec((1, LANES))] * 2,
        out_shape=[
            shape((length, width), SINGLE),
            shape((length, width), SINGLE),
            shape((length, width), NARROW),
            shape((length, width), NARROW),
            shape((length, width), NARROW),
            shape((length, LANES), NARROW),
            shape((length, LANES), SINGLE),
            shape((length, LANES), SINGLE),
            shape((length, LANES), SINGLE),
            shape((1, width), SINGLE),
            shape((1, width), SINGLE),
            shape((1, LANES), SINGLE),
            shape((1, LANES), SINGLE),
        ],
        scratch_shapes=[pltpu.VMEM((MIX_ROWS, width), SINGLE)],
        compiler_params=params(),
        cost_estimate=cost(2 * 10**8, 10**7),
        name="mixing",
    )(
        chip_at,
        last,
        attn_own,
        *attn_rest,
        *mlp_parts,
        branch_bias,
        gain,
        mix_first,
        jnp.pad(b_mix1, (0, LANES - hid))[None],
        mix_second,
        jnp.pad(b_mix2, (0, LANES - mixes))[None],
        cotangent,
        token_weight,
        dots,
    )
    (
        entry,
        grad_entry,
        grad_low,
        grad_turned,
        scaled_low,
        grad_pre_low,
        mix_act,
        grad_coef,
        coef,
        grad_rms_gain,
        grad_branch_bias,
        grad_pre_sum,
        grad_coef_sum,
    ) = order.wait(*mixed_results)

    grad_hops = [hop_rep(grad_turned, k) for k in range(1, rep)]

    def attend_back(own, other, heads, qkv, rope, pair):
        return pl.pallas_call(
            attend_back_kernel,
            out_shape=[
                shape((3, 2 * length, cols), NARROW),
                shape((1, 3 * cols), SINGLE),
                shape((3, length, width), SINGLE),
                shape((3, length, width), NARROW),
            ],
            compiler_params=params(),
            cost_estimate=cost(4 * 2 * 2 * length * width * cols, 8 * 10**6),
            name="attend_back",
        )(own, other, heads, qkv, rope, *pair)


    def back(inner, m, own, other):
        own, other = inner.hold(own, other)
        return inner.wait(*attend_back(own, other, heads, qkv_low[m], rope, doc_pairs[m]))

    def spread_branch(inner):
        swapped = inner.wait(swap_core(grad_low))
        near = [hop_chip(inner.hold(grad_low), m) for m in around]
        result = back(inner, 0, grad_low, swapped)
        near = inner.wait(*near)
        halves = pass_on(near, 0)
        next_streams = pl.pallas_call(
            next_kernel,
            grid=(steps,),
            in_specs=[tall(entries), flat(width), flat(LANES)],
            out_specs=tall(count),
            out_shape=shape((count, length, width), NARROW),
            compiler_params=params(),
            cost_estimate=cost(10**8, 10**7),
            name="next_streams",
        )(inner.hold(history), entry, coef)
        next_streams = inner.wait(next_streams)
        if square:
            near.append(inner.wait(jnp.concatenate(inner.wait(*halves), 0)))
        others = list(swap_core(jnp.stack(near)))
        others = inner.wait(*others)
        last = back(inner, far, near[far - 1], others[far - 1])
        grad_w_mix2 = transposed_times(mix_act, grad_coef, EXACT)[:hid, :mixes]
        grad_w_mix1 = transposed_times(scaled_low, grad_pre_low)[:, :hid]
        grad_w_mix1, grad_w_mix2 = inner.wait(grad_w_mix1, grad_w_mix2)
        return result, last, near, [swapped, *others], next_streams, grad_w_mix1, grad_w_mix2

    returned, terms = [None] * chips, [None] * chips
    returned[0], returned[far], branch_near, branch_other, *rest = order.scope(spread_branch)
    next_streams, grad_w_mix1, grad_w_mix2 = rest
    branch_own = [grad_low, *branch_near]
    grad_hops = order.wait(*grad_hops)

    interleave = lambda a, b: [values for pair in zip(a, b) for values in pair]
    row_block = width // fsdp

    def hidden_back_side(firsts, seconds, grad, slope, *came):
        return pl.pallas_call(
            functools.partial(hidden_back_kernel, chips, bool(came)),
            grid=(blocks,),
            in_specs=[token_block(width), token_block(hid_cols)]
            + weight_specs(0)
            + weight_specs(1)
            + [token_block(width)] * len(came),
            out_specs=[token_block(hid_cols), spec((1, hid_cols))]
            + (place_specs if came else [token_block(width)]),
            out_shape=[shape((rep * length, hid_cols), NARROW), shape((1, hid_cols), SINGLE)]
            + (places if came else [side]),
            compiler_params=params(),
            cost_estimate=cost(4 * rep * length * width * hid_cols, 2 * 10**7),
            name="hidden_back",
        )(grad, slope, *firsts, *seconds, *came)

    def outer(inner, lefts, rights):
        whole = lambda n: spec((rep * length, n))
        return inner.wait(
            *pl.pallas_call(
                outer_kernel,
                grid=(chips,),
                in_specs=[spec((rep * length, part), lambda i: (0, i))] * 2 + [whole(hid_cols)] * 2,
                out_specs=[spec((part, hid_cols))] * chips,
                out_shape=[shape((part, hid_cols), NARROW)] * chips,
                compiler_params=params(),
                cost_estimate=cost(4 * rep * length * width * hid_cols, 2 * 10**7),
                name="outer",
            )(*lefts, *rights)
        )

    def feed_forward_back(inner):
        whole = inner.wait(jnp.stack([grad_turned, *grad_hops]))
        came = [swap_core(returned[far][3]), swap_core(whole), swap_core(returned[0][3])]
        grad_own = whole.reshape(rep * length, width)
        low_own, sum_own, back_own = inner.wait(
            *hidden_back_side(first_parts, second_parts, inner.hold(grad_own), slopes[0])
        )
        came = inner.wait(*came)
        grad_other = came[1].reshape(rep * length, width)
        far_term = inner.wait(add_up(returned[far][2], came[0]))
        halves = send_far(far_term, 1) if square else ()
        low_other, sum_other, back = inner.wait(
            *hidden_back_side(first_parts, second_parts, inner.hold(grad_other), slopes[1])
        )

        def sums_of_cores(_):
            came = swap_core(back)
            at = lambda values, k: values[k * length : (k + 1) * length]
            return [merge(at(back_own, k), at(came, k)) for k in range(rep)]

        merged = inner.scope(sums_of_cores)
        halves = inner.wait(*halves) if square else [far_term]
        lows = (low_own, low_other)
        return (grad_own, grad_other), lows, sum_own + sum_other, merged, halves, came[0], came[2]

    grad_sides, grad_hidden, grad_first_bias, grad_resid, halves, far_came, own_came = order.scope(
        feed_forward_back
    )

    def total_hidden(inner, own, hops):
        total = own.astype(SINGLE)
        for values in inner.wait(*hops):
            total = total + values.astype(SINGLE)
        return inner.wait(total.astype(NARROW).reshape(group, rows, hid_cols))

    def whole_rows(came):
        return came.transpose(1, 0, 2).reshape(rows, hidden).astype(SINGLE)

    def exchange(sums):
        widths = [values.shape[1] for values in sums]
        return widths, lax.all_to_all(jnp.concatenate(sums, 1), AXES, 0, 0, tiled=True)

    def attention_back(inner):
        results = {0: returned[0], far: returned[far]}
        second_grads = outer(inner, (inner.hold(grad_sides[0]), grad_sides[1]), acts)
        halves_out = send_far(inner.hold(second_grads[far]), 0)
        results[1] = back(inner, 1, branch_own[1], branch_other[1])
        held = second_grads[1:]
        if square:
            halves_out = inner.wait(*halves_out)
            held = inner.wait(*take_along(second_grads[1:far], halves_out, 0))
        hops = [hop_chip(held[m - 1], m) for m in around]
        for m in range(2, far):
            results[m] = back(inner, m, branch_own[m], branch_other[m])
        linears = inner.hold(*[results[m][0] for m in range(chips)])
        grad_heads = pl.pallas_call(
            functools.partial(heads_grad_kernel, chips),
            grid=(fsdp,),
            in_specs=[spec((3, length, row_block), lambda i: (0, 0, i))] * fsdp
            + [spec((length, row_block), lambda i: (0, i))] * fsdp
            + [spec((3, 2 * length, cols))] * chips
            + [spec((2 * length, cols))] * chips,
            out_specs=spec((rep, 1, rows, 4 * cols), lambda i: (0, i, 0, 0)),
            out_shape=shape((rep, fsdp, rows, 4 * cols), NARROW),
            compiler_params=params(),
            cost_estimate=cost(8 * fsdp * length * width * cols, 3 * 10**7),
            name="heads_grad",
        )(
            *interleave(qkv_own, qkv_other),
            *interleave(branch_own, branch_other),
            *linears,
            *mixed_low,
        )
        grad_heads = inner.wait(grad_heads)
        hops = inner.wait(*hops)
        middle = [results[m] for m in range(1, far)]
        return grad_heads, middle, second_grads[0], hops

    def residual_back(inner):
        hops = inner.hold(*grad_resid)
        hops = [hop_rep(hops[k], k) for k in range(1, rep)]
        results = inner.scope(attention_back)
        return inner.wait(*hops), *results

    resid_hops, grad_heads, returned[1:far], second_own_grad, second_hops = order.scope(residual_back)
    qkv_biases = [results[1] for results in returned]
    grad_resid = [grad_resid[0], *resid_hops]

    def by_owner(vector):
        return vector.reshape(-1, devices, rows).transpose(1, 0, 2).reshape(devices, -1)

    grad_heads = lax.psum_scatter(grad_heads, "rep", scatter_dimension=0, tiled=False)
    def second_sum(inner):
        return total_hidden(inner, second_own_grad, second_hops)

    second_total = order.scope(second_sum)
    second_came = lax.all_to_all(order.hold(second_total), GROUP, 0, 0, tiled=True)

    def send_terms(inner):
        middle = range(1, far)
        swaps = [swap_core(inner.hold(returned[m][3])) for m in middle]
        first_grads = outer(inner, (inner.hold(resid_sides[0]), resid_sides[1]), grad_hidden)
        swaps = list(inner.wait(*swaps)) if len(swaps) > 1 else [inner.wait(*swaps)]
        owns = [results[2] for results in returned]
        near_terms = near_sums(inner, owns, [None, *swaps, far_came], halves)
        qkv_back = [hop_chip(near_terms[m - 1], m) for m in around]
        first_halves = send_far(inner.hold(first_grads[far]), 0)

        def pack_sums(_):
            qkv_bias_all = lax.dynamic_update_index_in_dim(
                jnp.zeros((3, fsdp, cols), SINGLE),
                sum(qkv_biases).reshape(3, cols),
                chip * 2 + core,
                1,
            )
            tail = jnp.concatenate(
                [grad_pre_sum[0, :hid], grad_w_mix2.reshape(-1), grad_coef_sum[0, :mixes]]
            )
            sums = [
                by_owner(grad_rms_gain[0]),
                qkv_bias_all.reshape(devices, -1),
                grad_branch_bias.reshape(devices, -1),
                grad_w_mix1.reshape(devices, -1),
                jnp.broadcast_to(tail[None], (devices, tail.shape[0])),
            ]
            size = sum(values.shape[1] for values in sums)
            empty = -size % (ROWS * LANES)
            sums.append(jnp.zeros((devices, empty), SINGLE))
            return jnp.concatenate(sums, 1).astype(NARROW).reshape(devices, ROWS, -1)

        sums = inner.scope(pack_sums)
        held = first_grads[1:]
        if square:
            first_halves = inner.wait(*first_halves)
        qkv_back = inner.wait(*qkv_back)
        if square:
            held = inner.wait(*take_along(first_grads[1:far], first_halves, 0))
        return first_grads[0], held, qkv_back, sums

    first_own_grad, first_terms, qkv_back, sums = order.scope(send_terms)
    second_came = order.wait(second_came)
    sums = order.hold(sums)
    sums = lax.all_to_all(sums, AXES, 0, 0, tiled=True)
    widths = [rows, 3 * cols * fsdp // devices, rows, rows * hid]

    qkv_rest = [own_came, *qkv_back]

    def close_layer(inner):
        held = inner.hold(*first_terms)
        first_hops = [hop_chip(held[m - 1], m) for m in around]
        close_from = inner.hold(history, cotangent)
        grad_history, grad_mix_in, grad_affine = pl.pallas_call(
            functools.partial(close_kernel, chips, len(qkv_rest), rep),
            grid=(steps,),
            in_specs=[
                scalar_spec(),
                tall(entries),
                tall(count),
                flat(LANES),
                flat(1),
                flat(LANES),
                spec((4, width)),
                flat(width),
                *[tall(3)] * (1 + len(qkv_rest)),
                *[flat(width)] * rep,
            ],
            out_specs=[tall(entries), flat(count * entries), spec((4, width))],
            out_shape=[
                shape((entries, length, width), SINGLE),
                shape((length, count * entries), SINGLE),
                shape((4, width), SINGLE),
            ],
            scratch_shapes=[
                pltpu.VMEM((count, ROWS, width), SINGLE),
                pltpu.VMEM((ROWS, width), SINGLE),
                pltpu.VMEM((5 * count * ROWS, width), NARROW),
            ],
            compiler_params=params(),
            cost_estimate=cost(2 * 10**8, 2 * 10**7),
            name="close",
        )(
            chip_at,
            *close_from,
            coef,
            token_weight,
            mix_padded,
            affine,
            grad_entry,
            returned[0][2],
            *qkv_rest,
            *grad_resid,
        )
        grad_history, grad_mix_in, grad_affine = inner.wait(grad_history, grad_mix_in, grad_affine)

        return grad_history, grad_mix_in, grad_affine, total_hidden(inner, first_own_grad, first_hops)

    grad_history, grad_mix_in, grad_affine, first_total = order.scope(close_layer)
    sums = order.wait(sums)
    first_bias_all = lax.dynamic_update_index_in_dim(
        jnp.zeros((group, hid_cols), SINGLE), grad_first_bias[0], core * rep + line, 0
    )
    every = order.wait(
        jnp.concatenate([by_owner(grad_affine), first_bias_all.reshape(devices, -1)], 1)
    )
    every = order.wait(lax.all_to_all(every, AXES, 0, 0, tiled=True))
    first_came = lax.all_to_all(order.hold(first_total), GROUP, 0, 0, tiled=True)
    grad_w_fc2 = order.wait(whole_rows(second_came))
    every = order.wait(jnp.sum(every, 0))
    total = order.wait(jnp.sum(sums.astype(SINGLE), 0).reshape(-1))
    grad_heads = order.wait(grad_heads)

    def around_ring(inner):
        split = inner.hold(grad_heads).reshape(chips, 2, rows, 4 * cols)
        parts = [lax.dynamic_index_in_dim(split, chip ^ m, 0, False) for m in range(chips)]
        parts = [parts[0]] + [hop_chip(parts[m], m) for m in range(1, chips)]
        parts = jnp.stack(inner.wait(*parts))
        mine = lax.dynamic_index_in_dim(parts, core, 1, False)
        came = swap_core(lax.dynamic_index_in_dim(parts, 1 - core, 1, False))
        result = jnp.zeros((chips, 2, rows, 4 * cols), NARROW)
        for m in range(chips):
            pair = jnp.where(core == 0, jnp.stack([mine[m], came[m]]), jnp.stack([came[m], mine[m]]))
            result = lax.dynamic_update_index_in_dim(result, pair, chip ^ m, 0)
        result = result.reshape(fsdp, rows, 4, cols).transpose(1, 2, 0, 3).astype(SINGLE)
        return result[:, :3].reshape(rows, 3 * width), result[:, 3].reshape(rows, width)

    grad_w_qkv, grad_w_out = order.scope(around_ring)
    first_came = order.wait(first_came)
    grad_w_fc1 = whole_rows(first_came)
    outs, start = [], 0
    for size in widths:
        outs.append(total[start : start + size])
        start += size
    outs.append(total[start:])
    affine_sums = every[: 4 * rows].reshape(4, rows)
    gain_grads = jnp.stack([affine_sums[0], affine_sums[2], outs[0]])
    bias_grads = jnp.stack([affine_sums[1], affine_sums[3]])
    return (
        next_streams,
        grad_history,
        grad_mix_in,
        gain_grads,
        bias_grads,
        grad_w_qkv,
        outs[1],
        grad_w_out,
        outs[2],
        grad_w_fc1,
        every[4 * rows :],
        grad_w_fc2,
        outs[2],
        outs[3].reshape(rows, hid),
        outs[4][:hid],
        outs[4][hid : hid + hid * mixes].reshape(hid, mixes),
        outs[4][hid + hid * mixes : hid + hid * mixes + mixes],
    )


def solution(mesh):
    fsdp, rep = mesh.shape["fsdp"], mesh.shape["rep"]
    chips = fsdp // 2
    finer = Mesh(mesh.devices.reshape(chips, 2, rep), AXES)
    rows = P(AXES, None)
    line = P(AXES)
    streams = P(None, AXES, None)
    columns = P(None, AXES)
    in_specs = (
        streams,
        rows,
        rows,
        rows,
        P(),
        columns,
        columns,
        rows,
        line,
        rows,
        line,
        rows,
        line,
        rows,
        line,
        rows,
        P(),
        P(),
        P(),
        streams,
    )
    out_specs = (
        streams,
        streams,
        rows,
        columns,
        columns,
        rows,
        line,
        rows,
        line,
        rows,
        line,
        rows,
        line,
        rows,
        P(),
        P(),
        P(),
    )
    return jax.shard_map(
        functools.partial(on_device, chips, rep),
        mesh=finer,
        in_specs=in_specs,
        out_specs=out_specs,
        check_vma=False,
    )
```

```python
import functools
import math

import jax
import jax.numpy as jnp
from jax import lax
from jax.experimental import pallas as pl
from jax.experimental.pallas import tpu as pltpu
from jax.sharding import Mesh
from jax.sharding import PartitionSpec as P

HEAD_DIM = 128
ROT = 32
LANES = 128
NARROW = jnp.bfloat16
SINGLE = jnp.float32
NORM_EPSILON = 1e-05
RMS_EPSILON = 1e-06
AXES = ("chip", "core", "rep")
GROUP = ("core", "rep")
RING = ("chip", "core")
ROWS = 16
MIX_ROWS = 32
CHUNK = 512
VMEM_BYTES = 56 * 1024 * 1024
EXACT = lax.Precision.HIGHEST


def times(left, right, precision=None):
    return lax.dot_general(
        left, right, (((1,), (0,)), ((), ())), precision=precision, preferred_element_type=SINGLE
    )


def times_transposed(left, right, precision=None):
    return lax.dot_general(
        left, right, (((1,), (1,)), ((), ())), precision=precision, preferred_element_type=SINGLE
    )


def transposed_times(left, right, precision=None):
    return lax.dot_general(
        left, right, (((0,), (0,)), ((), ())), precision=precision, preferred_element_type=SINGLE
    )


def gelu_parts(values):
    cumulative = 0.5 * (1.0 + lax.erf(values * math.sqrt(0.5)))
    density = jnp.exp(-0.5 * values * values) * (1.0 / math.sqrt(2.0 * math.pi))
    return values * cumulative, cumulative + values * density


def params(*semantics):
    return pltpu.CompilerParams(vmem_limit_bytes=VMEM_BYTES)


def spec(shape, index=None):
    if index is None:
        index = lambda *i: (0,) * len(shape)
    return pl.BlockSpec(shape, index)


def scalar_spec():
    return pl.BlockSpec(memory_space=pltpu.SMEM)


def cost(flops, moved):
    return pl.CostEstimate(flops=flops // 1000, bytes_accessed=moved // 1000, transcendentals=0)


def mean(values):
    return jnp.mean(values, -1, keepdims=True)


def same_token(shape):
    row = lax.broadcasted_iota(jnp.int32, shape, 0)
    col = lax.broadcasted_iota(jnp.int32, shape, 1)
    return row == col % ROWS


def places(first, count):
    row = lax.broadcasted_iota(jnp.int32, (LANES, count * ROWS), 0)
    col = lax.broadcasted_iota(jnp.int32, (LANES, count * ROWS), 1)
    return (row == first + col // ROWS).astype(NARROW)


def two_parts(values):
    high = values.astype(NARROW)
    return jnp.concatenate([high, (values - high.astype(SINGLE)).astype(NARROW)], 0)


def spread_out(coef, count, entries, stride):
    mask = same_token((ROWS, entries * ROWS))
    parts = two_parts(coef)
    highs, lows = [], []
    for s in range(count):
        full = times(parts, places(s * stride, entries))
        highs.append(jnp.where(mask, full[:ROWS], 0.0).astype(NARROW))
        lows.append(jnp.where(mask, full[ROWS:], 0.0).astype(NARROW))
    return jnp.concatenate(highs, 0), jnp.concatenate(lows, 0)


def draw_in(products, count, entries, stride):
    mask = same_token((ROWS, entries * ROWS))
    total = None
    for s in range(count):
        own = jnp.where(mask, products[s * ROWS : (s + 1) * ROWS], 0.0)
        term = times_transposed(two_parts(own), places(s * stride, entries))
        total = term if s == 0 else total + term
    return total[:ROWS] + total[ROWS:]


def blend_streams(hist, mix, streams):
    entries, _, width = hist.shape
    count = streams.shape[0]
    both = jnp.concatenate(spread_out(mix[...], count, entries, entries), 0)
    for start in range(0, width, CHUNK):
        sources = hist[:, :, start : start + CHUNK].reshape(entries * ROWS, CHUNK)
        total = times(both, sources)
        total = total[: count * ROWS] + total[count * ROWS :]
        streams[:, :, start : start + CHUNK] = total.reshape(count, ROWS, CHUNK)


def streams_kernel(chips, chip, hist, mix, affine, qkv, resid, last, streams):
    width = hist.shape[2]
    blend_streams(hist, mix, streams)
    for s in range(4):
        values = streams[s]
        center = values - mean(values)
        row = 0 if s < 3 else 2
        normed = (
            center * lax.rsqrt(mean(center * center) + NORM_EPSILON) * affine[row : row + 1]
            + affine[row + 1 : row + 2]
        )
        if s < 3:
            qkv[s] = normed.astype(NARROW)
        else:
            last[...] = values
            streams[0] = normed
    part = width // chips
    for m in range(chips):
        start = pl.multiple_of((chip[0] ^ m) * part, part)
        resid[:, m * part : (m + 1) * part] = streams[0, :, pl.ds(start, part)].astype(NARROW)


def history_dots_kernel(hist, cot, weight, out):
    entries, rows, width = hist.shape
    count = cot.shape[0]
    products = times_transposed(
        cot[...].reshape(count * rows, width), hist[...].reshape(entries * rows, width)
    )
    out[...] = draw_in(products, count, entries, entries + 1) * weight[...]


def mix_kernel(
    chips,
    near,
    rep,
    entries,
    chip,
    last,
    attn_own,
    *refs,
):
    attn_rest, mlp_parts, refs = refs[:near], refs[near : near + rep], refs[near + rep :]
    mix_body(chips, entries, chip, last, attn_own, attn_rest, mlp_parts, *refs)


def mix_body(
    chips,
    entries,
    chip,
    last,
    attn_own,
    attn_rest,
    mlp_parts,
    branch_bias,
    gain,
    first,
    first_bias,
    second,
    second_bias,
    cot,
    weight,
    dots,
    entry_out,
    grad_out,
    grad_low,
    grad_turned,
    scaled_out,
    grad_pre_low,
    act_out,
    grad_coef_out,
    coef_out,
    grad_gain,
    grad_bias,
    grad_pre_sum,
    grad_coef_sum,
    turned,
):
    rows, width = last.shape
    count = cot.shape[0]
    entry = last[...] + attn_own[...] + branch_bias[...]
    for part in attn_rest:
        entry = entry + part[...].astype(SINGLE)
    total = mlp_parts[0][...].astype(SINGLE)
    for values in mlp_parts[1:]:
        total = total + values[...].astype(SINGLE)
    part = width // chips
    for m in range(chips):
        start = pl.multiple_of((chip[0] ^ m) * part, part)
        turned[:, pl.ds(start, part)] = total[:, m * part : (m + 1) * part]
    entry = entry + turned[...]
    entry_out[...] = entry
    scale = lax.rsqrt(mean(entry * entry) + RMS_EPSILON)
    scaled = (entry * scale * gain[...]).astype(NARROW)
    scaled_out[...] = scaled
    pre = times(scaled, first[...]) + first_bias[...]
    act, slope = gelu_parts(pre)
    act_out[...] = act
    coef = times(act, second[...], EXACT) + second_bias[...]
    coef_out[...] = coef
    lane = lax.broadcasted_iota(jnp.int32, (rows, LANES), 1)
    grad_coef = dots[...]
    grad = jnp.zeros((rows, width), SINGLE)
    for s in range(count):
        arriving = cot[s].astype(SINGLE)
        place = s * (entries + 1) + entries
        total = jnp.sum(arriving * entry, -1, keepdims=True) * weight[:, :1]
        grad_coef = jnp.where(lane == place, total, grad_coef)
        grad = grad + (coef[:, place : place + 1] * weight[:, :1]) * arriving
    grad_coef_out[...] = grad_coef
    grad_pre = slope * times_transposed(grad_coef, second[...], EXACT)
    grad_pre_narrow = grad_pre.astype(NARROW)
    grad_pre_low[...] = grad_pre_narrow
    grad_scaled = times_transposed(grad_pre_narrow, first[...])
    gained = grad_scaled * gain[...]
    grad = grad + scale * gained - entry * (scale * scale * scale * mean(gained * entry))
    grad_out[...] = grad
    grad_low[...] = grad.astype(NARROW)
    for m in range(chips):
        start = pl.multiple_of((chip[0] ^ m) * part, part)
        grad_turned[:, m * part : (m + 1) * part] = grad_out[:, pl.ds(start, part)].astype(NARROW)

    @pl.when(pl.program_id(0) == 0)
    def _():
        grad_gain[...] = jnp.zeros_like(grad_gain)
        grad_bias[...] = jnp.zeros_like(grad_bias)
        grad_pre_sum[...] = jnp.zeros_like(grad_pre_sum)
        grad_coef_sum[...] = jnp.zeros_like(grad_coef_sum)

    grad_gain[...] += jnp.sum(grad_scaled * entry * scale, 0, keepdims=True)
    grad_bias[...] += jnp.sum(grad, 0, keepdims=True)
    grad_pre_sum[...] += jnp.sum(grad_pre, 0, keepdims=True)
    grad_coef_sum[...] += jnp.sum(grad_coef, 0, keepdims=True)


def next_kernel(hist, entry, coef, out):
    entries, _, width = hist.shape
    count = out.shape[0]
    both = jnp.concatenate(spread_out(coef[...], count, entries, entries + 1), 0)
    for start in range(0, width, CHUNK):
        cols = slice(start, start + CHUNK)
        sources = hist[:, :, cols].reshape(entries * ROWS, CHUNK)
        total = times(both, sources)
        total = total[: count * ROWS] + total[count * ROWS :]
        for s in range(count):
            place = s * (entries + 1) + entries
            out[s, :, cols] = (
                total[s * ROWS : (s + 1) * ROWS] + coef[:, place : place + 1] * entry[:, cols]
            ).astype(NARROW)


def close_kernel(
    chips,
    near,
    rep,
    chip,
    hist,
    cot,
    coef,
    weight,
    mix,
    affine,
    grad_entry,
    qkv_own,
    *refs,
):
    qkv_rest, resid, refs = refs[:near], refs[near : near + rep], refs[near + rep :]
    close_body(
        chips, chip, hist, cot, coef, weight, mix, affine, grad_entry, resid, qkv_own, qkv_rest, *refs
    )


def close_body(
    chips,
    chip,
    hist,
    cot,
    coef,
    weight,
    mix,
    affine,
    grad_entry,
    resid,
    qkv_own,
    qkv_rest,
    grad_hist,
    grad_mix,
    grad_affine,
    streams,
    turned,
    stacked,
):
    entries, rows, width = hist.shape
    count = cot.shape[0]
    part = width // chips

    @pl.when(pl.program_id(0) == 0)
    def _():
        grad_affine[...] = jnp.zeros_like(grad_affine)

    blend_streams(hist, mix, streams)
    for s in range(count):
        values = streams[s]
        center = values - mean(values)
        scale = lax.rsqrt(mean(center * center) + NORM_EPSILON)
        unit = center * scale
        if s < 3:
            arriving = qkv_own[s].astype(SINGLE)
            for rest in qkv_rest:
                arriving = arriving + rest[s].astype(SINGLE)
        else:
            total = resid[0][...].astype(SINGLE)
            for rest in resid[1:]:
                total = total + rest[...].astype(SINGLE)
            for m in range(chips):
                start = pl.multiple_of((chip[0] ^ m) * part, part)
                turned[:, pl.ds(start, part)] = total[:, m * part : (m + 1) * part]
            arriving = turned[...]
        row = 0 if s < 3 else 2
        grad_affine[row : row + 1] += jnp.sum(arriving * unit, 0, keepdims=True)
        grad_affine[row + 1 : row + 2] += jnp.sum(arriving, 0, keepdims=True)
        gained = arriving * affine[row : row + 1]
        grad = scale * (gained - mean(gained) - unit * mean(gained * unit))
        streams[s] = grad if s < 3 else grad + grad_entry[...]
    size = count * rows
    grads = streams[...].reshape(size, width)
    high = grads.astype(NARROW)
    stacked[0:size] = high
    stacked[size : 2 * size] = (grads - high.astype(SINGLE)).astype(NARROW)
    stacked[2 * size : 3 * size] = high
    arriving = cot[...].reshape(size, width)
    stacked[3 * size : 4 * size] = arriving
    stacked[4 * size : 5 * size] = arriving
    mix_high, mix_low = spread_out(mix[...], count, entries, entries)
    out_high, out_low = spread_out(coef[...] * weight[...], count, entries, entries + 1)
    spread = jnp.concatenate([mix_high, mix_high, mix_low, out_high, out_low], 0)
    products = jnp.zeros((2 * size, entries * rows), SINGLE)
    for start in range(0, width, CHUNK):
        cols = slice(start, start + CHUNK)
        grad_hist[:, :, cols] = transposed_times(spread, stacked[:, cols]).reshape(
            entries, rows, CHUNK
        )
        sources = hist[:, :, cols].reshape(entries * rows, CHUNK)
        products = products + times_transposed(stacked[0 : 2 * size, cols], sources)
    products = products[:size] + products[size:]
    grad_mix[...] = draw_in(products, count, entries, entries)[:, : grad_mix.shape[1]]


def turn(values, rope, sign):
    forward = pltpu.roll(values, HEAD_DIM - ROT // 2, 1)
    backward = pltpu.roll(values, ROT // 2, 1)
    return values * rope[0] + sign * (forward * rope[1] + backward * rope[2])


def allowed_pairs(row, column):
    size = row.shape[1]
    query = lax.broadcasted_iota(jnp.int32, (size, size), 0)
    key = lax.broadcasted_iota(jnp.int32, (size, size), 1)
    return (key <= query) & (row == column[:, :1])


def probabilities(query, key, allowed):
    scores = jnp.where(allowed, times_transposed(query, key) * HEAD_DIM ** (-0.5), -1e30)
    raised = jnp.exp(scores - jnp.max(scores, -1, keepdims=True))
    return raised / jnp.sum(raised, -1, keepdims=True)


def attend_kernel(own, other, weight, bias, rope, doc_row, doc_column, qkv, mixed, out_own, out_other):
    _, length, _ = own.shape
    cols = bias.shape[1] // 3
    for i in range(3):
        tokens = jnp.concatenate([own[i], other[i]], 0)
        linear = times(tokens, weight[:, i * cols : (i + 1) * cols]) + bias[:, i * cols : (i + 1) * cols]
        for start in range(0, cols, HEAD_DIM):
            head = slice(start, start + HEAD_DIM)
            piece = linear[:, head]
            qkv[i, :, head] = (turn(piece, rope, 1.0) if i < 2 else piece).astype(NARROW)
    allowed = allowed_pairs(doc_row[...], doc_column[...])
    for start in range(0, cols, HEAD_DIM):
        head = slice(start, start + HEAD_DIM)
        probs = probabilities(qkv[0, :, head], qkv[1, :, head], allowed)
        mixed[:, head] = times(probs.astype(NARROW), qkv[2, :, head]).astype(NARROW)
    result = times_transposed(mixed[...], weight[:, 3 * cols :])
    out_own[...] = result[:length]
    out_other[...] = result[length:].astype(NARROW)


def attend_back_kernel(
    own, other, weight, qkv, rope, doc_row, doc_column, grad_linear, grad_bias, out_own, out_other
):
    length = own.shape[0]
    cols = qkv.shape[2]
    scale = HEAD_DIM ** (-0.5)
    arriving = jnp.concatenate([own[...], other[...]], 0)
    grad_mixed = times(arriving, weight[:, 3 * cols :]).astype(NARROW)
    allowed = allowed_pairs(doc_row[...], doc_column[...])
    for start in range(0, cols, HEAD_DIM):
        head = slice(start, start + HEAD_DIM)
        query, key, value = (qkv[i, :, head] for i in range(3))
        grad = grad_mixed[:, head]
        probs = probabilities(query, key, allowed)
        grad_value = transposed_times(probs.astype(NARROW), grad)
        grad_probs = times_transposed(grad, value)
        inner = jnp.sum(probs * grad_probs, -1, keepdims=True)
        grad_scores = (probs * (grad_probs - inner)).astype(NARROW)
        grad_query = turn(times(grad_scores, key) * scale, rope, -1.0)
        grad_key = turn(transposed_times(grad_scores, query) * scale, rope, -1.0)
        for i, values in enumerate((grad_query, grad_key, grad_value)):
            grad_bias[:, i * cols + start : i * cols + start + HEAD_DIM] = jnp.sum(
                values, 0, keepdims=True
            )
            grad_linear[i, :, head] = values.astype(NARROW)
    for i in range(3):
        result = times_transposed(grad_linear[i], weight[:, i * cols : (i + 1) * cols])
        out_own[i] = result[:length].astype(NARROW)
        out_other[i] = result[length:].astype(NARROW)


def heads_grad_kernel(chips, *refs):
    norms, branches = refs[: 2 * chips], refs[2 * chips : 4 * chips]
    linears, mixeds, out = refs[4 * chips : 5 * chips], refs[5 * chips : 6 * chips], refs[6 * chips]
    cols = mixeds[0].shape[1]
    rep, _, rows, _ = out.shape
    for i in range(4):
        total = None
        for m in range(chips):
            sides = norms[2 * m : 2 * m + 2] if i < 3 else branches[2 * m : 2 * m + 2]
            left = jnp.concatenate([values[i] if i < 3 else values[...] for values in sides], 0)
            right = linears[m][i] if i < 3 else mixeds[m][...]
            term = transposed_times(left, right)
            total = term if total is None else total + term
        total = total.astype(NARROW)
        for k in range(rep):
            out[k, 0, :, i * cols : (i + 1) * cols] = total[k * rows : (k + 1) * rows]


def rows_of_weight(block):
    group, _, rows, cols = block.shape
    return block[...].reshape(group * rows, cols)


def hidden_kernel(chips, tokens, *refs):
    weights, (bias, act_out, slope_out) = refs[:chips], refs[chips:]
    part = weights[0].shape[0] * weights[0].shape[2]
    total = bias[...]
    for m in range(chips):
        total = total + times(tokens[:, m * part : (m + 1) * part], rows_of_weight(weights[m]))
    act, slope = gelu_parts(total)
    act_out[...] = act.astype(NARROW)
    slope_out[...] = slope


def put_places(outs, length, cols, result):
    many = result.shape[0] // length
    for k, out in enumerate(outs):

        @pl.when(pl.program_id(0) == k // many)
        def _():
            out[:, cols] = result[(k % many) * length : (k % many + 1) * length].astype(NARROW)


def branch_kernel(chips, merged, act, *refs):
    weights, refs = refs[:chips], refs[chips:]
    part = weights[0].shape[0] * weights[0].shape[2]
    for m in range(chips):
        cols = slice(m * part, (m + 1) * part)
        result = times_transposed(act[...], rows_of_weight(weights[m]))
        if merged:
            put_places(refs[1:], refs[1].shape[0], cols, result + refs[0][:, cols].astype(SINGLE))
        else:
            refs[0][:, cols] = result.astype(NARROW)


def hidden_back_kernel(chips, merged, grad, slope, *refs):
    firsts, seconds, refs = refs[:chips], refs[chips : 2 * chips], refs[2 * chips :]
    came, refs = (refs[0], refs[1:]) if merged else (None, refs)
    grad_low, grad_sum, *outs = refs
    part = firsts[0].shape[0] * firsts[0].shape[2]
    total = None
    for m in range(chips):
        term = times(grad[:, m * part : (m + 1) * part], rows_of_weight(seconds[m]))
        total = term if m == 0 else total + term
    total = total * slope[...]

    @pl.when(pl.program_id(0) == 0)
    def _():
        grad_sum[...] = jnp.zeros_like(grad_sum)

    grad_sum[...] += jnp.sum(total, 0, keepdims=True)
    low = total.astype(NARROW)
    grad_low[...] = low
    for m in range(chips):
        cols = slice(m * part, (m + 1) * part)
        result = times_transposed(low, rows_of_weight(firsts[m]))
        if merged:
            put_places(outs, outs[0].shape[0], cols, result + came[:, cols].astype(SINGLE))
        else:
            outs[0][:, cols] = result.astype(NARROW)


def outer_kernel(left_own, left_other, right_own, right_other, *outs):
    result = (
        transposed_times(left_own[...], right_own[...])
        + transposed_times(left_other[...], right_other[...])
    ).astype(NARROW)
    for m, out in enumerate(outs):

        @pl.when(pl.program_id(0) == m)
        def _():
            out[...] = result


def merge_kernel(first, count, own, came, *refs):
    total = own[...].astype(SINGLE) + came[...].astype(SINGLE)
    refs[-1][...] = total.astype(NARROW)
    if len(refs) > 1:

        @pl.when((pl.program_id(0) >= first) & (pl.program_id(0) < first + count))
        def _():
            refs[-1][...] = (total + refs[0][...].astype(SINGLE)).astype(NARROW)


def pack_hidden_kernel(first, second, out):
    cols = out.shape[3]
    for b in range(out.shape[0]):
        out[b, 0] = first[:, b * cols : (b + 1) * cols].astype(NARROW)
        out[b, 1] = second[:, b * cols : (b + 1) * cols].astype(NARROW)


def join_heads_kernel(chips, chip, core, swapped, *refs):
    parts, out = refs[:chips], refs[chips]
    for m in range(chips):
        place = 2 * (chip[0] ^ m)
        out[place + core[0]] = parts[m][core[0]]
        out[place + 1 - core[0]] = swapped[m]


def pack_small_kernel(*refs):
    out = refs[-1]
    row = 0
    out[...] = jnp.zeros_like(out)
    for values in refs[:-1]:
        for i in range(values.shape[0]):
            for start in range(0, values.shape[1], LANES):
                stop = min(start + LANES, values.shape[1])
                piece = values[i : i + 1, start:stop].astype(NARROW)
                out[:, row, : stop - start] = jnp.broadcast_to(piece, (out.shape[0], stop - start))
                row += 1


def pack_heads_kernel(chips, chip, qkv, out_weight, *outs):
    cols = outs[0].shape[2] // 4
    width = out_weight.shape[1]
    for m in range(chips):
        for c in range(2):
            start = pl.multiple_of(((chip[0] ^ m) * 2 + c) * cols, cols)
            for i in range(3):
                outs[m][c, :, i * cols : (i + 1) * cols] = qkv[
                    :, pl.ds(i * width + start, cols)
                ].astype(NARROW)
            outs[m][c, :, 3 * cols :] = out_weight[:, pl.ds(start, cols)].astype(NARROW)


class Order:
    def __init__(self, legal):
        self.legal = legal
        self.last = ()

    def hold(self, *values):
        tied = lax.optimization_barrier(tuple(values) + self.last)[: len(values)]
        return tied[0] if len(values) == 1 else tied

    def wait(self, *values):
        tied = lax.optimization_barrier(tuple(values) + self.last)[: len(values)]
        self.last = (tied[0],)
        return tied[0] if len(values) == 1 else list(tied)

    def scope(self, steps):
        inside = lambda: steps(Order(self.legal))
        shapes = jax.eval_shape(inside)
        never = lambda: jax.tree.map(lambda leaf: jnp.zeros(leaf.shape, leaf.dtype), shapes)
        results = lax.cond(self.hold(self.legal), inside, never)
        smallest = min(jax.tree.leaves(results), key=lambda leaf: leaf.size)
        self.last = (smallest,)
        return results


def on_device(
    chips,
    rep,
    history,
    mix_in,
    doc_ids,
    doc_group,
    group_weight,
    norm_gain,
    norm_bias,
    w_qkv,
    b_qkv,
    w_out,
    b_out,
    w_fc1,
    b_fc1,
    w_fc2,
    b_fc2,
    w_mix1,
    b_mix1,
    w_mix2,
    b_mix2,
    cotangent,
):
    entries, length, width = history.shape
    count = cotangent.shape[0]
    rows = w_qkv.shape[0]
    hidden = w_fc1.shape[1]
    hid = b_mix1.shape[0]
    mixes = b_mix2.shape[0]
    fsdp = 2 * chips
    group = 2 * rep
    devices = fsdp * rep
    cols = width // fsdp
    hid_cols = hidden // group
    part = width // chips
    chip = lax.axis_index("chip")
    core = lax.axis_index("core")
    line = lax.axis_index("rep")
    chip_at = chip.astype(jnp.int32).reshape(1)
    core_at = core.astype(jnp.int32).reshape(1)
    line_at = line.astype(jnp.int32).reshape(1)
    shape = jax.ShapeDtypeStruct

    def swap_core(values):
        return lax.ppermute(values, "core", [(0, 1), (1, 0)])

    def hop_chip(values, m):
        return lax.ppermute(values, "chip", [(i, i ^ m) for i in range(chips)])

    def hop_rep(values, k):
        return lax.ppermute(values, "rep", [(i, i ^ k) for i in range(rep)])

    def merge(own, came):
        return (own.astype(SINGLE) + came.astype(SINGLE)).astype(NARROW)

    def pieces(values, axis):
        size = values.shape[axis] // 2
        return (
            lax.slice_in_dim(values, 0, size, axis=axis),
            lax.slice_in_dim(values, size, 2 * size, axis=axis),
        )

    square = chips == 4
    around = range(1, 3 if square else chips)
    far = chips - 1

    def pass_on(first, axis):
        if not square:
            return ()
        return hop_chip(pieces(first[0], axis)[0], 2), hop_chip(pieces(first[1], axis)[1], 1)

    def joined_halves(halves, axis):
        return [jnp.concatenate(halves, axis)] if square else []

    def send_far(far, axis):
        if not square:
            return ()
        upper, lower = pieces(far, axis)
        return hop_chip(upper, 1), hop_chip(lower, 2)

    def take_along(terms, halves, axis):
        if not square:
            return terms
        upper, lower = halves
        near = pieces(terms[0], axis)
        far = pieces(terms[1], axis)
        return [
            jnp.concatenate([near[0], merge(near[1], lower)], axis),
            jnp.concatenate([merge(far[0], upper), far[1]], axis),
        ]

    order = Order(doc_ids[0, 0] >= 0)
    steps = length // ROWS
    block = 256
    blocks = rep * length // block
    tall = lambda n: spec((n, ROWS, width), lambda i: (0, i, 0))
    flat = lambda n: spec((ROWS, n), lambda i: (i, 0))
    tall2 = lambda n: spec((n, MIX_ROWS, width), lambda i: (0, i, 0))
    flat2 = lambda n: spec((MIX_ROWS, n), lambda i: (i, 0))
    token_block = lambda n: spec((block, n), lambda i: (i, 0))
    weight_block = (group, 1, rows, hid_cols)
    weight_specs = lambda which: [spec(weight_block, lambda *_: (0, which, 0, 0))] * (
        3 if square else chips
    ) + [spec(weight_block)] * square
    in_vmem = pl.BlockSpec(memory_space=pltpu.VMEM)

    small = (norm_gain, norm_bias, b_qkv, b_out, b_fc1, b_fc2, doc_ids)
    flat_small = [values.reshape(-1, values.shape[-1]) for values in small]
    rows_of = [values.shape[0] * -(-values.shape[1] // LANES) for values in flat_small]
    packed = pl.pallas_call(
        pack_small_kernel,
        in_specs=[in_vmem] * len(small),
        out_shape=shape((devices, -(-sum(rows_of) // ROWS) * ROWS, LANES), NARROW),
        compiler_params=params(),
        cost_estimate=cost(10**6, 10**6),
        name="pack_small",
    )(*flat_small)
    packed = order.wait(packed)
    gathered = lax.all_to_all(packed, AXES, 0, 0, tiled=True)
    hidden_sends = pl.pallas_call(
        pack_hidden_kernel,
        in_specs=[in_vmem] * 2,
        out_shape=shape((group, 2, rows, hid_cols), NARROW),
        compiler_params=params(),
        cost_estimate=cost(10**6, 6 * 10**6),
        name="pack_hidden",
    )(*order.hold(w_fc1, w_fc2))
    hidden_sends = order.wait(hidden_sends)
    heads_sends = pl.pallas_call(
        functools.partial(pack_heads_kernel, chips),
        in_specs=[scalar_spec()] + [in_vmem] * 2,
        out_shape=[shape((2, rows, 4 * cols), NARROW)] * chips,
        compiler_params=params(),
        cost_estimate=cost(10**6, 3 * 10**6),
        name="pack_heads",
    )(chip_at, *order.hold(w_qkv, w_out))
    heads_sends = order.wait(*heads_sends)
    gathered = order.wait(gathered)
    hidden_own = lax.all_to_all(order.hold(hidden_sends), GROUP, 0, 0, tiled=True)

    def fields_of(gathered):
        fields, row = [], 0
        for values, count_of in zip(flat_small, rows_of):
            field = gathered[:, row : row + count_of]
            if values.shape[1] <= LANES:
                field = field[:, :, : values.shape[1]]
            else:
                field = field.reshape(devices, values.shape[0], -1)[:, :, : values.shape[1]]
            fields.append(field)
            row += count_of
        return fields

    def join_heads(parts):
        def steps(inner):
            for_other = jnp.stack(
                [lax.dynamic_index_in_dim(values, 1 - core, 0, False) for values in parts]
            )
            return pl.pallas_call(
                functools.partial(join_heads_kernel, chips),
                in_specs=[scalar_spec()] * 2 + [in_vmem] * (chips + 1),
                out_shape=shape((fsdp, rows, 4 * cols), NARROW),
                compiler_params=params(),
                cost_estimate=cost(10**6, 3 * 10**6),
                name="join_heads",
            )(chip_at, core_at, swap_core(for_other), *parts)

        return steps

    def norm_streams(inner):
        heads_hops = [hop_chip(heads_sends[m], m) for m in range(1, chips)]
        mix_padded = jnp.pad(mix_in, ((0, 0), (0, LANES - count * entries)))
        fields = fields_of(gathered)
        gains = fields[0].transpose(1, 0, 2).reshape(3, width)
        shifts = fields[1].transpose(1, 0, 2).reshape(2, width)
        affine = jnp.stack([gains[0], shifts[0], gains[1], shifts[1]]).astype(SINGLE)
        normed = pl.pallas_call(
            functools.partial(streams_kernel, chips),
            grid=(steps,),
            in_specs=[scalar_spec(), tall(entries), flat(LANES), spec((4, width))],
            out_specs=[tall(3), flat(width), flat(width)],
            out_shape=[
                shape((3, length, width), NARROW),
                shape((length, width), NARROW),
                shape((length, width), SINGLE),
            ],
            scratch_shapes=[pltpu.VMEM((count, ROWS, width), SINGLE)],
            compiler_params=params(),
            cost_estimate=cost(10**8, 10**7),
            name="streams",
        )(chip_at, history, mix_padded, affine)
        normed = inner.wait(*normed)
        return normed, affine, mix_padded, inner.wait(*heads_hops)

    def open_layer(inner):
        normed, affine, mix_padded, heads_hops = inner.scope(norm_streams)
        qkv_near = [hop_chip(inner.hold(normed[0]), m) for m in around]
        documents, group_of, weight_of = inner.hold(doc_ids[0], doc_group[0], group_weight)
        doc_match = documents[:, None] == jnp.arange(doc_group.shape[1], dtype=jnp.int32)[None, :]
        token_group = jnp.sum(jnp.where(doc_match, group_of[None, :], 0), axis=1)
        group_match = (
            token_group[:, None] == jnp.arange(group_weight.shape[0], dtype=jnp.int32)[None, :]
        )
        token_weight = jnp.sum(jnp.where(group_match, weight_of[None, :], 0.0), 1, keepdims=True)
        token_weight = inner.wait(jnp.broadcast_to(token_weight, (length, LANES)))
        dots = pl.pallas_call(
            history_dots_kernel,
            grid=(steps,),
            in_specs=[tall(entries), tall(count), flat(LANES)],
            out_specs=flat(LANES),
            out_shape=shape((length, LANES), SINGLE),
            compiler_params=params(),
            cost_estimate=cost(10**8, 10**7),
            name="history_dots",
        )(history, cotangent, token_weight)
        dots = inner.wait(dots)
        heads_came = inner.scope(join_heads([heads_sends[0], *heads_hops]))
        return normed, affine, dots, token_weight, inner.wait(*qkv_near), mix_padded, heads_came

    normed, affine, dots, token_weight, qkv_near, mix_padded, heads_came = order.scope(open_layer)
    qkv_norm, resid_norm, last = normed
    hidden_own = order.wait(hidden_own)

    resid_norm = order.hold(resid_norm)
    resid_hops = [hop_rep(resid_norm, k) for k in range(1, rep)]

    def prepare(inner):
        mix_copies = jnp.pad(w_mix1.astype(NARROW), ((0, 0), (0, LANES - hid)))
        mix_copies = inner.wait(jnp.broadcast_to(mix_copies[None], (devices, rows, LANES)))
        fields = fields_of(inner.hold(gathered))
        gain = fields[0][:, 2].reshape(1, width).astype(SINGLE)
        qkv_bias = fields[2].reshape(3, fsdp, cols).astype(SINGLE)
        branch_bias = fields[3].reshape(1, width).astype(SINGLE)
        branch_bias = branch_bias + fields[5].reshape(1, width).astype(SINGLE)
        first_bias = fields[4].reshape(group, hid_cols).astype(SINGLE)
        docs_all = fields[6].reshape(chips, 2, rep, length)
        my_qkv_bias = lax.dynamic_index_in_dim(qkv_bias, chip * 2 + core, 1, False)
        my_first_bias = lax.dynamic_index_in_dim(first_bias, core * rep + line, 0, True)
        docs_line = lax.dynamic_index_in_dim(docs_all, line, 2, False).astype(SINGLE)
        doc_rows = []
        for m in range(chips):
            pair = lax.dynamic_index_in_dim(docs_line, chip ^ m, 0, False)
            pair = pair + doc_group.shape[1] * jnp.arange(2, dtype=SINGLE)[:, None]
            doc_rows.append(jnp.where(core == 0, pair, pair[::-1]).reshape(1, 2 * length))
        position = jnp.arange(length).astype(SINGLE)
        frequency = 10000.0 ** (-jnp.arange(0, ROT, 2).astype(SINGLE) / ROT)
        angle = position[:, None] * frequency[None, :]
        cosine, sine = jnp.cos(angle), jnp.sin(angle)
        nothing = jnp.zeros_like(sine)
        rest = HEAD_DIM - ROT
        rope = jnp.stack(
            [
                jnp.concatenate([cosine, cosine, jnp.ones((length, rest), SINGLE)], 1),
                jnp.concatenate([-sine, nothing, jnp.zeros((length, rest), SINGLE)], 1),
                jnp.concatenate([nothing, sine, jnp.zeros((length, rest), SINGLE)], 1),
            ]
        )
        rope = jnp.concatenate([rope, rope], 1)
        pairs = [
            (pair, jnp.broadcast_to(pair.reshape(2 * length, 1), (2 * length, LANES)))
            for pair in doc_rows
        ]
        ready = (gain, my_qkv_bias.reshape(1, 3 * cols), my_first_bias, branch_bias, rope, pairs)
        leaves, tree = jax.tree.flatten(ready)
        return mix_copies, jax.tree.unflatten(tree, inner.wait(*leaves))

    def spread_weights(inner):
        near = [hop_chip(inner.hold(hidden_own), m) for m in around]
        mix_copies, prepared = inner.scope(prepare)
        first_mix = lax.all_to_all(inner.hold(mix_copies), AXES, 0, 0, tiled=True)
        near = inner.wait(*near)
        return near, inner.wait(first_mix).reshape(width, LANES), prepared

    hidden_near, mix_first, prepared = order.scope(spread_weights)
    gain, my_qkv_bias, my_first_bias, branch_bias, rope, doc_pairs = prepared
    resid_hops = order.wait(*resid_hops)

    heads_all = lax.all_gather(order.hold(heads_came), "rep", axis=0)

    def hidden_side(firsts, tokens):
        return pl.pallas_call(
            functools.partial(hidden_kernel, chips),
            grid=(blocks,),
            in_specs=[token_block(width)] + weight_specs(0) + [spec((1, hid_cols))],
            out_specs=[token_block(hid_cols)] * 2,
            out_shape=[
                shape((rep * length, hid_cols), NARROW),
                shape((rep * length, hid_cols), SINGLE),
            ],
            compiler_params=params(),
            cost_estimate=cost(2 * rep * length * width * hid_cols, 10**7),
            name="hidden",
        )(tokens, *firsts, my_first_bias)

    side = shape((rep * length, width), NARROW)
    places = [shape((length, width), NARROW)] * rep
    place_specs = [spec((length, width))] * rep

    def branch_side(seconds, act, *came):
        return pl.pallas_call(
            functools.partial(branch_kernel, chips, bool(came)),
            grid=(blocks,),
            in_specs=[token_block(hid_cols)] + weight_specs(1) + [token_block(width)] * len(came),
            out_specs=place_specs if came else token_block(width),
            out_shape=places if came else side,
            compiler_params=params(),
            cost_estimate=cost(2 * rep * length * width * hid_cols, 10**7),
            name="branch",
        )(act, *seconds, *came)


    qkv_first = [qkv_norm, *qkv_near]

    def feed_forward(inner):
        ends = []
        if square:
            upper = hop_chip(inner.hold(hidden_near[0])[:, 0:1], 2)
            lower = hop_chip(inner.hold(hidden_near[1])[:, 1:2], 1)
        whole = inner.wait(jnp.stack([resid_norm, *resid_hops]))
        other = inner.wait(swap_core(whole))
        qkv_other = inner.scope(lambda _: [swap_core(values) for values in qkv_first])
        if square:
            ends = inner.wait(upper, lower)
            halves = pass_on(inner.hold(*qkv_near), 1)
        firsts = [hidden_own, *hidden_near, *ends[:1]]
        seconds = [hidden_own, *hidden_near, *ends[1:]]
        sides = [values.reshape(rep * length, width) for values in (whole, other)]
        act_other, slope_other = inner.wait(*hidden_side(firsts, inner.hold(sides[1])))

        def branch_both(inner):
            back = inner.wait(branch_side(seconds, act_other))
            came = swap_core(back)
            act_own, slope_own = inner.wait(*hidden_side(firsts, inner.hold(sides[0])))
            return act_own, slope_own, branch_side(seconds, act_own, inner.wait(came))

        act_own, slope_own, branch_places = inner.scope(branch_both)
        qkv_last = []
        if square:
            qkv_last.append(inner.wait(jnp.concatenate(inner.wait(*halves), 1)))
            qkv_other.append(inner.wait(swap_core(qkv_last[0])))
        acts, slopes = (act_own, act_other), (slope_own, slope_other)
        return ends, sides, acts, slopes, branch_places, qkv_last, qkv_other

    ends, resid_sides, acts, slopes, branch_places, qkv_last, qkv_other = order.scope(
        feed_forward
    )
    first_parts = [hidden_own, *hidden_near, *ends[:1]]
    second_parts = [hidden_own, *hidden_near, *ends[1:]]
    qkv_own = [*qkv_first, *qkv_last]
    heads_all = order.wait(heads_all)

    branch_places = order.hold(*branch_places)
    mlp_hops = [hop_rep(branch_places[k], k) for k in range(1, rep)]

    def attend(heads, own, other, m):
        return pl.pallas_call(
            attend_kernel,
            out_shape=[
                shape((3, 2 * length, cols), NARROW),
                shape((2 * length, cols), NARROW),
                shape((length, width), SINGLE),
                shape((length, width), NARROW),
            ],
            compiler_params=params(),
            cost_estimate=cost(4 * 2 * 2 * length * width * cols, 8 * 10**6),
            name="attend",
        )(own, other, heads, my_qkv_bias, rope, *doc_pairs[m])


    def add_up(own, came, first=0, *along):
        rows_of = 32
        half = length // 2 // rows_of
        block_of = lambda index: spec((3, rows_of, width), index)
        return pl.pallas_call(
            functools.partial(merge_kernel, first, half),
            grid=(2 * half,),
            in_specs=[block_of(lambda i: (0, i, 0))] * 2
            + [block_of(lambda i: (0, jnp.clip(i - first, 0, half - 1), 0))] * len(along),
            out_specs=block_of(lambda i: (0, i, 0)),
            out_shape=shape(own.shape, NARROW),
            compiler_params=params(),
            cost_estimate=cost(10**6, 10**7),
            name="merge",
        )(own, came, *along)

    def near_sums(inner, results, came, halves):
        terms = []
        for m in around:
            along = ()
            if square:
                along = (length // 2 // 32, halves[1]) if m == 1 else (0, halves[0])
            terms.append(inner.wait(add_up(results[m], came[m], *along)))
        return terms

    def attention(inner):
        heads = inner.wait(heads_all.transpose(1, 0, 2, 3).reshape(width, 4 * cols))
        results, came = [None] * chips, [None] * chips

        def step(m):
            own, other = inner.hold(qkv_own[m], qkv_other[m])
            results[m] = inner.wait(*attend(heads, own, other, m))

        step(far)
        came[far] = swap_core(inner.hold(results[far][3]))
        step(1)
        came[far] = inner.wait(came[far])
        halves = None
        if square:
            halves = send_far(inner.wait(merge(results[far][2], came[far])), 0)
        for m in range(2, far):
            step(m)
        if square:
            halves = inner.wait(*halves)
        middle = range(1, far)
        swapped = inner.wait(swap_core(inner.wait(jnp.stack([results[m][3] for m in middle]))))
        for m in middle:
            came[m] = swapped[m - 1]
        terms = [merge(results[m][2], came[m]) for m in around]
        terms = inner.wait(*take_along(terms, halves, 0))
        hops = [hop_chip(terms[m - 1], m) for m in around]
        step(0)
        hops = inner.wait(*hops)
        came[0] = inner.wait(swap_core(inner.hold(results[0][3])))
        lows = [values[0] for values in results]
        return heads, lows, [values[1] for values in results], results[0][2], [came[0], *hops]

    heads, qkv_low, mixed_low, attn_own, attn_rest = order.scope(attention)
    mlp_parts = [branch_places[0], *order.wait(*mlp_hops)]

    mix_second = jnp.pad(w_mix2, ((0, LANES - hid), (0, LANES - mixes)))
    mixed_results = pl.pallas_call(
        functools.partial(mix_kernel, chips, len(attn_rest), rep, entries),
        grid=(length // MIX_ROWS,),
        in_specs=[
            scalar_spec(),
            flat2(width),
            flat2(width),
            *[flat2(width)] * (len(attn_rest) + rep),
            spec((1, width)),
            spec((1, width)),
            spec((width, LANES)),
            spec((1, LANES)),
            spec((LANES, LANES)),
            spec((1, LANES)),
            tall2(count),
            flat2(LANES),
            flat2(LANES),
        ],
        out_specs=[flat2(width)] * 5
        + [flat2(LANES)] * 4
        + [spec((1, width))] * 2
        + [spec((1, LANES))] * 2,
        out_shape=[
            shape((length, width), SINGLE),
            shape((length, width), SINGLE),
            shape((length, width), NARROW),
            shape((length, width), NARROW),
            shape((length, width), NARROW),
            shape((length, LANES), NARROW),
            shape((length, LANES), SINGLE),
            shape((length, LANES), SINGLE),
            shape((length, LANES), SINGLE),
            shape((1, width), SINGLE),
            shape((1, width), SINGLE),
            shape((1, LANES), SINGLE),
            shape((1, LANES), SINGLE),
        ],
        scratch_shapes=[pltpu.VMEM((MIX_ROWS, width), SINGLE)],
        compiler_params=params(),
        cost_estimate=cost(2 * 10**8, 10**7),
        name="mixing",
    )(
        chip_at,
        last,
        attn_own,
        *attn_rest,
        *mlp_parts,
        branch_bias,
        gain,
        mix_first,
        jnp.pad(b_mix1, (0, LANES - hid))[None],
        mix_second,
        jnp.pad(b_mix2, (0, LANES - mixes))[None],
        cotangent,
        token_weight,
        dots,
    )
    (
        entry,
        grad_entry,
        grad_low,
        grad_turned,
        scaled_low,
        grad_pre_low,
        mix_act,
        grad_coef,
        coef,
        grad_rms_gain,
        grad_branch_bias,
        grad_pre_sum,
        grad_coef_sum,
    ) = order.wait(*mixed_results)

    grad_hops = [hop_rep(grad_turned, k) for k in range(1, rep)]

    def attend_back(own, other, heads, qkv, rope, pair):
        return pl.pallas_call(
            attend_back_kernel,
            out_shape=[
                shape((3, 2 * length, cols), NARROW),
                shape((1, 3 * cols), SINGLE),
                shape((3, length, width), NARROW),
                shape((3, length, width), NARROW),
            ],
            compiler_params=params(),
            cost_estimate=cost(4 * 2 * 2 * length * width * cols, 8 * 10**6),
            name="attend_back",
        )(own, other, heads, qkv, rope, *pair)


    def back(inner, m, own, other):
        own, other = inner.hold(own, other)
        return inner.wait(*attend_back(own, other, heads, qkv_low[m], rope, doc_pairs[m]))

    def spread_branch(inner):
        swapped = inner.wait(swap_core(grad_low))
        near = [hop_chip(inner.hold(grad_low), m) for m in around]
        result = back(inner, 0, grad_low, swapped)
        near = inner.wait(*near)
        halves = pass_on(near, 0)
        next_streams = pl.pallas_call(
            next_kernel,
            grid=(steps,),
            in_specs=[tall(entries), flat(width), flat(LANES)],
            out_specs=tall(count),
            out_shape=shape((count, length, width), NARROW),
            compiler_params=params(),
            cost_estimate=cost(10**8, 10**7),
            name="next_streams",
        )(inner.hold(history), entry, coef)
        next_streams = inner.wait(next_streams)
        if square:
            near.append(inner.wait(jnp.concatenate(inner.wait(*halves), 0)))
        others = list(swap_core(jnp.stack(near)))
        others = inner.wait(*others)
        last = back(inner, far, near[far - 1], others[far - 1])
        grad_w_mix2 = transposed_times(mix_act, grad_coef, EXACT)[:hid, :mixes]
        grad_w_mix1 = transposed_times(scaled_low, grad_pre_low)[:, :hid]
        grad_w_mix1, grad_w_mix2 = inner.wait(grad_w_mix1, grad_w_mix2)
        return result, last, near, [swapped, *others], next_streams, grad_w_mix1, grad_w_mix2

    returned, terms = [None] * chips, [None] * chips
    returned[0], returned[far], branch_near, branch_other, *rest = order.scope(spread_branch)
    next_streams, grad_w_mix1, grad_w_mix2 = rest
    branch_own = [grad_low, *branch_near]
    grad_hops = order.wait(*grad_hops)

    interleave = lambda a, b: [values for pair in zip(a, b) for values in pair]
    row_block = width // fsdp

    def hidden_back_side(firsts, seconds, grad, slope, *came):
        return pl.pallas_call(
            functools.partial(hidden_back_kernel, chips, bool(came)),
            grid=(blocks,),
            in_specs=[token_block(width), token_block(hid_cols)]
            + weight_specs(0)
            + weight_specs(1)
            + [token_block(width)] * len(came),
            out_specs=[token_block(hid_cols), spec((1, hid_cols))]
            + (place_specs if came else [token_block(width)]),
            out_shape=[shape((rep * length, hid_cols), NARROW), shape((1, hid_cols), SINGLE)]
            + (places if came else [side]),
            compiler_params=params(),
            cost_estimate=cost(4 * rep * length * width * hid_cols, 2 * 10**7),
            name="hidden_back",
        )(grad, slope, *firsts, *seconds, *came)

    def outer(inner, lefts, rights):
        whole = lambda n: spec((rep * length, n))
        return inner.wait(
            *pl.pallas_call(
                outer_kernel,
                grid=(chips,),
                in_specs=[spec((rep * length, part), lambda i: (0, i))] * 2 + [whole(hid_cols)] * 2,
                out_specs=[spec((part, hid_cols))] * chips,
                out_shape=[shape((part, hid_cols), NARROW)] * chips,
                compiler_params=params(),
                cost_estimate=cost(4 * rep * length * width * hid_cols, 2 * 10**7),
                name="outer",
            )(*lefts, *rights)
        )

    def feed_forward_back(inner):
        whole = inner.wait(jnp.stack([grad_turned, *grad_hops]))
        came = [swap_core(returned[far][3]), swap_core(whole), swap_core(returned[0][3])]
        grad_own = whole.reshape(rep * length, width)
        low_own, sum_own, back_own = inner.wait(
            *hidden_back_side(first_parts, second_parts, inner.hold(grad_own), slopes[0])
        )
        came = inner.wait(*came)
        grad_other = came[1].reshape(rep * length, width)
        far_term = inner.wait(add_up(returned[far][2], came[0]))
        halves = send_far(far_term, 1) if square else ()
        low_other, sum_other, back = inner.wait(
            *hidden_back_side(first_parts, second_parts, inner.hold(grad_other), slopes[1])
        )

        def sums_of_cores(_):
            came = swap_core(back)
            at = lambda values, k: values[k * length : (k + 1) * length]
            return [merge(at(back_own, k), at(came, k)) for k in range(rep)]

        merged = inner.scope(sums_of_cores)
        halves = inner.wait(*halves) if square else [far_term]
        lows = (low_own, low_other)
        return (grad_own, grad_other), lows, sum_own + sum_other, merged, halves, came[0], came[2]

    grad_sides, grad_hidden, grad_first_bias, grad_resid, halves, far_came, own_came = order.scope(
        feed_forward_back
    )

    def total_hidden(inner, own, hops):
        total = own.astype(SINGLE)
        for values in inner.wait(*hops):
            total = total + values.astype(SINGLE)
        return inner.wait(total.astype(NARROW).reshape(group, rows, hid_cols))

    def whole_rows(came):
        return came.transpose(1, 0, 2).reshape(rows, hidden).astype(SINGLE)

    def exchange(sums):
        widths = [values.shape[1] for values in sums]
        return widths, lax.all_to_all(jnp.concatenate(sums, 1), AXES, 0, 0, tiled=True)

    def attention_back(inner):
        results = {0: returned[0], far: returned[far]}
        second_grads = outer(inner, (inner.hold(grad_sides[0]), grad_sides[1]), acts)
        halves_out = send_far(inner.hold(second_grads[far]), 0)
        results[1] = back(inner, 1, branch_own[1], branch_other[1])
        held = second_grads[1:]
        if square:
            halves_out = inner.wait(*halves_out)
            held = inner.wait(*take_along(second_grads[1:far], halves_out, 0))
        hops = [hop_chip(held[m - 1], m) for m in around]
        for m in range(2, far):
            results[m] = back(inner, m, branch_own[m], branch_other[m])
        linears = inner.hold(*[results[m][0] for m in range(chips)])
        grad_heads = pl.pallas_call(
            functools.partial(heads_grad_kernel, chips),
            grid=(fsdp,),
            in_specs=[spec((3, length, row_block), lambda i: (0, 0, i))] * fsdp
            + [spec((length, row_block), lambda i: (0, i))] * fsdp
            + [spec((3, 2 * length, cols))] * chips
            + [spec((2 * length, cols))] * chips,
            out_specs=spec((rep, 1, rows, 4 * cols), lambda i: (0, i, 0, 0)),
            out_shape=shape((rep, fsdp, rows, 4 * cols), NARROW),
            compiler_params=params(),
            cost_estimate=cost(8 * fsdp * length * width * cols, 3 * 10**7),
            name="heads_grad",
        )(
            *interleave(qkv_own, qkv_other),
            *interleave(branch_own, branch_other),
            *linears,
            *mixed_low,
        )
        grad_heads = inner.wait(grad_heads)
        hops = inner.wait(*hops)
        middle = [results[m] for m in range(1, far)]
        return grad_heads, middle, second_grads[0], hops

    def residual_back(inner):
        hops = inner.hold(*grad_resid)
        hops = [hop_rep(hops[k], k) for k in range(1, rep)]
        results = inner.scope(attention_back)
        return inner.wait(*hops), *results

    resid_hops, grad_heads, returned[1:far], second_own_grad, second_hops = order.scope(residual_back)
    qkv_biases = [results[1] for results in returned]
    grad_resid = [grad_resid[0], *resid_hops]

    def by_owner(vector):
        return vector.reshape(-1, devices, rows).transpose(1, 0, 2).reshape(devices, -1)

    grad_heads = lax.psum_scatter(grad_heads, "rep", scatter_dimension=0, tiled=False)
    def second_sum(inner):
        return total_hidden(inner, second_own_grad, second_hops)

    second_total = order.scope(second_sum)
    second_came = lax.all_to_all(order.hold(second_total), GROUP, 0, 0, tiled=True)

    def send_terms(inner):
        middle = range(1, far)
        swaps = [swap_core(inner.hold(returned[m][3])) for m in middle]
        swaps = list(inner.wait(*swaps)) if len(swaps) > 1 else [inner.wait(*swaps)]
        owns = [results[2] for results in returned]
        near_terms = near_sums(inner, owns, [None, *swaps, far_came], halves)
        qkv_back = [hop_chip(near_terms[m - 1], m) for m in around]
        first_grads = outer(inner, (inner.hold(resid_sides[0]), resid_sides[1]), grad_hidden)
        first_halves = send_far(inner.hold(first_grads[far]), 0)

        def pack_sums(_):
            qkv_bias_all = lax.dynamic_update_index_in_dim(
                jnp.zeros((3, fsdp, cols), SINGLE),
                sum(qkv_biases).reshape(3, cols),
                chip * 2 + core,
                1,
            )
            tail = jnp.concatenate(
                [grad_pre_sum[0, :hid], grad_w_mix2.reshape(-1), grad_coef_sum[0, :mixes]]
            )
            sums = [
                by_owner(grad_rms_gain[0]),
                qkv_bias_all.reshape(devices, -1),
                grad_branch_bias.reshape(devices, -1),
                grad_w_mix1.reshape(devices, -1),
                jnp.broadcast_to(tail[None], (devices, tail.shape[0])),
            ]
            size = sum(values.shape[1] for values in sums)
            empty = -size % (ROWS * LANES)
            sums.append(jnp.zeros((devices, empty), SINGLE))
            return jnp.concatenate(sums, 1).astype(NARROW).reshape(devices, ROWS, -1)

        sums = inner.scope(pack_sums)
        held = first_grads[1:]
        if square:
            first_halves = inner.wait(*first_halves)
        qkv_back = inner.wait(*qkv_back)
        if square:
            held = inner.wait(*take_along(first_grads[1:far], first_halves, 0))
        return first_grads[0], held, qkv_back, sums

    first_own_grad, first_terms, qkv_back, sums = order.scope(send_terms)
    second_came = order.wait(second_came)
    widths = [rows, 3 * cols * fsdp // devices, rows, rows * hid]

    qkv_rest = [own_came, *qkv_back]

    def close_layer(inner):
        every = lax.all_to_all(inner.hold(sums), AXES, 0, 0, tiled=True)
        held = inner.hold(*first_terms)
        first_hops = [hop_chip(held[m - 1], m) for m in around]
        close_from = inner.hold(history, cotangent)
        grad_history, grad_mix_in, grad_affine = pl.pallas_call(
            functools.partial(close_kernel, chips, len(qkv_rest), rep),
            grid=(steps,),
            in_specs=[
                scalar_spec(),
                tall(entries),
                tall(count),
                flat(LANES),
                flat(LANES),
                flat(LANES),
                spec((4, width)),
                flat(width),
                *[tall(3)] * (1 + len(qkv_rest)),
                *[flat(width)] * rep,
            ],
            out_specs=[tall(entries), flat(count * entries), spec((4, width))],
            out_shape=[
                shape((entries, length, width), SINGLE),
                shape((length, count * entries), SINGLE),
                shape((4, width), SINGLE),
            ],
            scratch_shapes=[
                pltpu.VMEM((count, ROWS, width), SINGLE),
                pltpu.VMEM((ROWS, width), SINGLE),
                pltpu.VMEM((5 * count * ROWS, width), NARROW),
            ],
            compiler_params=params(),
            cost_estimate=cost(2 * 10**8, 2 * 10**7),
            name="close",
        )(
            chip_at,
            *close_from,
            coef,
            token_weight,
            mix_padded,
            affine,
            grad_entry,
            returned[0][2],
            *qkv_rest,
            *grad_resid,
        )
        grad_history, grad_mix_in, grad_affine = inner.wait(grad_history, grad_mix_in, grad_affine)
        every = inner.wait(every)
        first_bias_all = lax.dynamic_update_index_in_dim(
            jnp.zeros((group, hid_cols), SINGLE), grad_first_bias[0], core * rep + line, 0
        )
        late = [by_owner(grad_affine), first_bias_all.reshape(devices, -1)]
        late = inner.wait(jnp.concatenate(late, 1))
        late = lax.all_to_all(late, AXES, 0, 0, tiled=True)

        first_total = total_hidden(inner, first_own_grad, first_hops)
        return grad_history, grad_mix_in, first_total, inner.wait(late), every

    grad_history, grad_mix_in, first_total, every, sums = order.scope(close_layer)
    first_came = lax.all_to_all(order.hold(first_total), GROUP, 0, 0, tiled=True)
    grad_w_fc2 = order.wait(whole_rows(second_came))
    every = order.wait(jnp.sum(every, 0))
    total = order.wait(jnp.sum(sums.astype(SINGLE), 0).reshape(-1))
    grad_heads = order.wait(grad_heads)

    def around_ring(inner):
        split = inner.hold(grad_heads).reshape(chips, 2, rows, 4 * cols)
        parts = [lax.dynamic_index_in_dim(split, chip ^ m, 0, False) for m in range(chips)]
        parts = [parts[0]] + [hop_chip(parts[m], m) for m in range(1, chips)]
        parts = jnp.stack(inner.wait(*parts))
        mine = lax.dynamic_index_in_dim(parts, core, 1, False)
        came = swap_core(lax.dynamic_index_in_dim(parts, 1 - core, 1, False))
        result = jnp.zeros((chips, 2, rows, 4 * cols), NARROW)
        for m in range(chips):
            pair = jnp.where(core == 0, jnp.stack([mine[m], came[m]]), jnp.stack([came[m], mine[m]]))
            result = lax.dynamic_update_index_in_dim(result, pair, chip ^ m, 0)
        result = result.reshape(fsdp, rows, 4, cols).transpose(1, 2, 0, 3).astype(SINGLE)
        return result[:, :3].reshape(rows, 3 * width), result[:, 3].reshape(rows, width)

    grad_w_qkv, grad_w_out = order.scope(around_ring)
    first_came = order.wait(first_came)
    grad_w_fc1 = whole_rows(first_came)
    outs, start = [], 0
    for size in widths:
        outs.append(total[start : start + size])
        start += size
    outs.append(total[start:])
    affine_sums = every[: 4 * rows].reshape(4, rows)
    gain_grads = jnp.stack([affine_sums[0], affine_sums[2], outs[0]])
    bias_grads = jnp.stack([affine_sums[1], affine_sums[3]])
    return (
        next_streams,
        grad_history,
        grad_mix_in,
        gain_grads,
        bias_grads,
        grad_w_qkv,
        outs[1],
        grad_w_out,
        outs[2],
        grad_w_fc1,
        every[4 * rows :],
        grad_w_fc2,
        outs[2],
        outs[3].reshape(rows, hid),
        outs[4][:hid],
        outs[4][hid : hid + hid * mixes].reshape(hid, mixes),
        outs[4][hid + hid * mixes : hid + hid * mixes + mixes],
    )


def solution(mesh):
    fsdp, rep = mesh.shape["fsdp"], mesh.shape["rep"]
    chips = fsdp // 2
    finer = Mesh(mesh.devices.reshape(chips, 2, rep), AXES)
    rows = P(AXES, None)
    line = P(AXES)
    streams = P(None, AXES, None)
    columns = P(None, AXES)
    in_specs = (
        streams,
        rows,
        rows,
        rows,
        P(),
        columns,
        columns,
        rows,
        line,
        rows,
        line,
        rows,
        line,
        rows,
        line,
        rows,
        P(),
        P(),
        P(),
        streams,
    )
    out_specs = (
        streams,
        streams,
        rows,
        columns,
        columns,
        rows,
        line,
        rows,
        line,
        rows,
        line,
        rows,
        line,
        rows,
        P(),
        P(),
        P(),
    )
    return jax.shard_map(
        functools.partial(on_device, chips, rep),
        mesh=finer,
        in_specs=in_specs,
        out_specs=out_specs,
        check_vma=False,
    )
```

```python
import functools
import math

import jax
import jax.numpy as jnp
from jax import lax
from jax.experimental import pallas as pl
from jax.experimental.pallas import tpu as pltpu
from jax.sharding import Mesh
from jax.sharding import PartitionSpec as P

HEAD_DIM = 128
ROT = 32
LANES = 128
NARROW = jnp.bfloat16
SINGLE = jnp.float32
NORM_EPSILON = 1e-05
RMS_EPSILON = 1e-06
AXES = ("chip", "core", "rep")
GROUP = ("core", "rep")
RING = ("chip", "core")
ROWS = 16
MIX_ROWS = 64
CHUNK = 512
VMEM_BYTES = 56 * 1024 * 1024
EXACT = lax.Precision.HIGHEST


def times(left, right, precision=None):
    return lax.dot_general(
        left, right, (((1,), (0,)), ((), ())), precision=precision, preferred_element_type=SINGLE
    )


def times_transposed(left, right, precision=None):
    return lax.dot_general(
        left, right, (((1,), (1,)), ((), ())), precision=precision, preferred_element_type=SINGLE
    )


def transposed_times(left, right, precision=None):
    return lax.dot_general(
        left, right, (((0,), (0,)), ((), ())), precision=precision, preferred_element_type=SINGLE
    )


def gelu_parts(values):
    cumulative = 0.5 * (1.0 + lax.erf(values * math.sqrt(0.5)))
    density = jnp.exp(-0.5 * values * values) * (1.0 / math.sqrt(2.0 * math.pi))
    return values * cumulative, cumulative + values * density


def params(*semantics):
    return pltpu.CompilerParams(vmem_limit_bytes=VMEM_BYTES)


def spec(shape, index=None):
    if index is None:
        index = lambda *i: (0,) * len(shape)
    return pl.BlockSpec(shape, index)


def scalar_spec():
    return pl.BlockSpec(memory_space=pltpu.SMEM)


def cost(flops, moved):
    return pl.CostEstimate(flops=flops // 1000, bytes_accessed=moved // 1000, transcendentals=0)


def mean(values):
    return jnp.mean(values, -1, keepdims=True)


def same_token(shape):
    row = lax.broadcasted_iota(jnp.int32, shape, 0)
    col = lax.broadcasted_iota(jnp.int32, shape, 1)
    return row == col % ROWS


def places(first, count):
    row = lax.broadcasted_iota(jnp.int32, (LANES, count * ROWS), 0)
    col = lax.broadcasted_iota(jnp.int32, (LANES, count * ROWS), 1)
    return (row == first + col // ROWS).astype(NARROW)


def two_parts(values):
    high = values.astype(NARROW)
    return jnp.concatenate([high, (values - high.astype(SINGLE)).astype(NARROW)], 0)


def spread_out(coef, count, entries, stride):
    mask = same_token((ROWS, entries * ROWS))
    parts = two_parts(coef)
    highs, lows = [], []
    for s in range(count):
        full = times(parts, places(s * stride, entries))
        highs.append(jnp.where(mask, full[:ROWS], 0.0).astype(NARROW))
        lows.append(jnp.where(mask, full[ROWS:], 0.0).astype(NARROW))
    return jnp.concatenate(highs, 0), jnp.concatenate(lows, 0)


def draw_in(products, count, entries, stride):
    mask = same_token((ROWS, entries * ROWS))
    total = None
    for s in range(count):
        own = jnp.where(mask, products[s * ROWS : (s + 1) * ROWS], 0.0)
        term = times_transposed(two_parts(own), places(s * stride, entries))
        total = term if s == 0 else total + term
    return total[:ROWS] + total[ROWS:]


def blend_streams(hist, mix, streams):
    entries, _, width = hist.shape
    count = streams.shape[0]
    both = jnp.concatenate(spread_out(mix[...], count, entries, entries), 0)
    for start in range(0, width, CHUNK):
        sources = hist[:, :, start : start + CHUNK].reshape(entries * ROWS, CHUNK)
        total = times(both, sources)
        total = total[: count * ROWS] + total[count * ROWS :]
        streams[:, :, start : start + CHUNK] = total.reshape(count, ROWS, CHUNK)


def streams_kernel(chips, chip, hist, mix, affine, qkv, resid, last, streams):
    width = hist.shape[2]
    blend_streams(hist, mix, streams)
    for s in range(4):
        values = streams[s]
        center = values - mean(values)
        row = 0 if s < 3 else 2
        normed = (
            center * lax.rsqrt(mean(center * center) + NORM_EPSILON) * affine[row : row + 1]
            + affine[row + 1 : row + 2]
        )
        if s < 3:
            qkv[s] = normed.astype(NARROW)
        else:
            last[...] = values
            streams[0] = normed
    part = width // chips
    for m in range(chips):
        start = pl.multiple_of((chip[0] ^ m) * part, part)
        resid[:, m * part : (m + 1) * part] = streams[0, :, pl.ds(start, part)].astype(NARROW)


def history_dots_kernel(hist, cot, weight, out):
    entries, rows, width = hist.shape
    count = cot.shape[0]
    products = times_transposed(
        cot[...].reshape(count * rows, width), hist[...].reshape(entries * rows, width)
    )
    out[...] = draw_in(products, count, entries, entries + 1) * weight[...]


def mix_kernel(
    chips,
    near,
    rep,
    entries,
    chip,
    last,
    attn_own,
    *refs,
):
    attn_rest, mlp_parts, refs = refs[:near], refs[near : near + rep], refs[near + rep :]
    mix_body(chips, entries, chip, last, attn_own, attn_rest, mlp_parts, *refs)


def mix_body(
    chips,
    entries,
    chip,
    last,
    attn_own,
    attn_rest,
    mlp_parts,
    branch_bias,
    gain,
    first,
    first_bias,
    second,
    second_bias,
    cot,
    weight,
    dots,
    entry_out,
    grad_out,
    grad_low,
    grad_turned,
    scaled_out,
    grad_pre_low,
    act_out,
    grad_coef_out,
    coef_out,
    grad_gain,
    grad_bias,
    grad_pre_sum,
    grad_coef_sum,
    turned,
):
    rows, width = last.shape
    count = cot.shape[0]
    entry = last[...] + attn_own[...] + branch_bias[...]
    for part in attn_rest:
        entry = entry + part[...].astype(SINGLE)
    total = mlp_parts[0][...].astype(SINGLE)
    for values in mlp_parts[1:]:
        total = total + values[...].astype(SINGLE)
    part = width // chips
    for m in range(chips):
        start = pl.multiple_of((chip[0] ^ m) * part, part)
        turned[:, pl.ds(start, part)] = total[:, m * part : (m + 1) * part]
    entry = entry + turned[...]
    entry_out[...] = entry
    scale = lax.rsqrt(mean(entry * entry) + RMS_EPSILON)
    scaled = (entry * scale * gain[...]).astype(NARROW)
    scaled_out[...] = scaled
    pre = times(scaled, first[...]) + first_bias[...]
    act, slope = gelu_parts(pre)
    act_out[...] = act
    coef = times(act, second[...], EXACT) + second_bias[...]
    coef_out[...] = coef
    lane = lax.broadcasted_iota(jnp.int32, (rows, LANES), 1)
    grad_coef = dots[...]
    grad = jnp.zeros((rows, width), SINGLE)
    for s in range(count):
        arriving = cot[s].astype(SINGLE)
        place = s * (entries + 1) + entries
        total = jnp.sum(arriving * entry, -1, keepdims=True) * weight[:, :1]
        grad_coef = jnp.where(lane == place, total, grad_coef)
        grad = grad + (coef[:, place : place + 1] * weight[:, :1]) * arriving
    grad_coef_out[...] = grad_coef
    grad_pre = slope * times_transposed(grad_coef, second[...], EXACT)
    grad_pre_narrow = grad_pre.astype(NARROW)
    grad_pre_low[...] = grad_pre_narrow
    grad_scaled = times_transposed(grad_pre_narrow, first[...])
    gained = grad_scaled * gain[...]
    grad = grad + scale * gained - entry * (scale * scale * scale * mean(gained * entry))
    grad_out[...] = grad
    grad_low[...] = grad.astype(NARROW)
    for m in range(chips):
        start = pl.multiple_of((chip[0] ^ m) * part, part)
        grad_turned[:, m * part : (m + 1) * part] = grad_out[:, pl.ds(start, part)].astype(NARROW)

    @pl.when(pl.program_id(0) == 0)
    def _():
        grad_gain[...] = jnp.zeros_like(grad_gain)
        grad_bias[...] = jnp.zeros_like(grad_bias)
        grad_pre_sum[...] = jnp.zeros_like(grad_pre_sum)
        grad_coef_sum[...] = jnp.zeros_like(grad_coef_sum)

    grad_gain[...] += jnp.sum(grad_scaled * entry * scale, 0, keepdims=True)
    grad_bias[...] += jnp.sum(grad, 0, keepdims=True)
    grad_pre_sum[...] += jnp.sum(grad_pre, 0, keepdims=True)
    grad_coef_sum[...] += jnp.sum(grad_coef, 0, keepdims=True)


def next_kernel(hist, entry, coef, out):
    entries, _, width = hist.shape
    count = out.shape[0]
    both = jnp.concatenate(spread_out(coef[...], count, entries, entries + 1), 0)
    for start in range(0, width, CHUNK):
        cols = slice(start, start + CHUNK)
        sources = hist[:, :, cols].reshape(entries * ROWS, CHUNK)
        total = times(both, sources)
        total = total[: count * ROWS] + total[count * ROWS :]
        for s in range(count):
            place = s * (entries + 1) + entries
            out[s, :, cols] = (
                total[s * ROWS : (s + 1) * ROWS] + coef[:, place : place + 1] * entry[:, cols]
            ).astype(NARROW)


def close_kernel(
    chips,
    near,
    rep,
    chip,
    hist,
    cot,
    coef,
    weight,
    mix,
    affine,
    grad_entry,
    qkv_own,
    *refs,
):
    qkv_rest, resid, refs = refs[:near], refs[near : near + rep], refs[near + rep :]
    close_body(
        chips, chip, hist, cot, coef, weight, mix, affine, grad_entry, resid, qkv_own, qkv_rest, *refs
    )


def close_body(
    chips,
    chip,
    hist,
    cot,
    coef,
    weight,
    mix,
    affine,
    grad_entry,
    resid,
    qkv_own,
    qkv_rest,
    grad_hist,
    grad_mix,
    grad_affine,
    streams,
    turned,
    stacked,
):
    entries, rows, width = hist.shape
    count = cot.shape[0]
    part = width // chips

    @pl.when(pl.program_id(0) == 0)
    def _():
        grad_affine[...] = jnp.zeros_like(grad_affine)

    blend_streams(hist, mix, streams)
    for s in range(count):
        values = streams[s]
        center = values - mean(values)
        scale = lax.rsqrt(mean(center * center) + NORM_EPSILON)
        unit = center * scale
        if s < 3:
            arriving = qkv_own[s].astype(SINGLE)
            for rest in qkv_rest:
                arriving = arriving + rest[s].astype(SINGLE)
        else:
            total = resid[0][...].astype(SINGLE)
            for rest in resid[1:]:
                total = total + rest[...].astype(SINGLE)
            for m in range(chips):
                start = pl.multiple_of((chip[0] ^ m) * part, part)
                turned[:, pl.ds(start, part)] = total[:, m * part : (m + 1) * part]
            arriving = turned[...]
        row = 0 if s < 3 else 2
        grad_affine[row : row + 1] += jnp.sum(arriving * unit, 0, keepdims=True)
        grad_affine[row + 1 : row + 2] += jnp.sum(arriving, 0, keepdims=True)
        gained = arriving * affine[row : row + 1]
        grad = scale * (gained - mean(gained) - unit * mean(gained * unit))
        streams[s] = grad if s < 3 else grad + grad_entry[...]
    size = count * rows
    grads = streams[...].reshape(size, width)
    high = grads.astype(NARROW)
    stacked[0:size] = high
    stacked[size : 2 * size] = (grads - high.astype(SINGLE)).astype(NARROW)
    stacked[2 * size : 3 * size] = high
    arriving = cot[...].reshape(size, width)
    stacked[3 * size : 4 * size] = arriving
    stacked[4 * size : 5 * size] = arriving
    mix_high, mix_low = spread_out(mix[...], count, entries, entries)
    out_high, out_low = spread_out(coef[...] * weight[...], count, entries, entries + 1)
    spread = jnp.concatenate([mix_high, mix_high, mix_low, out_high, out_low], 0)
    products = jnp.zeros((2 * size, entries * rows), SINGLE)
    for start in range(0, width, CHUNK):
        cols = slice(start, start + CHUNK)
        grad_hist[:, :, cols] = transposed_times(spread, stacked[:, cols]).reshape(
            entries, rows, CHUNK
        )
        sources = hist[:, :, cols].reshape(entries * rows, CHUNK)
        products = products + times_transposed(stacked[0 : 2 * size, cols], sources)
    products = products[:size] + products[size:]
    grad_mix[...] = draw_in(products, count, entries, entries)[:, : grad_mix.shape[1]]


def turn(values, rope, sign):
    forward = pltpu.roll(values, HEAD_DIM - ROT // 2, 1)
    backward = pltpu.roll(values, ROT // 2, 1)
    return values * rope[0] + sign * (forward * rope[1] + backward * rope[2])


def allowed_pairs(row, column):
    size = row.shape[1]
    query = lax.broadcasted_iota(jnp.int32, (size, size), 0)
    key = lax.broadcasted_iota(jnp.int32, (size, size), 1)
    return (key <= query) & (row == column[:, :1])


def probabilities(query, key, allowed):
    scores = jnp.where(allowed, times_transposed(query, key) * HEAD_DIM ** (-0.5), -1e30)
    raised = jnp.exp(scores - jnp.max(scores, -1, keepdims=True))
    return raised / jnp.sum(raised, -1, keepdims=True)


def attend_kernel(own, other, weight, bias, rope, doc_row, doc_column, qkv, mixed, out_own, out_other):
    _, length, _ = own.shape
    cols = bias.shape[1] // 3
    for i in range(3):
        tokens = jnp.concatenate([own[i], other[i]], 0)
        linear = times(tokens, weight[:, i * cols : (i + 1) * cols]) + bias[:, i * cols : (i + 1) * cols]
        for start in range(0, cols, HEAD_DIM):
            head = slice(start, start + HEAD_DIM)
            piece = linear[:, head]
            qkv[i, :, head] = (turn(piece, rope, 1.0) if i < 2 else piece).astype(NARROW)
    allowed = allowed_pairs(doc_row[...], doc_column[...])
    for start in range(0, cols, HEAD_DIM):
        head = slice(start, start + HEAD_DIM)
        probs = probabilities(qkv[0, :, head], qkv[1, :, head], allowed)
        mixed[:, head] = times(probs.astype(NARROW), qkv[2, :, head]).astype(NARROW)
    result = times_transposed(mixed[...], weight[:, 3 * cols :])
    out_own[...] = result[:length]
    out_other[...] = result[length:].astype(NARROW)


def attend_back_kernel(
    own, other, weight, qkv, rope, doc_row, doc_column, grad_linear, grad_bias, out_own, out_other
):
    length = own.shape[0]
    cols = qkv.shape[2]
    scale = HEAD_DIM ** (-0.5)
    arriving = jnp.concatenate([own[...], other[...]], 0)
    grad_mixed = times(arriving, weight[:, 3 * cols :]).astype(NARROW)
    allowed = allowed_pairs(doc_row[...], doc_column[...])
    for start in range(0, cols, HEAD_DIM):
        head = slice(start, start + HEAD_DIM)
        query, key, value = (qkv[i, :, head] for i in range(3))
        grad = grad_mixed[:, head]
        probs = probabilities(query, key, allowed)
        grad_value = transposed_times(probs.astype(NARROW), grad)
        grad_probs = times_transposed(grad, value)
        inner = jnp.sum(probs * grad_probs, -1, keepdims=True)
        grad_scores = (probs * (grad_probs - inner)).astype(NARROW)
        grad_query = turn(times(grad_scores, key) * scale, rope, -1.0)
        grad_key = turn(transposed_times(grad_scores, query) * scale, rope, -1.0)
        for i, values in enumerate((grad_query, grad_key, grad_value)):
            grad_bias[:, i * cols + start : i * cols + start + HEAD_DIM] = jnp.sum(
                values, 0, keepdims=True
            )
            grad_linear[i, :, head] = values.astype(NARROW)
    for i in range(3):
        result = times_transposed(grad_linear[i], weight[:, i * cols : (i + 1) * cols])
        out_own[i] = result[:length].astype(NARROW)
        out_other[i] = result[length:].astype(NARROW)


def heads_grad_kernel(chips, *refs):
    norms, branches = refs[: 2 * chips], refs[2 * chips : 4 * chips]
    linears, mixeds, out = refs[4 * chips : 5 * chips], refs[5 * chips : 6 * chips], refs[6 * chips]
    cols = mixeds[0].shape[1]
    rep, _, rows, _ = out.shape
    for i in range(4):
        total = None
        for m in range(chips):
            sides = norms[2 * m : 2 * m + 2] if i < 3 else branches[2 * m : 2 * m + 2]
            left = jnp.concatenate([values[i] if i < 3 else values[...] for values in sides], 0)
            right = linears[m][i] if i < 3 else mixeds[m][...]
            term = transposed_times(left, right)
            total = term if total is None else total + term
        total = total.astype(NARROW)
        for k in range(rep):
            out[k, 0, :, i * cols : (i + 1) * cols] = total[k * rows : (k + 1) * rows]


def rows_of_weight(block):
    group, _, rows, cols = block.shape
    return block[...].reshape(group * rows, cols)


def hidden_kernel(chips, tokens, *refs):
    weights, (bias, act_out, slope_out) = refs[:chips], refs[chips:]
    part = weights[0].shape[0] * weights[0].shape[2]
    total = bias[...]
    for m in range(chips):
        total = total + times(tokens[:, m * part : (m + 1) * part], rows_of_weight(weights[m]))
    act, slope = gelu_parts(total)
    act_out[...] = act.astype(NARROW)
    slope_out[...] = slope


def put_places(outs, length, cols, result):
    many = result.shape[0] // length
    for k, out in enumerate(outs):

        @pl.when(pl.program_id(0) == k // many)
        def _():
            out[:, cols] = result[(k % many) * length : (k % many + 1) * length].astype(NARROW)


def branch_kernel(chips, merged, act, *refs):
    weights, refs = refs[:chips], refs[chips:]
    part = weights[0].shape[0] * weights[0].shape[2]
    for m in range(chips):
        cols = slice(m * part, (m + 1) * part)
        result = times_transposed(act[...], rows_of_weight(weights[m]))
        if merged:
            put_places(refs[1:], refs[1].shape[0], cols, result + refs[0][:, cols].astype(SINGLE))
        else:
            refs[0][:, cols] = result.astype(NARROW)


def hidden_back_kernel(chips, merged, grad, slope, *refs):
    firsts, seconds, refs = refs[:chips], refs[chips : 2 * chips], refs[2 * chips :]
    came, refs = (refs[0], refs[1:]) if merged else (None, refs)
    grad_low, grad_sum, *outs = refs
    part = firsts[0].shape[0] * firsts[0].shape[2]
    total = None
    for m in range(chips):
        term = times(grad[:, m * part : (m + 1) * part], rows_of_weight(seconds[m]))
        total = term if m == 0 else total + term
    total = total * slope[...]

    @pl.when(pl.program_id(0) == 0)
    def _():
        grad_sum[...] = jnp.zeros_like(grad_sum)

    grad_sum[...] += jnp.sum(total, 0, keepdims=True)
    low = total.astype(NARROW)
    grad_low[...] = low
    for m in range(chips):
        cols = slice(m * part, (m + 1) * part)
        result = times_transposed(low, rows_of_weight(firsts[m]))
        if merged:
            put_places(outs, outs[0].shape[0], cols, result + came[:, cols].astype(SINGLE))
        else:
            outs[0][:, cols] = result.astype(NARROW)


def outer_kernel(left_own, left_other, right_own, right_other, *outs):
    result = (
        transposed_times(left_own[...], right_own[...])
        + transposed_times(left_other[...], right_other[...])
    ).astype(NARROW)
    for m, out in enumerate(outs):

        @pl.when(pl.program_id(0) == m)
        def _():
            out[...] = result


def merge_kernel(first, count, own, came, *refs):
    total = own[...].astype(SINGLE) + came[...].astype(SINGLE)
    refs[-1][...] = total.astype(NARROW)
    if len(refs) > 1:

        @pl.when((pl.program_id(0) >= first) & (pl.program_id(0) < first + count))
        def _():
            refs[-1][...] = (total + refs[0][...].astype(SINGLE)).astype(NARROW)


def pack_hidden_kernel(first, second, out):
    cols = out.shape[3]
    for b in range(out.shape[0]):
        out[b, 0] = first[:, b * cols : (b + 1) * cols].astype(NARROW)
        out[b, 1] = second[:, b * cols : (b + 1) * cols].astype(NARROW)


def join_heads_kernel(chips, chip, core, swapped, *refs):
    parts, out = refs[:chips], refs[chips]
    for m in range(chips):
        place = 2 * (chip[0] ^ m)
        out[place + core[0]] = parts[m][core[0]]
        out[place + 1 - core[0]] = swapped[m]


def pack_small_kernel(*refs):
    out = refs[-1]
    row = 0
    out[...] = jnp.zeros_like(out)
    for values in refs[:-1]:
        for i in range(values.shape[0]):
            for start in range(0, values.shape[1], LANES):
                stop = min(start + LANES, values.shape[1])
                piece = values[i : i + 1, start:stop].astype(NARROW)
                out[:, row, : stop - start] = jnp.broadcast_to(piece, (out.shape[0], stop - start))
                row += 1


def pack_heads_kernel(chips, chip, qkv, out_weight, *outs):
    cols = outs[0].shape[2] // 4
    width = out_weight.shape[1]
    for m in range(chips):
        for c in range(2):
            start = pl.multiple_of(((chip[0] ^ m) * 2 + c) * cols, cols)
            for i in range(3):
                outs[m][c, :, i * cols : (i + 1) * cols] = qkv[
                    :, pl.ds(i * width + start, cols)
                ].astype(NARROW)
            outs[m][c, :, 3 * cols :] = out_weight[:, pl.ds(start, cols)].astype(NARROW)


class Order:
    def __init__(self, legal):
        self.legal = legal
        self.last = ()

    def hold(self, *values):
        tied = lax.optimization_barrier(tuple(values) + self.last)[: len(values)]
        return tied[0] if len(values) == 1 else tied

    def wait(self, *values):
        tied = lax.optimization_barrier(tuple(values) + self.last)[: len(values)]
        self.last = (tied[0],)
        return tied[0] if len(values) == 1 else list(tied)

    def scope(self, steps):
        inside = lambda: steps(Order(self.legal))
        shapes = jax.eval_shape(inside)
        never = lambda: jax.tree.map(lambda leaf: jnp.zeros(leaf.shape, leaf.dtype), shapes)
        results = lax.cond(self.hold(self.legal), inside, never)
        smallest = min(jax.tree.leaves(results), key=lambda leaf: leaf.size)
        self.last = (smallest,)
        return results


def on_device(
    chips,
    rep,
    history,
    mix_in,
    doc_ids,
    doc_group,
    group_weight,
    norm_gain,
    norm_bias,
    w_qkv,
    b_qkv,
    w_out,
    b_out,
    w_fc1,
    b_fc1,
    w_fc2,
    b_fc2,
    w_mix1,
    b_mix1,
    w_mix2,
    b_mix2,
    cotangent,
):
    entries, length, width = history.shape
    count = cotangent.shape[0]
    rows = w_qkv.shape[0]
    hidden = w_fc1.shape[1]
    hid = b_mix1.shape[0]
    mixes = b_mix2.shape[0]
    fsdp = 2 * chips
    group = 2 * rep
    devices = fsdp * rep
    cols = width // fsdp
    hid_cols = hidden // group
    part = width // chips
    chip = lax.axis_index("chip")
    core = lax.axis_index("core")
    line = lax.axis_index("rep")
    chip_at = chip.astype(jnp.int32).reshape(1)
    core_at = core.astype(jnp.int32).reshape(1)
    line_at = line.astype(jnp.int32).reshape(1)
    shape = jax.ShapeDtypeStruct

    def swap_core(values):
        return lax.ppermute(values, "core", [(0, 1), (1, 0)])

    def hop_chip(values, m):
        return lax.ppermute(values, "chip", [(i, i ^ m) for i in range(chips)])

    def hop_rep(values, k):
        return lax.ppermute(values, "rep", [(i, i ^ k) for i in range(rep)])

    def merge(own, came):
        return (own.astype(SINGLE) + came.astype(SINGLE)).astype(NARROW)

    def pieces(values, axis):
        size = values.shape[axis] // 2
        return (
            lax.slice_in_dim(values, 0, size, axis=axis),
            lax.slice_in_dim(values, size, 2 * size, axis=axis),
        )

    square = chips == 4
    around = range(1, 3 if square else chips)
    far = chips - 1

    def pass_on(first, axis):
        if not square:
            return ()
        return hop_chip(pieces(first[0], axis)[0], 2), hop_chip(pieces(first[1], axis)[1], 1)

    def joined_halves(halves, axis):
        return [jnp.concatenate(halves, axis)] if square else []

    def send_far(far, axis):
        if not square:
            return ()
        upper, lower = pieces(far, axis)
        return hop_chip(upper, 1), hop_chip(lower, 2)

    def take_along(terms, halves, axis):
        if not square:
            return terms
        upper, lower = halves
        near = pieces(terms[0], axis)
        far = pieces(terms[1], axis)
        return [
            jnp.concatenate([near[0], merge(near[1], lower)], axis),
            jnp.concatenate([merge(far[0], upper), far[1]], axis),
        ]

    order = Order(doc_ids[0, 0] >= 0)
    steps = length // ROWS
    block = 256
    blocks = rep * length // block
    tall = lambda n: spec((n, ROWS, width), lambda i: (0, i, 0))
    flat = lambda n: spec((ROWS, n), lambda i: (i, 0))
    tall2 = lambda n: spec((n, MIX_ROWS, width), lambda i: (0, i, 0))
    flat2 = lambda n: spec((MIX_ROWS, n), lambda i: (i, 0))
    token_block = lambda n: spec((block, n), lambda i: (i, 0))
    weight_block = (group, 1, rows, hid_cols)
    weight_specs = lambda which: [spec(weight_block, lambda *_: (0, which, 0, 0))] * (
        3 if square else chips
    ) + [spec(weight_block)] * square
    in_vmem = pl.BlockSpec(memory_space=pltpu.VMEM)

    small = (norm_gain, norm_bias, b_qkv, b_out, b_fc1, b_fc2, doc_ids)
    flat_small = [values.reshape(-1, values.shape[-1]) for values in small]
    rows_of = [values.shape[0] * -(-values.shape[1] // LANES) for values in flat_small]
    packed = pl.pallas_call(
        pack_small_kernel,
        in_specs=[in_vmem] * len(small),
        out_shape=shape((devices, -(-sum(rows_of) // ROWS) * ROWS, LANES), NARROW),
        compiler_params=params(),
        cost_estimate=cost(10**6, 10**6),
        name="pack_small",
    )(*flat_small)
    packed = order.wait(packed)
    gathered = lax.all_to_all(packed, AXES, 0, 0, tiled=True)
    hidden_sends = pl.pallas_call(
        pack_hidden_kernel,
        in_specs=[in_vmem] * 2,
        out_shape=shape((group, 2, rows, hid_cols), NARROW),
        compiler_params=params(),
        cost_estimate=cost(10**6, 6 * 10**6),
        name="pack_hidden",
    )(*order.hold(w_fc1, w_fc2))
    hidden_sends = order.wait(hidden_sends)
    heads_sends = pl.pallas_call(
        functools.partial(pack_heads_kernel, chips),
        in_specs=[scalar_spec()] + [in_vmem] * 2,
        out_shape=[shape((2, rows, 4 * cols), NARROW)] * chips,
        compiler_params=params(),
        cost_estimate=cost(10**6, 3 * 10**6),
        name="pack_heads",
    )(chip_at, *order.hold(w_qkv, w_out))
    heads_sends = order.wait(*heads_sends)
    gathered = order.wait(gathered)
    hidden_own = lax.all_to_all(order.hold(hidden_sends), GROUP, 0, 0, tiled=True)

    def fields_of(gathered):
        fields, row = [], 0
        for values, count_of in zip(flat_small, rows_of):
            field = gathered[:, row : row + count_of]
            if values.shape[1] <= LANES:
                field = field[:, :, : values.shape[1]]
            else:
                field = field.reshape(devices, values.shape[0], -1)[:, :, : values.shape[1]]
            fields.append(field)
            row += count_of
        return fields

    def join_heads(parts):
        def steps(inner):
            for_other = jnp.stack(
                [lax.dynamic_index_in_dim(values, 1 - core, 0, False) for values in parts]
            )
            return pl.pallas_call(
                functools.partial(join_heads_kernel, chips),
                in_specs=[scalar_spec()] * 2 + [in_vmem] * (chips + 1),
                out_shape=shape((fsdp, rows, 4 * cols), NARROW),
                compiler_params=params(),
                cost_estimate=cost(10**6, 3 * 10**6),
                name="join_heads",
            )(chip_at, core_at, swap_core(for_other), *parts)

        return steps

    def norm_streams(inner):
        heads_hops = [hop_chip(heads_sends[m], m) for m in range(1, chips)]
        mix_padded = jnp.pad(mix_in, ((0, 0), (0, LANES - count * entries)))
        fields = fields_of(gathered)
        gains = fields[0].transpose(1, 0, 2).reshape(3, width)
        shifts = fields[1].transpose(1, 0, 2).reshape(2, width)
        affine = jnp.stack([gains[0], shifts[0], gains[1], shifts[1]]).astype(SINGLE)
        normed = pl.pallas_call(
            functools.partial(streams_kernel, chips),
            grid=(steps,),
            in_specs=[scalar_spec(), tall(entries), flat(LANES), spec((4, width))],
            out_specs=[tall(3), flat(width), flat(width)],
            out_shape=[
                shape((3, length, width), NARROW),
                shape((length, width), NARROW),
                shape((length, width), SINGLE),
            ],
            scratch_shapes=[pltpu.VMEM((count, ROWS, width), SINGLE)],
            compiler_params=params(),
            cost_estimate=cost(10**8, 10**7),
            name="streams",
        )(chip_at, history, mix_padded, affine)
        normed = inner.wait(*normed)
        return normed, affine, mix_padded, inner.wait(*heads_hops)

    def open_layer(inner):
        normed, affine, mix_padded, heads_hops = inner.scope(norm_streams)
        qkv_near = [hop_chip(inner.hold(normed[0]), m) for m in around]
        documents, group_of, weight_of = inner.hold(doc_ids[0], doc_group[0], group_weight)
        doc_match = documents[:, None] == jnp.arange(doc_group.shape[1], dtype=jnp.int32)[None, :]
        token_group = jnp.sum(jnp.where(doc_match, group_of[None, :], 0), axis=1)
        group_match = (
            token_group[:, None] == jnp.arange(group_weight.shape[0], dtype=jnp.int32)[None, :]
        )
        token_weight = jnp.sum(jnp.where(group_match, weight_of[None, :], 0.0), 1, keepdims=True)
        token_weight = inner.wait(jnp.broadcast_to(token_weight, (length, LANES)))
        dots = pl.pallas_call(
            history_dots_kernel,
            grid=(steps,),
            in_specs=[tall(entries), tall(count), flat(LANES)],
            out_specs=flat(LANES),
            out_shape=shape((length, LANES), SINGLE),
            compiler_params=params(),
            cost_estimate=cost(10**8, 10**7),
            name="history_dots",
        )(history, cotangent, token_weight)
        dots = inner.wait(dots)
        heads_came = inner.scope(join_heads([heads_sends[0], *heads_hops]))
        return normed, affine, dots, token_weight, inner.wait(*qkv_near), mix_padded, heads_came

    normed, affine, dots, token_weight, qkv_near, mix_padded, heads_came = order.scope(open_layer)
    qkv_norm, resid_norm, last = normed
    hidden_own = order.wait(hidden_own)

    resid_norm = order.hold(resid_norm)
    resid_hops = [hop_rep(resid_norm, k) for k in range(1, rep)]

    def prepare(inner):
        mix_copies = jnp.pad(w_mix1.astype(NARROW), ((0, 0), (0, LANES - hid)))
        mix_copies = inner.wait(jnp.broadcast_to(mix_copies[None], (devices, rows, LANES)))
        fields = fields_of(inner.hold(gathered))
        gain = fields[0][:, 2].reshape(1, width).astype(SINGLE)
        qkv_bias = fields[2].reshape(3, fsdp, cols).astype(SINGLE)
        branch_bias = fields[3].reshape(1, width).astype(SINGLE)
        branch_bias = branch_bias + fields[5].reshape(1, width).astype(SINGLE)
        first_bias = fields[4].reshape(group, hid_cols).astype(SINGLE)
        docs_all = fields[6].reshape(chips, 2, rep, length)
        my_qkv_bias = lax.dynamic_index_in_dim(qkv_bias, chip * 2 + core, 1, False)
        my_first_bias = lax.dynamic_index_in_dim(first_bias, core * rep + line, 0, True)
        docs_line = lax.dynamic_index_in_dim(docs_all, line, 2, False).astype(SINGLE)
        doc_rows = []
        for m in range(chips):
            pair = lax.dynamic_index_in_dim(docs_line, chip ^ m, 0, False)
            pair = pair + doc_group.shape[1] * jnp.arange(2, dtype=SINGLE)[:, None]
            doc_rows.append(jnp.where(core == 0, pair, pair[::-1]).reshape(1, 2 * length))
        position = jnp.arange(length).astype(SINGLE)
        frequency = 10000.0 ** (-jnp.arange(0, ROT, 2).astype(SINGLE) / ROT)
        angle = position[:, None] * frequency[None, :]
        cosine, sine = jnp.cos(angle), jnp.sin(angle)
        nothing = jnp.zeros_like(sine)
        rest = HEAD_DIM - ROT
        rope = jnp.stack(
            [
                jnp.concatenate([cosine, cosine, jnp.ones((length, rest), SINGLE)], 1),
                jnp.concatenate([-sine, nothing, jnp.zeros((length, rest), SINGLE)], 1),
                jnp.concatenate([nothing, sine, jnp.zeros((length, rest), SINGLE)], 1),
            ]
        )
        rope = jnp.concatenate([rope, rope], 1)
        pairs = [
            (pair, jnp.broadcast_to(pair.reshape(2 * length, 1), (2 * length, LANES)))
            for pair in doc_rows
        ]
        ready = (gain, my_qkv_bias.reshape(1, 3 * cols), my_first_bias, branch_bias, rope, pairs)
        leaves, tree = jax.tree.flatten(ready)
        return mix_copies, jax.tree.unflatten(tree, inner.wait(*leaves))

    def spread_weights(inner):
        near = [hop_chip(inner.hold(hidden_own), m) for m in around]
        mix_copies, prepared = inner.scope(prepare)
        first_mix = lax.all_to_all(inner.hold(mix_copies), AXES, 0, 0, tiled=True)
        near = inner.wait(*near)
        return near, inner.wait(first_mix).reshape(width, LANES), prepared

    hidden_near, mix_first, prepared = order.scope(spread_weights)
    gain, my_qkv_bias, my_first_bias, branch_bias, rope, doc_pairs = prepared
    resid_hops = order.wait(*resid_hops)

    heads_all = lax.all_gather(order.hold(heads_came), "rep", axis=0)

    def hidden_side(firsts, tokens):
        return pl.pallas_call(
            functools.partial(hidden_kernel, chips),
            grid=(blocks,),
            in_specs=[token_block(width)] + weight_specs(0) + [spec((1, hid_cols))],
            out_specs=[token_block(hid_cols)] * 2,
            out_shape=[
                shape((rep * length, hid_cols), NARROW),
                shape((rep * length, hid_cols), SINGLE),
            ],
            compiler_params=params(),
            cost_estimate=cost(2 * rep * length * width * hid_cols, 10**7),
            name="hidden",
        )(tokens, *firsts, my_first_bias)

    side = shape((rep * length, width), NARROW)
    places = [shape((length, width), NARROW)] * rep
    place_specs = [spec((length, width))] * rep

    def branch_side(seconds, act, *came):
        return pl.pallas_call(
            functools.partial(branch_kernel, chips, bool(came)),
            grid=(blocks,),
            in_specs=[token_block(hid_cols)] + weight_specs(1) + [token_block(width)] * len(came),
            out_specs=place_specs if came else token_block(width),
            out_shape=places if came else side,
            compiler_params=params(),
            cost_estimate=cost(2 * rep * length * width * hid_cols, 10**7),
            name="branch",
        )(act, *seconds, *came)


    qkv_first = [qkv_norm, *qkv_near]

    def feed_forward(inner):
        ends = []
        if square:
            upper = hop_chip(inner.hold(hidden_near[0])[:, 0:1], 2)
            lower = hop_chip(inner.hold(hidden_near[1])[:, 1:2], 1)
        whole = inner.wait(jnp.stack([resid_norm, *resid_hops]))
        other = inner.wait(swap_core(whole))
        qkv_other = inner.scope(lambda _: [swap_core(values) for values in qkv_first])
        if square:
            ends = inner.wait(upper, lower)
            halves = pass_on(inner.hold(*qkv_near), 1)
        firsts = [hidden_own, *hidden_near, *ends[:1]]
        seconds = [hidden_own, *hidden_near, *ends[1:]]
        sides = [values.reshape(rep * length, width) for values in (whole, other)]
        act_other, slope_other = inner.wait(*hidden_side(firsts, inner.hold(sides[1])))

        def branch_both(inner):
            back = inner.wait(branch_side(seconds, act_other))
            came = swap_core(back)
            act_own, slope_own = inner.wait(*hidden_side(firsts, inner.hold(sides[0])))
            return act_own, slope_own, branch_side(seconds, act_own, inner.wait(came))

        act_own, slope_own, branch_places = inner.scope(branch_both)
        qkv_last = []
        if square:
            qkv_last.append(inner.wait(jnp.concatenate(inner.wait(*halves), 1)))
            qkv_other.append(inner.wait(swap_core(qkv_last[0])))
        acts, slopes = (act_own, act_other), (slope_own, slope_other)
        return ends, sides, acts, slopes, branch_places, qkv_last, qkv_other

    ends, resid_sides, acts, slopes, branch_places, qkv_last, qkv_other = order.scope(
        feed_forward
    )
    first_parts = [hidden_own, *hidden_near, *ends[:1]]
    second_parts = [hidden_own, *hidden_near, *ends[1:]]
    qkv_own = [*qkv_first, *qkv_last]
    heads_all = order.wait(heads_all)

    branch_places = order.hold(*branch_places)
    mlp_hops = [hop_rep(branch_places[k], k) for k in range(1, rep)]

    def attend(heads, own, other, m):
        return pl.pallas_call(
            attend_kernel,
            out_shape=[
                shape((3, 2 * length, cols), NARROW),
                shape((2 * length, cols), NARROW),
                shape((length, width), SINGLE),
                shape((length, width), NARROW),
            ],
            compiler_params=params(),
            cost_estimate=cost(4 * 2 * 2 * length * width * cols, 8 * 10**6),
            name="attend",
        )(own, other, heads, my_qkv_bias, rope, *doc_pairs[m])


    def add_up(own, came, first=0, *along):
        rows_of = 32
        half = length // 2 // rows_of
        block_of = lambda index: spec((3, rows_of, width), index)
        return pl.pallas_call(
            functools.partial(merge_kernel, first, half),
            grid=(2 * half,),
            in_specs=[block_of(lambda i: (0, i, 0))] * 2
            + [block_of(lambda i: (0, jnp.clip(i - first, 0, half - 1), 0))] * len(along),
            out_specs=block_of(lambda i: (0, i, 0)),
            out_shape=shape(own.shape, NARROW),
            compiler_params=params(),
            cost_estimate=cost(10**6, 10**7),
            name="merge",
        )(own, came, *along)

    def near_sums(inner, results, came, halves):
        terms = []
        for m in around:
            along = ()
            if square:
                along = (length // 2 // 32, halves[1]) if m == 1 else (0, halves[0])
            terms.append(inner.wait(add_up(results[m], came[m], *along)))
        return terms

    def attention(inner):
        heads = inner.wait(heads_all.transpose(1, 0, 2, 3).reshape(width, 4 * cols))
        results, came = [None] * chips, [None] * chips

        def step(m):
            own, other = inner.hold(qkv_own[m], qkv_other[m])
            results[m] = inner.wait(*attend(heads, own, other, m))

        step(far)
        came[far] = swap_core(inner.hold(results[far][3]))
        step(1)
        came[far] = inner.wait(came[far])
        halves = None
        if square:
            halves = send_far(inner.wait(merge(results[far][2], came[far])), 0)
        for m in range(2, far):
            step(m)
        if square:
            halves = inner.wait(*halves)
        middle = range(1, far)
        swapped = inner.wait(swap_core(inner.wait(jnp.stack([results[m][3] for m in middle]))))
        for m in middle:
            came[m] = swapped[m - 1]
        terms = [merge(results[m][2], came[m]) for m in around]
        terms = inner.wait(*take_along(terms, halves, 0))
        hops = [hop_chip(terms[m - 1], m) for m in around]
        step(0)
        hops = inner.wait(*hops)
        came[0] = inner.wait(swap_core(inner.hold(results[0][3])))
        lows = [values[0] for values in results]
        return heads, lows, [values[1] for values in results], results[0][2], [came[0], *hops]

    heads, qkv_low, mixed_low, attn_own, attn_rest = order.scope(attention)
    mlp_parts = [branch_places[0], *order.wait(*mlp_hops)]

    mix_second = jnp.pad(w_mix2, ((0, LANES - hid), (0, LANES - mixes)))
    mixed_results = pl.pallas_call(
        functools.partial(mix_kernel, chips, len(attn_rest), rep, entries),
        grid=(length // MIX_ROWS,),
        in_specs=[
            scalar_spec(),
            flat2(width),
            flat2(width),
            *[flat2(width)] * (len(attn_rest) + rep),
            spec((1, width)),
            spec((1, width)),
            spec((width, LANES)),
            spec((1, LANES)),
            spec((LANES, LANES)),
            spec((1, LANES)),
            tall2(count),
            flat2(LANES),
            flat2(LANES),
        ],
        out_specs=[flat2(width)] * 5
        + [flat2(LANES)] * 4
        + [spec((1, width))] * 2
        + [spec((1, LANES))] * 2,
        out_shape=[
            shape((length, width), SINGLE),
            shape((length, width), SINGLE),
            shape((length, width), NARROW),
            shape((length, width), NARROW),
            shape((length, width), NARROW),
            shape((length, LANES), NARROW),
            shape((length, LANES), SINGLE),
            shape((length, LANES), SINGLE),
            shape((length, LANES), SINGLE),
            shape((1, width), SINGLE),
            shape((1, width), SINGLE),
            shape((1, LANES), SINGLE),
            shape((1, LANES), SINGLE),
        ],
        scratch_shapes=[pltpu.VMEM((MIX_ROWS, width), SINGLE)],
        compiler_params=params(),
        cost_estimate=cost(2 * 10**8, 10**7),
        name="mixing",
    )(
        chip_at,
        last,
        attn_own,
        *attn_rest,
        *mlp_parts,
        branch_bias,
        gain,
        mix_first,
        jnp.pad(b_mix1, (0, LANES - hid))[None],
        mix_second,
        jnp.pad(b_mix2, (0, LANES - mixes))[None],
        cotangent,
        token_weight,
        dots,
    )
    (
        entry,
        grad_entry,
        grad_low,
        grad_turned,
        scaled_low,
        grad_pre_low,
        mix_act,
        grad_coef,
        coef,
        grad_rms_gain,
        grad_branch_bias,
        grad_pre_sum,
        grad_coef_sum,
    ) = order.wait(*mixed_results)

    grad_hops = [hop_rep(grad_turned, k) for k in range(1, rep)]

    def attend_back(own, other, heads, qkv, rope, pair):
        return pl.pallas_call(
            attend_back_kernel,
            out_shape=[
                shape((3, 2 * length, cols), NARROW),
                shape((1, 3 * cols), SINGLE),
                shape((3, length, width), NARROW),
                shape((3, length, width), NARROW),
            ],
            compiler_params=params(),
            cost_estimate=cost(4 * 2 * 2 * length * width * cols, 8 * 10**6),
            name="attend_back",
        )(own, other, heads, qkv, rope, *pair)


    def back(inner, m, own, other):
        own, other = inner.hold(own, other)
        return inner.wait(*attend_back(own, other, heads, qkv_low[m], rope, doc_pairs[m]))

    def spread_branch(inner):
        swapped = inner.wait(swap_core(grad_low))
        near = [hop_chip(inner.hold(grad_low), m) for m in around]
        result = back(inner, 0, grad_low, swapped)
        near = inner.wait(*near)
        halves = pass_on(near, 0)
        next_streams = pl.pallas_call(
            next_kernel,
            grid=(steps,),
            in_specs=[tall(entries), flat(width), flat(LANES)],
            out_specs=tall(count),
            out_shape=shape((count, length, width), NARROW),
            compiler_params=params(),
            cost_estimate=cost(10**8, 10**7),
            name="next_streams",
        )(inner.hold(history), entry, coef)
        next_streams = inner.wait(next_streams)
        if square:
            near.append(inner.wait(jnp.concatenate(inner.wait(*halves), 0)))
        others = list(swap_core(jnp.stack(near)))
        others = inner.wait(*others)
        last = back(inner, far, near[far - 1], others[far - 1])
        grad_w_mix2 = transposed_times(mix_act, grad_coef, EXACT)[:hid, :mixes]
        grad_w_mix1 = transposed_times(scaled_low, grad_pre_low)[:, :hid]
        grad_w_mix1, grad_w_mix2 = inner.wait(grad_w_mix1, grad_w_mix2)
        return result, last, near, [swapped, *others], next_streams, grad_w_mix1, grad_w_mix2

    returned, terms = [None] * chips, [None] * chips
    returned[0], returned[far], branch_near, branch_other, *rest = order.scope(spread_branch)
    next_streams, grad_w_mix1, grad_w_mix2 = rest
    branch_own = [grad_low, *branch_near]
    grad_hops = order.wait(*grad_hops)

    interleave = lambda a, b: [values for pair in zip(a, b) for values in pair]
    row_block = width // fsdp

    def hidden_back_side(firsts, seconds, grad, slope, *came):
        return pl.pallas_call(
            functools.partial(hidden_back_kernel, chips, bool(came)),
            grid=(blocks,),
            in_specs=[token_block(width), token_block(hid_cols)]
            + weight_specs(0)
            + weight_specs(1)
            + [token_block(width)] * len(came),
            out_specs=[token_block(hid_cols), spec((1, hid_cols))]
            + (place_specs if came else [token_block(width)]),
            out_shape=[shape((rep * length, hid_cols), NARROW), shape((1, hid_cols), SINGLE)]
            + (places if came else [side]),
            compiler_params=params(),
            cost_estimate=cost(4 * rep * length * width * hid_cols, 2 * 10**7),
            name="hidden_back",
        )(grad, slope, *firsts, *seconds, *came)

    def outer(inner, lefts, rights):
        whole = lambda n: spec((rep * length, n))
        return inner.wait(
            *pl.pallas_call(
                outer_kernel,
                grid=(chips,),
                in_specs=[spec((rep * length, part), lambda i: (0, i))] * 2 + [whole(hid_cols)] * 2,
                out_specs=[spec((part, hid_cols))] * chips,
                out_shape=[shape((part, hid_cols), NARROW)] * chips,
                compiler_params=params(),
                cost_estimate=cost(4 * rep * length * width * hid_cols, 2 * 10**7),
                name="outer",
            )(*lefts, *rights)
        )

    def feed_forward_back(inner):
        whole = inner.wait(jnp.stack([grad_turned, *grad_hops]))
        came = [swap_core(returned[far][3]), swap_core(whole), swap_core(returned[0][3])]
        grad_own = whole.reshape(rep * length, width)
        low_own, sum_own, back_own = inner.wait(
            *hidden_back_side(first_parts, second_parts, inner.hold(grad_own), slopes[0])
        )
        came = inner.wait(*came)
        grad_other = came[1].reshape(rep * length, width)
        far_term = inner.wait(add_up(returned[far][2], came[0]))
        halves = send_far(far_term, 1) if square else ()
        low_other, sum_other, back = inner.wait(
            *hidden_back_side(first_parts, second_parts, inner.hold(grad_other), slopes[1])
        )

        lows = (low_own, low_other)

        def sums_of_cores(inner):
            came = swap_core(back)
            grads = outer(inner, (inner.hold(resid_sides[0]), resid_sides[1]), lows)
            came = inner.wait(came)
            at = lambda values, k: values[k * length : (k + 1) * length]
            return grads, [merge(at(back_own, k), at(came, k)) for k in range(rep)]

        first_grads, merged = inner.scope(sums_of_cores)
        halves = inner.wait(*halves) if square else [far_term]
        sides = (grad_own, grad_other)
        return sides, first_grads, sum_own + sum_other, merged, halves, came[0], came[2]

    grad_sides, first_grads, grad_first_bias, grad_resid, halves, far_came, own_came = order.scope(
        feed_forward_back
    )

    def total_hidden(inner, own, hops):
        total = own.astype(SINGLE)
        for values in inner.wait(*hops):
            total = total + values.astype(SINGLE)
        return inner.wait(total.astype(NARROW).reshape(group, rows, hid_cols))

    def whole_rows(came):
        return came.transpose(1, 0, 2).reshape(rows, hidden).astype(SINGLE)

    def exchange(sums):
        widths = [values.shape[1] for values in sums]
        return widths, lax.all_to_all(jnp.concatenate(sums, 1), AXES, 0, 0, tiled=True)

    def attention_back(inner):
        results = {0: returned[0], far: returned[far]}
        second_grads = outer(inner, (inner.hold(grad_sides[0]), grad_sides[1]), acts)
        halves_out = send_far(inner.hold(second_grads[far]), 0)
        results[1] = back(inner, 1, branch_own[1], branch_other[1])
        held = second_grads[1:]
        if square:
            halves_out = inner.wait(*halves_out)
            held = inner.wait(*take_along(second_grads[1:far], halves_out, 0))
        hops = [hop_chip(held[m - 1], m) for m in around]
        for m in range(2, far):
            results[m] = back(inner, m, branch_own[m], branch_other[m])
        linears = inner.hold(*[results[m][0] for m in range(chips)])
        grad_heads = pl.pallas_call(
            functools.partial(heads_grad_kernel, chips),
            grid=(fsdp,),
            in_specs=[spec((3, length, row_block), lambda i: (0, 0, i))] * fsdp
            + [spec((length, row_block), lambda i: (0, i))] * fsdp
            + [spec((3, 2 * length, cols))] * chips
            + [spec((2 * length, cols))] * chips,
            out_specs=spec((rep, 1, rows, 4 * cols), lambda i: (0, i, 0, 0)),
            out_shape=shape((rep, fsdp, rows, 4 * cols), NARROW),
            compiler_params=params(),
            cost_estimate=cost(8 * fsdp * length * width * cols, 3 * 10**7),
            name="heads_grad",
        )(
            *interleave(qkv_own, qkv_other),
            *interleave(branch_own, branch_other),
            *linears,
            *mixed_low,
        )
        grad_heads = inner.wait(grad_heads)
        hops = inner.wait(*hops)
        middle = [results[m] for m in range(1, far)]
        return grad_heads, middle, second_grads[0], hops

    def residual_back(inner):
        hops = inner.hold(*grad_resid)
        hops = [hop_rep(hops[k], k) for k in range(1, rep)]
        results = inner.scope(attention_back)
        return inner.wait(*hops), *results

    resid_hops, grad_heads, returned[1:far], second_own_grad, second_hops = order.scope(residual_back)
    qkv_biases = [results[1] for results in returned]
    grad_resid = [grad_resid[0], *resid_hops]

    def by_owner(vector):
        return vector.reshape(-1, devices, rows).transpose(1, 0, 2).reshape(devices, -1)

    grad_heads = lax.psum_scatter(grad_heads, "rep", scatter_dimension=0, tiled=False)
    def second_sum(inner):
        return total_hidden(inner, second_own_grad, second_hops)

    second_total = order.scope(second_sum)
    second_came = lax.all_to_all(order.hold(second_total), GROUP, 0, 0, tiled=True)

    def near_terms_of(inner):
        first_halves = send_far(inner.hold(first_grads[far]), 0)
        middle = range(1, far)
        swaps = [swap_core(inner.hold(returned[m][3])) for m in middle]
        swaps = list(inner.wait(*swaps)) if len(swaps) > 1 else [inner.wait(*swaps)]
        owns = [results[2] for results in returned]
        near_terms = near_sums(inner, owns, [None, *swaps, far_came], halves)
        return near_terms, inner.wait(*first_halves) if square else ()

    def send_terms(inner):
        near_terms, first_halves = inner.scope(near_terms_of)
        near_terms = inner.hold(*near_terms)
        qkv_back = [hop_chip(near_terms[m - 1], m) for m in around]

        def pack_sums(_):
            qkv_bias_all = lax.dynamic_update_index_in_dim(
                jnp.zeros((3, fsdp, cols), SINGLE),
                sum(qkv_biases).reshape(3, cols),
                chip * 2 + core,
                1,
            )
            tail = jnp.concatenate(
                [grad_pre_sum[0, :hid], grad_w_mix2.reshape(-1), grad_coef_sum[0, :mixes]]
            )
            sums = [
                by_owner(grad_rms_gain[0]),
                qkv_bias_all.reshape(devices, -1),
                grad_branch_bias.reshape(devices, -1),
                grad_w_mix1.reshape(devices, -1),
                jnp.broadcast_to(tail[None], (devices, tail.shape[0])),
            ]
            size = sum(values.shape[1] for values in sums)
            empty = -size % (ROWS * LANES)
            sums.append(jnp.zeros((devices, empty), SINGLE))
            return jnp.concatenate(sums, 1).astype(NARROW).reshape(devices, ROWS, -1)

        sums = inner.scope(pack_sums)
        held = first_grads[1:]
        if square:
            held = inner.wait(*take_along(first_grads[1:far], first_halves, 0))
        qkv_back = inner.wait(*qkv_back)
        return held, qkv_back, sums

    first_terms, qkv_back, sums = order.scope(send_terms)
    second_came = order.wait(second_came)
    widths = [rows, 3 * cols * fsdp // devices, rows, rows * hid]

    qkv_rest = [own_came, *qkv_back]

    def close_layer(inner):
        held = inner.hold(*first_terms)
        first_hops = [hop_chip(held[m - 1], m) for m in around]
        close_from = inner.hold(history, cotangent)
        grad_history, grad_mix_in, grad_affine = pl.pallas_call(
            functools.partial(close_kernel, chips, len(qkv_rest), rep),
            grid=(steps,),
            in_specs=[
                scalar_spec(),
                tall(entries),
                tall(count),
                flat(LANES),
                flat(LANES),
                flat(LANES),
                spec((4, width)),
                flat(width),
                *[tall(3)] * (1 + len(qkv_rest)),
                *[flat(width)] * rep,
            ],
            out_specs=[tall(entries), flat(count * entries), spec((4, width))],
            out_shape=[
                shape((entries, length, width), SINGLE),
                shape((length, count * entries), SINGLE),
                shape((4, width), SINGLE),
            ],
            scratch_shapes=[
                pltpu.VMEM((count, ROWS, width), SINGLE),
                pltpu.VMEM((ROWS, width), SINGLE),
                pltpu.VMEM((5 * count * ROWS, width), NARROW),
            ],
            compiler_params=params(),
            cost_estimate=cost(2 * 10**8, 2 * 10**7),
            name="close",
        )(
            chip_at,
            *close_from,
            coef,
            token_weight,
            mix_padded,
            affine,
            grad_entry,
            returned[0][2],
            *qkv_rest,
            *grad_resid,
        )
        grad_history, grad_mix_in, grad_affine = inner.wait(grad_history, grad_mix_in, grad_affine)
        first_bias_all = lax.dynamic_update_index_in_dim(
            jnp.zeros((group, hid_cols), SINGLE), grad_first_bias[0], core * rep + line, 0
        )
        late = [by_owner(grad_affine), first_bias_all.reshape(devices, -1)]
        late = jnp.concatenate(late, 1).astype(NARROW)
        lanes = sums.shape[2]
        late = jnp.pad(late, ((0, 0), (0, -late.shape[1] % lanes))).reshape(devices, -1, lanes)
        late = inner.wait(jnp.concatenate([sums, late], 1))
        late = lax.all_to_all(late, AXES, 0, 0, tiled=True)

        first_total = total_hidden(inner, first_grads[0], first_hops)
        return grad_history, grad_mix_in, first_total, inner.wait(late)

    grad_history, grad_mix_in, first_total, everything = order.scope(close_layer)
    everything = everything.astype(SINGLE)
    sums, every = everything[:, :ROWS], everything[:, ROWS:].reshape(devices, -1)
    first_came = lax.all_to_all(order.hold(first_total), GROUP, 0, 0, tiled=True)
    grad_w_fc2 = order.wait(whole_rows(second_came))
    every = order.wait(jnp.sum(every, 0))
    total = order.wait(jnp.sum(sums.astype(SINGLE), 0).reshape(-1))
    grad_heads = order.wait(grad_heads)

    def around_ring(inner):
        split = inner.hold(grad_heads).reshape(chips, 2, rows, 4 * cols)
        parts = [lax.dynamic_index_in_dim(split, chip ^ m, 0, False) for m in range(chips)]
        parts = [parts[0]] + [hop_chip(parts[m], m) for m in range(1, chips)]
        parts = jnp.stack(inner.wait(*parts))
        mine = lax.dynamic_index_in_dim(parts, core, 1, False)
        came = swap_core(lax.dynamic_index_in_dim(parts, 1 - core, 1, False))
        result = jnp.zeros((chips, 2, rows, 4 * cols), NARROW)
        for m in range(chips):
            pair = jnp.where(core == 0, jnp.stack([mine[m], came[m]]), jnp.stack([came[m], mine[m]]))
            result = lax.dynamic_update_index_in_dim(result, pair, chip ^ m, 0)
        result = result.reshape(fsdp, rows, 4, cols).transpose(1, 2, 0, 3).astype(SINGLE)
        return result[:, :3].reshape(rows, 3 * width), result[:, 3].reshape(rows, width)

    grad_w_qkv, grad_w_out = order.scope(around_ring)
    first_came = order.wait(first_came)
    grad_w_fc1 = whole_rows(first_came)
    outs, start = [], 0
    for size in widths:
        outs.append(total[start : start + size])
        start += size
    outs.append(total[start:])
    affine_sums = every[: 4 * rows].reshape(4, rows)
    gain_grads = jnp.stack([affine_sums[0], affine_sums[2], outs[0]])
    bias_grads = jnp.stack([affine_sums[1], affine_sums[3]])
    return (
        next_streams,
        grad_history,
        grad_mix_in,
        gain_grads,
        bias_grads,
        grad_w_qkv,
        outs[1],
        grad_w_out,
        outs[2],
        grad_w_fc1,
        every[4 * rows : 4 * rows + hidden // devices],
        grad_w_fc2,
        outs[2],
        outs[3].reshape(rows, hid),
        outs[4][:hid],
        outs[4][hid : hid + hid * mixes].reshape(hid, mixes),
        outs[4][hid + hid * mixes : hid + hid * mixes + mixes],
    )


def solution(mesh):
    fsdp, rep = mesh.shape["fsdp"], mesh.shape["rep"]
    chips = fsdp // 2
    finer = Mesh(mesh.devices.reshape(chips, 2, rep), AXES)
    rows = P(AXES, None)
    line = P(AXES)
    streams = P(None, AXES, None)
    columns = P(None, AXES)
    in_specs = (
        streams,
        rows,
        rows,
        rows,
        P(),
        columns,
        columns,
        rows,
        line,
        rows,
        line,
        rows,
        line,
        rows,
        line,
        rows,
        P(),
        P(),
        P(),
        streams,
    )
    out_specs = (
        streams,
        streams,
        rows,
        columns,
        columns,
        rows,
        line,
        rows,
        line,
        rows,
        line,
        rows,
        line,
        rows,
        P(),
        P(),
        P(),
    )
    return jax.shard_map(
        functools.partial(on_device, chips, rep),
        mesh=finer,
        in_specs=in_specs,
        out_specs=out_specs,
        check_vma=False,
    )
```
